256 devices in a mesh: outer: 16 (over y, x), seq: 16 (over z, core).
Axes of the slice: x: 4, y: 4, z: 8, core: 2. Of those that a mesh axis runs over, the one named last changes fastest.
Arguments:
- query_rows: bfloat16 [32768, 1024], P(('outer', 'seq')), may hold values from -6 to 6
- key_rows: bfloat16 [32768, 1024], P(('outer', 'seq')), may hold values from -6 to 6
- value_rows: bfloat16 [32768, 1024], P(('outer', 'seq')), may hold values from -6 to 6
- out_grad: bfloat16 [32768, 1024], P(('outer', 'seq')), may hold values from -6 to 6
Outputs:
- attended: bfloat16 [32768, 1024], P(('outer', 'seq'))
- query_grad: float32 [32768, 1024], P(('outer', 'seq'))
- key_grad: float32 [32768, 1024], P(('outer', 'seq'))
- value_grad: float32 [32768, 1024], P(('outer', 'seq'))
The draws below stay inside these ranges and needn't reach their ends.
All inputs are finite; a program needn't handle non-finite values.
Results may differ from the reference program's by a relative error of at most 0.018.
Values may be sent and summed in bfloat16 or wider, within the bound.
No kernel may reach another device: no remote copies, remote signals or barrier semaphores. Data moves between devices by JAX's collectives and lax.ppermute only.
A program may use at most 128 MiB of HBM per device.

```python
import math
import jax
import jax.numpy as jnp
from jax import lax

HEADS = 8
HEAD = 128
D = 1024
BLOCK = 128
LEVELS = 3
TOKENS = 32768


def draw_query_rows(key, part):
    key = jax.random.fold_in(key, 3)
    return jnp.clip(jax.random.normal(key, (TOKENS, HEADS * HEAD), jnp.float32), -4.0, 4.0).astype(jnp.bfloat16)


def draw_key_rows(key, part):
    key = jax.random.fold_in(key, 5)
    return jnp.clip(jax.random.normal(key, (TOKENS, HEADS * HEAD), jnp.float32), -4.0, 4.0).astype(jnp.bfloat16)


def levels(key, dims, split, least, high):
    loudness = 1.0
    for dim, blocks in split:
        steps = jax.random.uniform(jax.random.fold_in(jax.random.fold_in(key, 6), dim), (blocks,), jnp.float32, least / len(split), high / len(split))
        loudness = loudness * jnp.repeat(jnp.exp(steps), dims[dim] // blocks).reshape((-1,) + (1,) * (len(dims) - 1 - dim))
    return loudness


def noise(key, dims, deviation, bound, cuts=(), kind=jnp.bfloat16):
    drawn = deviation * jax.random.normal(key, dims, jnp.float32)
    if cuts:
        drawn = drawn * levels(key, dims, cuts, -0.22, 0.18)
    return jnp.clip(drawn, -bound, bound).astype(kind)


def setup_inputs(seed: int = 0) -> dict:
    splits = jax.random.split(jax.random.key(seed), 5)
    return {
        "query_rows": draw_query_rows(jax.random.fold_in(splits[4], 71), 0),
        "key_rows": draw_key_rows(jax.random.fold_in(splits[4], 71), 0),
        "value_rows": noise(splits[2], (TOKENS, D), 1.0, 6.0, ((0, 256),)),
        "out_grad": noise(splits[3], (TOKENS, D), 1.0, 6.0, ((0, 256),)),
    }


LOG_TWO = math.log(2.0)
NEGATIVE = -1e+30

def attend(queries, keyvals, bias, grad_out):
    block_rows, features = queries.shape
    count_keys = keyvals.shape[0]
    factor = 1.0 / math.sqrt(HEAD)
    query_heads = queries.astype(jnp.float32).reshape(block_rows, HEADS, HEAD)
    key_heads = keyvals[:, :features].astype(jnp.float32).reshape(count_keys, HEADS, HEAD)
    value_heads = keyvals[:, features:].astype(jnp.float32).reshape(count_keys, HEADS, HEAD)
    scores = jnp.einsum('qhe,khe->hqk', query_heads, key_heads) * factor + bias
    highest = lax.optimization_barrier(jnp.max(scores, axis=2, keepdims=True))
    weights = jnp.exp(scores - highest)
    probs = weights / lax.optimization_barrier(jnp.sum(weights, axis=2, keepdims=True))
    probs_low = probs.astype(jnp.bfloat16).astype(jnp.float32)
    output_full = jnp.einsum('hqk,khe->qhe', probs_low, value_heads)
    grad_heads = grad_out.astype(jnp.float32).reshape(block_rows, HEADS, HEAD)
    dprob = jnp.einsum('qhe,khe->hqk', grad_heads, value_heads)
    delta = jnp.einsum('qhe,qhe->hq', grad_heads, output_full)
    dscore = (probs * (dprob - delta[:, :, None])).astype(jnp.bfloat16).astype(jnp.float32)
    query_grad = jnp.einsum('hqk,khe->qhe', dscore, key_heads) * factor
    key_grad = jnp.einsum('hqk,qhe->khe', dscore, query_heads) * factor
    value_grad = jnp.einsum('hqk,qhe->khe', probs_low, grad_heads)
    pair_grad = jnp.concatenate([key_grad.reshape(count_keys, features), value_grad.reshape(count_keys, features)], axis=1)
    return (output_full.reshape(block_rows, features), query_grad.reshape(block_rows, features), pair_grad)

def rounded(values):
    return lax.optimization_barrier(values.astype(jnp.bfloat16)).astype(jnp.float32)

def reference(query_rows, key_rows, value_rows, out_grad):
    features = HEADS * HEAD
    blocks = TOKENS // BLOCK
    half_rows = BLOCK // 2
    fine_pairs = jnp.concatenate([key_rows, value_rows], axis=1)
    fine_padded = jnp.pad(fine_pairs, ((BLOCK, BLOCK), (0, 0)))
    pooled_padded = []
    pooled_zero = []
    for height in range(1, LEVELS + 1):
        span = 2 ** height
        pooled = lax.optimization_barrier(jnp.mean(fine_pairs.astype(jnp.float32).reshape(TOKENS // span, span, 2 * features), axis=1)).astype(jnp.bfloat16)
        pooled_padded.append(jnp.pad(pooled, ((3 * half_rows, 3 * half_rows), (0, 0))))
        pooled_zero.append(jnp.zeros((TOKENS // span + 6 * half_rows, 2 * features), jnp.float32))
    fine_zero = jnp.zeros((TOKENS + 2 * BLOCK, 2 * features), jnp.float32)

    def advance(carry, block_id):
        fine_acc, pooled_acc = carry
        row_start = (block_id * BLOCK).astype(jnp.int32)
        queries = lax.dynamic_slice_in_dim(query_rows, row_start, BLOCK, 0)
        grad_out = lax.dynamic_slice_in_dim(out_grad, row_start, BLOCK, 0)
        key_parts = [lax.dynamic_slice_in_dim(fine_padded, row_start, 3 * BLOCK, 0)]
        neighbours = block_id + jnp.arange(-1, 2).astype(jnp.int32)
        fine_valid = (neighbours >= 0) & (neighbours < blocks)
        bias_parts = [jnp.repeat(jnp.where(fine_valid, 0.0, NEGATIVE).astype(jnp.float32), BLOCK)]
        offsets_all = []
        for height in range(1, LEVELS + 1):
            span = 2 ** height
            coarse = block_id // span
            parent = block_id // (span // 2)
            middle = jnp.where(parent % 2 == 0, 2 * coarse + 2, 2 * coarse - 1)
            group_total = blocks // (span // 2)
            offsets_level = []
            for group_id in (2 * coarse - 2, middle, 2 * coarse + 3):
                offset_rows = ((group_id + 3) * half_rows).astype(jnp.int32)
                key_parts.append(lax.dynamic_slice_in_dim(pooled_padded[height - 1], offset_rows, half_rows, 0))
                is_valid = (group_id >= 0) & (group_id < group_total)
                bias_parts.append(jnp.zeros((half_rows,), jnp.float32) + jnp.where(is_valid, height * LOG_TWO, NEGATIVE).astype(jnp.float32))
                offsets_level.append(offset_rows)
            offsets_all.append(offsets_level)
        keyvals = jnp.concatenate(key_parts, axis=0)
        bias = jnp.concatenate(bias_parts, axis=0)
        output_full, query_grad, pair_grad = attend(queries, keyvals, bias, grad_out)
        fine_term = pair_grad[:3 * BLOCK]
        fine_low = rounded(fine_term)
        fine_term = jnp.concatenate([fine_low[:BLOCK], fine_term[BLOCK:2 * BLOCK], fine_low[2 * BLOCK:]], axis=0)
        current = lax.dynamic_slice_in_dim(fine_acc, row_start, 3 * BLOCK, 0)
        fine_acc = lax.dynamic_update_slice_in_dim(fine_acc, current + fine_term, row_start, 0)
        cursor = 3 * BLOCK
        updated = []
        for height in range(1, LEVELS + 1):
            level_acc = pooled_acc[height - 1]
            for offset_rows in offsets_all[height - 1]:
                term = rounded(pair_grad[cursor:cursor + half_rows])
                current = lax.dynamic_slice_in_dim(level_acc, offset_rows, half_rows, 0)
                level_acc = lax.dynamic_update_slice_in_dim(level_acc, current + term, offset_rows, 0)
                cursor = cursor + half_rows
            updated.append(level_acc)
        return ((fine_acc, tuple(updated)), (output_full.astype(jnp.bfloat16), query_grad))
    (fine_acc, pooled_acc), (outputs, query_grads) = lax.scan(advance, (fine_zero, tuple(pooled_zero)), jnp.arange(blocks).astype(jnp.int32))
    attended = outputs.reshape(TOKENS, features)
    query_grad = query_grads.reshape(TOKENS, features)
    combined = fine_acc[BLOCK:BLOCK + TOKENS]
    for height in range(1, LEVELS + 1):
        span = 2 ** height
        level_sum = pooled_acc[height - 1][3 * half_rows:3 * half_rows + TOKENS // span]
        combined = combined + jnp.repeat(level_sum, span, axis=0) / span
    return (attended, query_grad, combined[:, :features], combined[:, features:])
```

```python
import math

import jax
import jax.numpy as jnp
from jax import lax
from jax.experimental import pallas as pl
from jax.experimental.pallas import tpu as pltpu
from jax.sharding import PartitionSpec as P

HEADS = 8
HEAD = 128
LEVELS = 3
BLOCK = 128
HALF = 512
PAIR = 1024
AXES = ("outer", "seq")
LOG_TWO = math.log(2.0)
NEGATIVE = -1e30
FACTOR = 1.0 / math.sqrt(HEAD)
BF16 = jnp.bfloat16
F32 = jnp.float32


def dot(a, b, dims=((1,), (0,))):
    return lax.dot_general(a, b, (dims, ((), ())), preferred_element_type=F32)


def pool_matrix(rows, columns, span):
    i = lax.broadcasted_iota(jnp.int32, (rows, columns), 0)
    j = lax.broadcasted_iota(jnp.int32, (rows, columns), 1)
    return jnp.where(j // span == i, 1.0 / span, 0.0).astype(BF16)


def spread_matrix(rows, columns, span):
    i = lax.broadcasted_iota(jnp.int32, (rows, columns), 0)
    j = lax.broadcasted_iota(jnp.int32, (rows, columns), 1)
    return jnp.where(i // span == j, 1.0 / span, 0.0).astype(BF16)


def half_columns(core):
    return pl.ds(pl.multiple_of(core * HALF, HALF), HALF)


def block_at(core):
    return pl.ds(pl.multiple_of(core * BLOCK, BLOCK), BLOCK)


def split_kernel(where, q, g, k, v, out):
    other = half_columns(1 - where[0] % 2)
    out[:, 0:512] = q[:, other]
    out[:, 512:1024] = g[:, other]
    out[:, 1024:1536] = k[:, other]
    out[:, 1536:2048] = v[:, other]


def pool_kernel(where, k, v, recv, up, down, pool2, pool3):
    core = where[0] % 2
    mine = half_columns(core)
    own = jnp.concatenate([k[:, mine], v[:, mine]], axis=1)
    swapped = recv[:, 1024:2048]
    first = core == 0
    low = jnp.where(first, own, swapped)
    high = jnp.where(first, swapped, own)
    matrix = jnp.concatenate(
        [pool_matrix(64, BLOCK, 2), pool_matrix(32, BLOCK, 4), pool_matrix(16, BLOCK, 8)], axis=0
    )
    pooled_low = dot(matrix, low).astype(BF16)
    pooled_high = dot(matrix, high).astype(BF16)
    up[0:128] = high
    up[128:192] = pooled_low[0:64]
    down[0:128] = low
    down[128:192] = pooled_high[0:64]
    pool2[0:32] = pooled_low[64:96]
    pool2[32:64] = pooled_high[64:96]
    pool3[0:16] = pooled_low[96:112]
    pool3[16:32] = pooled_high[96:112]


def attend_kernel(
    where, q, g, recv, up, down, below, above,
    m2, p2, s2, m3, m3x, p3, p3x, s3, s3x,
    out_keep, out_send, grad_own, grad_below, grad_above,
    gm2, gp2, gs2, gm3, gm3x, gp3, gp3x, gs3, gs3x,
    queries, grads, keyvals, spread,
):
    chips = where[1] // 2
    core = where[0] % 2
    chip = where[0] // 2
    quad = chip // 2
    mine = half_columns(core)
    queries[block_at(core), :] = q[:, mine]
    queries[block_at(1 - core), :] = recv[:, 0:512]
    grads[block_at(core), :] = g[:, mine]
    grads[block_at(1 - core), :] = recv[:, 512:1024]
    keyvals[0:128] = down[0:128]
    keyvals[128:256] = up[0:128]
    keyvals[256:320] = below[128:192]
    keyvals[320:384] = above[128:192]
    keyvals[384:448] = m2[...]
    keyvals[448:512] = p2[...]
    keyvals[512:576] = s2[...]
    for n, piece in enumerate((m3, m3x, p3, p3x, s3, s3x)):
        keyvals[576 + 32 * n : 608 + 32 * n] = piece[...]
    halve = pool_matrix(64, BLOCK, 2)
    keyvals[768:896] = below[0:128]
    keyvals[896:960] = dot(halve, above[0:128]).astype(BF16)
    keyvals[960:1088] = above[0:128]
    keyvals[1088:1152] = dot(halve, below[0:128]).astype(BF16)
    spread[...] = spread_matrix(BLOCK, 64, 2)

    def bias(valid, level):
        return jnp.where(valid, F32(level * LOG_TWO), F32(NEGATIVE))

    has_below = chip >= 1
    has_above = chip < chips - 1
    far2 = jnp.where(chip % 2 == 0, chip + 3, chip - 3)
    far3 = jnp.where(quad % 2 == 0, quad + 3, quad - 3)
    quads = chips // 2
    pieces = (
        (0, 256, F32(0.0)),
        (256, 64, bias(has_below, 1)),
        (320, 64, bias(has_above, 1)),
        (384, 64, bias(chip >= 2, 2)),
        (448, 64, bias(chip + 2 < chips, 2)),
        (512, 64, bias((far2 >= 0) & (far2 < chips), 2)),
        (576, 64, bias(quad >= 2, 3)),
        (640, 64, bias(quad + 2 < quads, 3)),
        (704, 64, bias((far3 >= 0) & (far3 < quads), 3)),
    )
    side = lax.broadcasted_iota(jnp.int32, (1, 256), 1) < 128
    fine_bias = jnp.where(side, bias(has_below, 0), bias(has_above, 0))
    half_bias = jnp.where(side, bias(has_above, 1), bias(has_below, 1))
    rows_bias = jnp.concatenate(
        [jnp.full((rows, 1), value, F32) for _, rows, value in pieces], axis=0
    )
    nt = ((1,), (1,))
    tn = ((0,), (0,))
    for h in range(4):
        kc = slice(h * HEAD, (h + 1) * HEAD)
        vc = slice(HALF + h * HEAD, HALF + (h + 1) * HEAD)
        qh = queries[:, kc]
        gh = grads[:, kc]
        keys = keyvals[0:768, kc]
        values = keyvals[0:768, vc]
        keys_a = keyvals[768:960, kc]
        keys_b = keyvals[960:1152, kc]
        values_a = keyvals[768:960, vc]
        values_b = keyvals[960:1152, vc]
        extra = jnp.concatenate([dot(keys_a, qh[0:128], nt), dot(keys_b, qh[128:256], nt)], axis=1)
        scores = jnp.concatenate(
            [
                dot(keys, qh, nt) * FACTOR + rows_bias,
                extra[0:128] * FACTOR + fine_bias,
                extra[128:192] * FACTOR + half_bias,
            ],
            axis=0,
        )
        weights = jnp.exp(scores - jnp.max(scores, axis=0, keepdims=True))
        probs = weights * (1.0 / jnp.sum(weights, axis=0, keepdims=True))
        low = probs.astype(BF16)
        dprob = jnp.concatenate(
            [
                dot(values, gh, nt),
                jnp.concatenate(
                    [dot(values_a, gh[0:128], nt), dot(values_b, gh[128:256], nt)], axis=1
                ),
            ],
            axis=0,
        )
        delta = jnp.sum(low.astype(F32) * dprob, axis=0, keepdims=True)
        dscore = (probs * (dprob - delta)).astype(BF16)

        def back(weight, shared, part_a, part_b):
            whole = dot(shared, weight[0:768], tn)
            edges = jnp.concatenate(
                [dot(part_a, weight[768:960, 0:128], tn), dot(part_b, weight[768:960, 128:256], tn)],
                axis=1,
            )
            return (whole + edges).T

        attended = back(low, values, values_a, values_b)
        query_grad = back(dscore, keys, keys_a, keys_b) * FACTOR

        @pl.when(core == 0)
        def _():
            out_keep[:, kc] = attended[0:128]
            out_send[:, kc] = attended[128:256]
            out_keep[:, vc] = query_grad[0:128]
            out_send[:, vc] = query_grad[128:256]

        @pl.when(core == 1)
        def _():
            out_keep[:, kc] = attended[128:256]
            out_send[:, kc] = attended[0:128]
            out_keep[:, vc] = query_grad[128:256]
            out_send[:, vc] = query_grad[0:128]

        for columns, weight, rows, scale in ((kc, dscore, qh, FACTOR), (vc, low, gh, 1.0)):
            shared = dot(weight[0:768], rows) * scale
            part_a = dot(weight[768:960, 0:128], rows[0:128]) * scale
            part_b = dot(weight[768:960, 128:256], rows[128:256]) * scale
            grad_own[:, columns] = shared[0:256]
            terms = shared.astype(BF16)
            grad_below[0:128, columns] = (
                part_a[0:128] + dot(spread[...], part_b[128:192].astype(BF16))
            ).astype(BF16)
            grad_below[128:192, columns] = terms[256:320]
            grad_above[0:128, columns] = (
                part_b[0:128] + dot(spread[...], part_a[128:192].astype(BF16))
            ).astype(BF16)
            grad_above[128:192, columns] = terms[320:384]
            for n, piece in enumerate((gm2, gp2, gs2)):
                piece[:, columns] = terms[384 + 64 * n : 448 + 64 * n]
            for n, piece in enumerate((gm3, gm3x, gp3, gp3x, gs3, gs3x)):
                piece[:, columns] = terms[576 + 32 * n : 608 + 32 * n]


def total_kernel(where, own, from_below, from_above, a2, b2, c2, a3, b3, c3, d3, e3, f3, keep, send):
    core = where[0] % 2
    matrix = jnp.concatenate(
        [spread_matrix(BLOCK, 64, 2)]
        + [spread_matrix(BLOCK, 32, 4)] * 3
        + [spread_matrix(BLOCK, 16, 8)] * 6,
        axis=1,
    )
    totals = []
    for n, (fine, half) in enumerate(((from_below, from_above), (from_above, from_below))):
        stack = jnp.concatenate(
            [half[128:192]]
            + [piece[32 * n : 32 * n + 32] for piece in (a2, b2, c2)]
            + [piece[16 * n : 16 * n + 16] for piece in (a3, b3, c3, d3, e3, f3)],
            axis=0,
        )
        totals.append(
            own[BLOCK * n : BLOCK * (n + 1)] + fine[0:128].astype(F32) + dot(matrix, stack)
        )
    first = core == 0
    keep[...] = jnp.where(first, totals[0], totals[1])
    send[...] = jnp.where(first, totals[1], totals[0])


def join_kernel(where, out_keep, out_recv, grad_keep, grad_recv, attended, qg, kg, vg):
    core = where[0] % 2
    mine = half_columns(core)
    other = half_columns(1 - core)
    attended[:, mine] = out_keep[:, 0:512].astype(BF16)
    attended[:, other] = out_recv[:, 0:512].astype(BF16)
    qg[:, mine] = out_keep[:, 512:1024]
    qg[:, other] = out_recv[:, 512:1024]
    kg[:, mine] = grad_keep[:, 0:512]
    kg[:, other] = grad_recv[:, 0:512]
    vg[:, mine] = grad_keep[:, 512:1024]
    vg[:, other] = grad_recv[:, 512:1024]


def call(kernel, where, args, outs, scratch=(), flops=0):
    return pl.pallas_call(
        kernel,
        out_shape=[jax.ShapeDtypeStruct(shape, dtype) for shape, dtype in outs],
        in_specs=[pl.BlockSpec(memory_space=pltpu.SMEM)]
        + [pl.BlockSpec(memory_space=pltpu.VMEM)] * len(args),
        out_specs=[pl.BlockSpec(memory_space=pltpu.VMEM)] * len(outs),
        scratch_shapes=list(scratch),
        compiler_params=pltpu.CompilerParams(vmem_limit_bytes=48 * 1024 * 1024),
    )(where, *args)


def sources(chips):
    def far2(p):
        return p + 3 if p % 2 == 0 else p - 3

    def far3(p):
        return p + 6 if (p // 2) % 2 == 0 else p - 6

    return {
        "below": lambda p: p - 1,
        "above": lambda p: p + 1,
        "m2": lambda p: p - 2,
        "p2": lambda p: p + 2,
        "s2": far2,
        "m3": lambda p: p - 4,
        "m3x": lambda p: (p - 4) ^ 1,
        "p3": lambda p: p + 4,
        "p3x": lambda p: (p + 4) ^ 1,
        "s3": far3,
        "s3x": lambda p: far3(p) ^ 1,
    }


def on_device(query_rows, key_rows, value_rows, out_grad):
    position = lax.axis_index(AXES)
    devices = lax.axis_size(AXES)
    chips = devices // 2
    plan = sources(chips)
    where = jnp.stack([position, jnp.int32(devices)]).astype(jnp.int32)

    def swap(x):
        return lax.ppermute(x, AXES, [(i, i ^ 1) for i in range(devices)])

    def pairs(name):
        found = []
        for chip in range(chips):
            source = plan[name](chip) % chips
            found += [(2 * source + core, 2 * chip + core) for core in range(2)]
        return found

    def fetch(x, name):
        return lax.ppermute(x, AXES, pairs(name))

    def give(x, name):
        return lax.ppermute(x, AXES, [(b, a) for a, b in pairs(name)])

    (sent,) = call(
        split_kernel, where, (query_rows, out_grad, key_rows, value_rows), [((BLOCK, 2048), BF16)]
    )
    recv = swap(sent)
    up, down, pool2, pool3 = call(
        pool_kernel,
        where,
        (key_rows, value_rows, recv),
        [((192, PAIR), BF16), ((192, PAIR), BF16), ((64, PAIR), BF16), ((32, PAIR), BF16)],
    )
    names3 = ("m3", "m3x", "p3", "p3x", "s3", "s3x")
    names2 = ("m2", "p2", "s2")
    pieces3 = [fetch(pool3, name) for name in names3]
    pieces2 = [fetch(pool2, name) for name in names2]
    below = fetch(up, "below")
    above = fetch(down, "above")
    result = call(
        attend_kernel,
        where,
        (query_rows, out_grad, recv, up, down, below, above, *pieces2, *pieces3),
        [
            ((BLOCK, PAIR), F32),
            ((BLOCK, PAIR), F32),
            ((2 * BLOCK, PAIR), F32),
            ((192, PAIR), BF16),
            ((192, PAIR), BF16),
        ]
        + [((64, PAIR), BF16)] * 3
        + [((32, PAIR), BF16)] * 6,
        scratch=[
            pltpu.VMEM((2 * BLOCK, HALF), BF16),
            pltpu.VMEM((2 * BLOCK, HALF), BF16),
            pltpu.VMEM((1152, PAIR), BF16),
            pltpu.VMEM((BLOCK, 64), BF16),
        ],
    )
    out_keep, out_send, grad_own, grad_below, grad_above = result[:5]
    out_recv = swap(out_send)
    back3 = [give(x, name) for x, name in zip(result[8:14], names3)]
    back2 = [give(x, name) for x, name in zip(result[5:8], names2)]
    from_above = give(grad_below, "below")
    from_below = give(grad_above, "above")
    grad_keep, grad_send = call(
        total_kernel,
        where,
        (grad_own, from_below, from_above, *back2, *back3),
        [((BLOCK, PAIR), F32), ((BLOCK, PAIR), F32)],
    )
    grad_recv = swap(grad_send)
    return tuple(
        call(
            join_kernel,
            where,
            (out_keep, out_recv, grad_keep, grad_recv),
            [((BLOCK, PAIR), BF16)] + [((BLOCK, PAIR), F32)] * 3,
        )
    )


def solution(mesh):
    spec = P(AXES, None)
    return jax.shard_map(
        on_device, mesh=mesh, in_specs=(spec,) * 4, out_specs=(spec,) * 4, check_vma=False
    )
```

```python
import math

import jax
import jax.numpy as jnp
from jax import lax
from jax.experimental import pallas as pl
from jax.experimental.pallas import tpu as pltpu
from jax.sharding import PartitionSpec as P

HEADS = 8
HEAD = 128
LEVELS = 3
BLOCK = 128
HALF = 512
PAIR = 1024
ROW = 8
AXES = ("outer", "seq")
LOG_TWO = math.log(2.0)
NEGATIVE = -1e30
FACTOR = 1.0 / math.sqrt(HEAD)
BF16 = jnp.bfloat16
F32 = jnp.float32


def dot(a, b, dims=((1,), (0,))):
    return lax.dot_general(a, b, (dims, ((), ())), preferred_element_type=F32)


def pool_matrix(rows, columns, span):
    i = lax.broadcasted_iota(jnp.int32, (rows, columns), 0)
    j = lax.broadcasted_iota(jnp.int32, (rows, columns), 1)
    return jnp.where(j // span == i, 1.0 / span, 0.0).astype(BF16)


def spread_matrix(rows, columns, span):
    i = lax.broadcasted_iota(jnp.int32, (rows, columns), 0)
    j = lax.broadcasted_iota(jnp.int32, (rows, columns), 1)
    return jnp.where(i // span == j, 1.0 / span, 0.0).astype(BF16)


def half_columns(core):
    return pl.ds(pl.multiple_of(core * HALF, HALF), HALF)


def block_at(core):
    return pl.ds(pl.multiple_of(core * BLOCK, BLOCK), BLOCK)


def split_kernel(where, q, g, k, v, out):
    other = half_columns(1 - where[0] % 2)
    out[:, 0:512] = q[:, other]
    out[:, 512:1024] = g[:, other]
    out[:, 1024:1536] = k[:, other]
    out[:, 1536:2048] = v[:, other]


def pool_kernel(where, k, v, recv, up, down):
    core = where[0] % 2
    mine = half_columns(core)
    own = jnp.concatenate([k[:, mine], v[:, mine]], axis=1)
    swapped = recv[:, 1024:2048]
    first = core == 0
    low = jnp.where(first, own, swapped)
    high = jnp.where(first, swapped, own)
    halve = pool_matrix(64, BLOCK, 2)
    up[0:128] = high
    up[128:192] = dot(halve, low).astype(BF16)
    down[0:128] = low
    down[128:192] = dot(halve, high).astype(BF16)


def coarse_kernel(where, up, down, below, above, below2, above2, other2, quad3):
    even = (where[0] // 2) % 2 == 0
    fine = jnp.concatenate([pool_matrix(32, BLOCK, 4), pool_matrix(16, BLOCK, 8)], axis=0)
    half = jnp.concatenate([pool_matrix(32, 64, 2), pool_matrix(16, 64, 4)], axis=0)
    own_low = dot(fine[32:48], down[0:128]).astype(BF16)
    own_high = dot(fine[32:48], up[0:128]).astype(BF16)
    below_low = dot(half, below[128:192]).astype(BF16)
    below_high = dot(fine, below[0:128]).astype(BF16)
    above_low = dot(fine, above[0:128]).astype(BF16)
    above_high = dot(half, above[128:192]).astype(BF16)
    b2 = jnp.concatenate([below_low[0:32], below_high[0:32]], axis=0)
    a2 = jnp.concatenate([above_low[0:32], above_high[0:32]], axis=0)
    below2[...] = b2
    above2[...] = a2
    other2[...] = jnp.where(even, a2, b2)
    own3 = jnp.concatenate([own_low, own_high], axis=0)
    b3 = jnp.concatenate([below_low[32:48], below_high[32:48]], axis=0)
    a3 = jnp.concatenate([above_low[32:48], above_high[32:48]], axis=0)
    quad3[0:32] = jnp.where(even, own3, b3)
    quad3[32:64] = jnp.where(even, a3, own3)


def attend_kernel(
    where, q, g, recv, up, down, below, above,
    m2, p2, s2, z3, x3, s3,
    out_keep, out_send, grad_own, grad_below, grad_above,
    gm2, gp2, gs2, gz3, gx3, gs3,
    queries, grads, keyvals, spread,
):
    chips = where[1] // 2
    core = where[0] % 2
    chip = where[0] // 2
    quad = chip // 2
    mine = half_columns(core)
    queries[block_at(core), :] = q[:, mine]
    queries[block_at(1 - core), :] = recv[:, 0:512]
    grads[block_at(core), :] = g[:, mine]
    grads[block_at(1 - core), :] = recv[:, 512:1024]
    keyvals[0:128] = down[0:128]
    keyvals[128:256] = up[0:128]
    keyvals[256:320] = below[128:192]
    keyvals[320:384] = above[128:192]
    for n, piece in enumerate((m2, p2, s2, z3, x3, s3)):
        keyvals[384 + 64 * n : 448 + 64 * n] = piece[...]
    halve = pool_matrix(64, BLOCK, 2)
    keyvals[768:896] = below[0:128]
    keyvals[896:960] = dot(halve, above[0:128]).astype(BF16)
    keyvals[960:1088] = above[0:128]
    keyvals[1088:1152] = dot(halve, below[0:128]).astype(BF16)
    spread[...] = spread_matrix(BLOCK, 64, 2)

    def bias(valid, level):
        return jnp.where(valid, F32(level * LOG_TWO), F32(NEGATIVE))

    has_below = chip >= 1
    has_above = chip < chips - 1
    far2 = jnp.where(chip % 2 == 0, chip + 3, chip - 3)
    far3 = jnp.where(quad % 2 == 0, quad + 3, quad - 3)
    quads = chips // 2
    pieces = (
        (0, 256, F32(0.0)),
        (256, 64, bias(has_below, 1)),
        (320, 64, bias(has_above, 1)),
        (384, 64, bias(chip >= 2, 2)),
        (448, 64, bias(chip + 2 < chips, 2)),
        (512, 64, bias((far2 >= 0) & (far2 < chips), 2)),
        (576, 64, F32(3 * LOG_TWO)),
        (640, 64, bias(jnp.where(chip % ROW < ROW // 2, chip >= ROW, chip + ROW < chips), 3)),
        (704, 64, bias((far3 >= 0) & (far3 < quads), 3)),
    )
    side = lax.broadcasted_iota(jnp.int32, (1, 256), 1) < 128
    fine_bias = jnp.where(side, bias(has_below, 0), bias(has_above, 0))
    half_bias = jnp.where(side, bias(has_above, 1), bias(has_below, 1))
    rows_bias = jnp.concatenate(
        [jnp.full((rows, 1), value, F32) for _, rows, value in pieces], axis=0
    )
    nt = ((1,), (1,))
    tn = ((0,), (0,))
    for h in range(4):
        kc = slice(h * HEAD, (h + 1) * HEAD)
        vc = slice(HALF + h * HEAD, HALF + (h + 1) * HEAD)
        qh = queries[:, kc]
        gh = grads[:, kc]
        keys = keyvals[0:768, kc]
        values = keyvals[0:768, vc]
        keys_a = keyvals[768:960, kc]
        keys_b = keyvals[960:1152, kc]
        values_a = keyvals[768:960, vc]
        values_b = keyvals[960:1152, vc]
        extra = jnp.concatenate([dot(keys_a, qh[0:128], nt), dot(keys_b, qh[128:256], nt)], axis=1)
        scores = jnp.concatenate(
            [
                dot(keys, qh, nt) * FACTOR + rows_bias,
                extra[0:128] * FACTOR + fine_bias,
                extra[128:192] * FACTOR + half_bias,
            ],
            axis=0,
        )
        weights = jnp.exp(scores - jnp.max(scores, axis=0, keepdims=True))
        probs = weights * (1.0 / jnp.sum(weights, axis=0, keepdims=True))
        low = probs.astype(BF16)
        dprob = jnp.concatenate(
            [
                dot(values, gh, nt),
                jnp.concatenate(
                    [dot(values_a, gh[0:128], nt), dot(values_b, gh[128:256], nt)], axis=1
                ),
            ],
            axis=0,
        )
        delta = jnp.sum(low.astype(F32) * dprob, axis=0, keepdims=True)
        dscore = (probs * (dprob - delta)).astype(BF16)

        def back(weight, shared, part_a, part_b):
            whole = dot(shared, weight[0:768], tn)
            edges = jnp.concatenate(
                [dot(part_a, weight[768:960, 0:128], tn), dot(part_b, weight[768:960, 128:256], tn)],
                axis=1,
            )
            return (whole + edges).T

        attended = back(low, values, values_a, values_b)
        query_grad = back(dscore, keys, keys_a, keys_b) * FACTOR

        @pl.when(core == 0)
        def _():
            out_keep[:, kc] = attended[0:128]
            out_send[:, kc] = attended[128:256]
            out_keep[:, vc] = query_grad[0:128]
            out_send[:, vc] = query_grad[128:256]

        @pl.when(core == 1)
        def _():
            out_keep[:, kc] = attended[128:256]
            out_send[:, kc] = attended[0:128]
            out_keep[:, vc] = query_grad[128:256]
            out_send[:, vc] = query_grad[0:128]

        for columns, weight, rows, scale in ((kc, dscore, qh, FACTOR), (vc, low, gh, 1.0)):
            shared = dot(weight[0:768], rows) * scale
            part_a = dot(weight[768:960, 0:128], rows[0:128]) * scale
            part_b = dot(weight[768:960, 128:256], rows[128:256]) * scale
            grad_own[:, columns] = shared[0:256]
            terms = shared.astype(BF16)
            grad_below[0:128, columns] = (
                part_a[0:128] + dot(spread[...], part_b[128:192].astype(BF16))
            ).astype(BF16)
            grad_below[128:192, columns] = terms[256:320]
            grad_above[0:128, columns] = (
                part_b[0:128] + dot(spread[...], part_a[128:192].astype(BF16))
            ).astype(BF16)
            grad_above[128:192, columns] = terms[320:384]
            for n, piece in enumerate((gm2, gp2, gs2, gz3, gx3, gs3)):
                piece[:, columns] = terms[384 + 64 * n : 448 + 64 * n]


def fold_kernel(where, grad_below, grad_above, from2, to2, other2, z3, s3, out_below, out_above):
    even = (where[0] // 2) % 2 == 0

    def weigh(matrix, use):
        return jnp.where(use, matrix, jnp.zeros_like(matrix))

    def fold(base, pieces2, rows, use, fine, half, out):
        def rows_of(n):
            return jnp.concatenate(
                [piece[32 * n : 32 * n + 32] for piece in (pieces2, other2)]
                + [piece[rows + 16 * n : rows + 16 * n + 16] for piece in (z3, s3)],
                axis=0,
            )

        fine_matrix = jnp.concatenate(
            [spread_matrix(128, 32, 4), weigh(spread_matrix(128, 32, 4), use)]
            + [weigh(spread_matrix(128, 16, 8), use)] * 2,
            axis=1,
        )
        half_matrix = jnp.concatenate(
            [spread_matrix(64, 32, 2), weigh(spread_matrix(64, 32, 2), use)]
            + [weigh(spread_matrix(64, 16, 4), use)] * 2,
            axis=1,
        )
        out[0:128] = (base[0:128].astype(F32) + dot(fine_matrix, rows_of(fine))).astype(BF16)
        out[128:192] = (base[128:192].astype(F32) + dot(half_matrix, rows_of(half))).astype(BF16)

    fold(grad_below, from2, 0, jnp.logical_not(even), 1, 0, out_below)
    fold(grad_above, to2, 32, even, 0, 1, out_above)


def total_kernel(where, own, from_below, from_above, z3, s3, keep, send):
    core = where[0] % 2
    row = pl.multiple_of((where[0] // 2) % 2 * 32, 32)
    matrix = jnp.concatenate(
        [spread_matrix(BLOCK, 64, 2)] + [spread_matrix(BLOCK, 16, 8)] * 2, axis=1
    )
    own_z = z3[pl.ds(row, 32), :]
    own_s = s3[pl.ds(row, 32), :]
    totals = []
    for n, (fine, half) in enumerate(((from_below, from_above), (from_above, from_below))):
        stack = jnp.concatenate(
            [half[128:192], own_z[16 * n : 16 * n + 16], own_s[16 * n : 16 * n + 16]], axis=0
        )
        totals.append(
            own[BLOCK * n : BLOCK * (n + 1)] + fine[0:128].astype(F32) + dot(matrix, stack)
        )
    first = core == 0
    keep[...] = jnp.where(first, totals[0], totals[1])
    send[...] = jnp.where(first, totals[1], totals[0])


def join_kernel(where, out_keep, out_recv, grad_keep, grad_recv, attended, qg, kg, vg):
    core = where[0] % 2
    mine = half_columns(core)
    other = half_columns(1 - core)
    attended[:, mine] = out_keep[:, 0:512].astype(BF16)
    attended[:, other] = out_recv[:, 0:512].astype(BF16)
    qg[:, mine] = out_keep[:, 512:1024]
    qg[:, other] = out_recv[:, 512:1024]
    kg[:, mine] = grad_keep[:, 0:512]
    kg[:, other] = grad_recv[:, 0:512]
    vg[:, mine] = grad_keep[:, 512:1024]
    vg[:, other] = grad_recv[:, 512:1024]


def call(kernel, where, args, outs, scratch=(), flops=0):
    return pl.pallas_call(
        kernel,
        out_shape=[jax.ShapeDtypeStruct(shape, dtype) for shape, dtype in outs],
        in_specs=[pl.BlockSpec(memory_space=pltpu.SMEM)]
        + [pl.BlockSpec(memory_space=pltpu.VMEM)] * len(args),
        out_specs=[pl.BlockSpec(memory_space=pltpu.VMEM)] * len(outs),
        scratch_shapes=list(scratch),
        compiler_params=pltpu.CompilerParams(vmem_limit_bytes=48 * 1024 * 1024),
    )(where, *args)


def sources():
    def opposite(p):
        turn = ROW // 2 + 1 if p % 2 == 0 else ROW // 2 - 1
        return p - p % ROW + (p + turn) % ROW

    return {
        "below": lambda p: p - 1,
        "above": lambda p: p + 1,
        "far2": lambda p: p + 2 if p % 2 == 0 else p - 2,
        "z3": opposite,
        "x3": lambda p: p - ROW if p % ROW < ROW // 2 else p + ROW,
        "s3": lambda p: p + 6 if p // 2 % 2 == 0 else p - 6,
    }


def on_device(query_rows, key_rows, value_rows, out_grad):
    position = lax.axis_index(AXES)
    devices = lax.axis_size(AXES)
    chips = devices // 2
    plan = sources()
    where = jnp.stack([position, jnp.int32(devices)]).astype(jnp.int32)

    def swap(x):
        return lax.ppermute(x, AXES, [(i, i ^ 1) for i in range(devices)])

    def pairs(name):
        found = []
        for chip in range(chips):
            source = plan[name](chip)
            if not 0 <= source < chips:
                continue
            found += [(2 * source + core, 2 * chip + core) for core in range(2)]
        return found

    def fetch(x, name):
        return lax.ppermute(x, AXES, pairs(name))

    def give(x, name):
        return lax.ppermute(x, AXES, [(b, a) for a, b in pairs(name)])

    (sent,) = call(
        split_kernel, where, (query_rows, out_grad, key_rows, value_rows), [((BLOCK, 2048), BF16)]
    )
    recv = swap(sent)
    up, down = call(
        pool_kernel,
        where,
        (key_rows, value_rows, recv),
        [((192, PAIR), BF16)] * 2,
    )
    below = fetch(up, "below")
    above = fetch(down, "above")
    below2, above2, other2, quad3 = call(
        coarse_kernel, where, (up, down, below, above), [((64, PAIR), BF16)] * 4
    )
    z3 = fetch(quad3, "z3")
    s3 = fetch(quad3, "s3")
    s2 = fetch(other2, "far2")
    m2 = fetch(below2, "below")
    p2 = fetch(above2, "above")
    x3 = fetch(z3, "x3")
    result = call(
        attend_kernel,
        where,
        (query_rows, out_grad, recv, up, down, below, above, m2, p2, s2, z3, x3, s3),
        [
            ((BLOCK, PAIR), F32),
            ((BLOCK, PAIR), F32),
            ((2 * BLOCK, PAIR), F32),
            ((192, PAIR), BF16),
            ((192, PAIR), BF16),
        ]
        + [((64, PAIR), BF16)] * 6,
        scratch=[
            pltpu.VMEM((2 * BLOCK, HALF), BF16),
            pltpu.VMEM((2 * BLOCK, HALF), BF16),
            pltpu.VMEM((1152, PAIR), BF16),
            pltpu.VMEM((BLOCK, 64), BF16),
        ],
    )
    out_keep, out_send, grad_own, grad_below, grad_above, gm2, gp2, gs2, gz3, gx3, gs3 = result
    out_recv = swap(out_send)
    gz3 = gz3 + give(gx3, "x3")
    back_z3 = give(gz3, "z3")
    back_s3 = give(gs3, "s3")
    back_s2 = give(gs2, "far2")
    back_m2 = give(gm2, "below")
    back_p2 = give(gp2, "above")
    fold_below, fold_above = call(
        fold_kernel,
        where,
        (grad_below, grad_above, back_m2, back_p2, back_s2, back_z3, back_s3),
        [((192, PAIR), BF16)] * 2,
    )
    from_above = give(fold_below, "below")
    from_below = give(fold_above, "above")
    grad_keep, grad_send = call(
        total_kernel,
        where,
        (grad_own, from_below, from_above, back_z3, back_s3),
        [((BLOCK, PAIR), F32), ((BLOCK, PAIR), F32)],
    )
    grad_recv = swap(grad_send)
    return tuple(
        call(
            join_kernel,
            where,
            (out_keep, out_recv, grad_keep, grad_recv),
            [((BLOCK, PAIR), BF16)] + [((BLOCK, PAIR), F32)] * 3,
        )
    )


def solution(mesh):
    spec = P(AXES, None)
    return jax.shard_map(
        on_device, mesh=mesh, in_specs=(spec,) * 4, out_specs=(spec,) * 4, check_vma=False
    )
```

```python
import math

import jax
import jax.numpy as jnp
from jax import lax
from jax.experimental import pallas as pl
from jax.experimental.pallas import tpu as pltpu
from jax.sharding import PartitionSpec as P

HEADS = 8
HEAD = 128
LEVELS = 3
BLOCK = 128
HALF = 512
PAIR = 1024
ROW = 8
AXES = ("outer", "seq")
LOG_TWO = math.log(2.0)
NEGATIVE = -1e30
FACTOR = 1.0 / math.sqrt(HEAD)
BF16 = jnp.bfloat16
F32 = jnp.float32


def dot(a, b, dims=((1,), (0,))):
    return lax.dot_general(a, b, (dims, ((), ())), preferred_element_type=F32)


def pool_matrix(rows, columns, span):
    i = lax.broadcasted_iota(jnp.int32, (rows, columns), 0)
    j = lax.broadcasted_iota(jnp.int32, (rows, columns), 1)
    return jnp.where(j // span == i, 1.0 / span, 0.0).astype(BF16)


def spread_matrix(rows, columns, span):
    i = lax.broadcasted_iota(jnp.int32, (rows, columns), 0)
    j = lax.broadcasted_iota(jnp.int32, (rows, columns), 1)
    return jnp.where(i // span == j, 1.0 / span, 0.0).astype(BF16)


def half_columns(core):
    return pl.ds(pl.multiple_of(core * HALF, HALF), HALF)


def block_at(core):
    return pl.ds(pl.multiple_of(core * BLOCK, BLOCK), BLOCK)


def split_kernel(where, a, b, out):
    other = half_columns(1 - where[0] % 2)
    out[:, 0:512] = a[:, other]
    out[:, 512:1024] = b[:, other]


def pool_kernel(where, k, v, recv, up, down):
    first = where[0] % 2 == 0
    mine = half_columns(where[0] % 2)
    own = jnp.concatenate([k[:, mine], v[:, mine]], axis=1)
    swapped = recv[...]
    low = jnp.where(first, own, swapped)
    high = jnp.where(first, swapped, own)
    halve = pool_matrix(64, BLOCK, 2)
    up[0:128] = high
    up[128:192] = dot(halve, low).astype(BF16)
    down[0:128] = low
    down[128:192] = dot(halve, high).astype(BF16)


def coarse_kernel(where, up, down, below, above, below2, above2, other2, quad3):
    even = (where[0] // 2) % 2 == 0
    fine = jnp.concatenate([pool_matrix(32, BLOCK, 4), pool_matrix(16, BLOCK, 8)], axis=0)
    half = jnp.concatenate([pool_matrix(32, 64, 2), pool_matrix(16, 64, 4)], axis=0)
    own_low = dot(fine[32:48], down[0:128]).astype(BF16)
    own_high = dot(fine[32:48], up[0:128]).astype(BF16)
    below_low = dot(half, below[128:192]).astype(BF16)
    below_high = dot(fine, below[0:128]).astype(BF16)
    above_low = dot(fine, above[0:128]).astype(BF16)
    above_high = dot(half, above[128:192]).astype(BF16)
    b2 = jnp.concatenate([below_low[0:32], below_high[0:32]], axis=0)
    a2 = jnp.concatenate([above_low[0:32], above_high[0:32]], axis=0)
    below2[...] = b2
    above2[...] = a2
    other2[...] = jnp.where(even, a2, b2)
    own3 = jnp.concatenate([own_low, own_high], axis=0)
    b3 = jnp.concatenate([below_low[32:48], below_high[32:48]], axis=0)
    a3 = jnp.concatenate([above_low[32:48], above_high[32:48]], axis=0)
    quad3[0:32] = jnp.where(even, own3, b3)
    quad3[32:64] = jnp.where(even, a3, own3)


def attend_kernel(
    where, q, g, recv, up, down, below, above,
    m2, p2, s2, z3, x3, s3,
    out_keep, out_send, grad_own, grad_below, grad_above,
    gm2, gp2, gs2, gz3, gx3, gs3,
    queries, grads, keyvals, spread,
):
    chips = where[1] // 2
    core = where[0] % 2
    chip = where[0] // 2
    quad = chip // 2
    mine = half_columns(core)
    queries[block_at(core), :] = q[:, mine]
    queries[block_at(1 - core), :] = recv[:, 0:512]
    grads[block_at(core), :] = g[:, mine]
    grads[block_at(1 - core), :] = recv[:, 512:1024]
    keyvals[0:128] = down[0:128]
    keyvals[128:256] = up[0:128]
    keyvals[256:320] = below[128:192]
    keyvals[320:384] = above[128:192]
    for n, piece in enumerate((m2, p2, s2, z3, x3, s3)):
        keyvals[384 + 64 * n : 448 + 64 * n] = piece[...]
    halve = pool_matrix(64, BLOCK, 2)
    keyvals[768:896] = below[0:128]
    keyvals[896:960] = dot(halve, above[0:128]).astype(BF16)
    keyvals[960:1088] = above[0:128]
    keyvals[1088:1152] = dot(halve, below[0:128]).astype(BF16)
    spread[...] = spread_matrix(BLOCK, 64, 2)

    def bias(valid, level):
        return jnp.where(valid, F32(level * LOG_TWO), F32(NEGATIVE))

    has_below = chip >= 1
    has_above = chip < chips - 1
    far2 = jnp.where(chip % 2 == 0, chip + 3, chip - 3)
    far3 = jnp.where(quad % 2 == 0, quad + 3, quad - 3)
    quads = chips // 2
    pieces = (
        (0, 256, F32(0.0)),
        (256, 64, bias(has_below, 1)),
        (320, 64, bias(has_above, 1)),
        (384, 64, bias(chip >= 2, 2)),
        (448, 64, bias(chip + 2 < chips, 2)),
        (512, 64, bias((far2 >= 0) & (far2 < chips), 2)),
        (576, 64, F32(3 * LOG_TWO)),
        (640, 64, bias(jnp.where(chip % ROW < ROW // 2, chip >= ROW, chip + ROW < chips), 3)),
        (704, 64, bias((far3 >= 0) & (far3 < quads), 3)),
    )
    side = lax.broadcasted_iota(jnp.int32, (1, 256), 1) < 128
    fine_bias = jnp.where(side, bias(has_below, 0), bias(has_above, 0))
    half_bias = jnp.where(side, bias(has_above, 1), bias(has_below, 1))
    rows_bias = jnp.concatenate(
        [jnp.full((rows, 1), value, F32) for _, rows, value in pieces], axis=0
    )
    nt = ((1,), (1,))
    tn = ((0,), (0,))
    for h in range(4):
        kc = slice(h * HEAD, (h + 1) * HEAD)
        vc = slice(HALF + h * HEAD, HALF + (h + 1) * HEAD)
        qh = queries[:, kc]
        gh = grads[:, kc]
        keys = keyvals[0:768, kc]
        values = keyvals[0:768, vc]
        keys_a = keyvals[768:960, kc]
        keys_b = keyvals[960:1152, kc]
        values_a = keyvals[768:960, vc]
        values_b = keyvals[960:1152, vc]
        extra = jnp.concatenate([dot(keys_a, qh[0:128], nt), dot(keys_b, qh[128:256], nt)], axis=1)
        scores = jnp.concatenate(
            [
                dot(keys, qh, nt) * FACTOR + rows_bias,
                extra[0:128] * FACTOR + fine_bias,
                extra[128:192] * FACTOR + half_bias,
            ],
            axis=0,
        )
        weights = jnp.exp(scores - jnp.max(scores, axis=0, keepdims=True))
        probs = weights * (1.0 / jnp.sum(weights, axis=0, keepdims=True))
        low = probs.astype(BF16)
        dprob = jnp.concatenate(
            [
                dot(values, gh, nt),
                jnp.concatenate(
                    [dot(values_a, gh[0:128], nt), dot(values_b, gh[128:256], nt)], axis=1
                ),
            ],
            axis=0,
        )
        delta = jnp.sum(low.astype(F32) * dprob, axis=0, keepdims=True)
        dscore = (probs * (dprob - delta)).astype(BF16)

        def back(weight, shared, part_a, part_b):
            whole = dot(shared, weight[0:768], tn)
            edges = jnp.concatenate(
                [dot(part_a, weight[768:960, 0:128], tn), dot(part_b, weight[768:960, 128:256], tn)],
                axis=1,
            )
            return (whole + edges).T

        attended = back(low, values, values_a, values_b)
        query_grad = back(dscore, keys, keys_a, keys_b) * FACTOR

        @pl.when(core == 0)
        def _():
            out_keep[:, kc] = attended[0:128]
            out_send[:, kc] = attended[128:256]
            out_keep[:, vc] = query_grad[0:128]
            out_send[:, vc] = query_grad[128:256]

        @pl.when(core == 1)
        def _():
            out_keep[:, kc] = attended[128:256]
            out_send[:, kc] = attended[0:128]
            out_keep[:, vc] = query_grad[128:256]
            out_send[:, vc] = query_grad[0:128]

        for columns, weight, rows, scale in ((kc, dscore, qh, FACTOR), (vc, low, gh, 1.0)):
            shared = dot(weight[0:768], rows) * scale
            part_a = dot(weight[768:960, 0:128], rows[0:128]) * scale
            part_b = dot(weight[768:960, 128:256], rows[128:256]) * scale
            grad_own[:, columns] = shared[0:256]
            terms = shared.astype(BF16)
            grad_below[0:128, columns] = (
                part_a[0:128] + dot(spread[...], part_b[128:192].astype(BF16))
            ).astype(BF16)
            grad_below[128:192, columns] = terms[256:320]
            grad_above[0:128, columns] = (
                part_b[0:128] + dot(spread[...], part_a[128:192].astype(BF16))
            ).astype(BF16)
            grad_above[128:192, columns] = terms[320:384]
            for n, piece in enumerate((gm2, gp2, gs2, gz3, gx3, gs3)):
                piece[:, columns] = terms[384 + 64 * n : 448 + 64 * n]


def fold_kernel(
    where, grad_below, grad_above, own, from2, to2, other2, z3, s3,
    out_below, out_above, keep, send,
):
    even = (where[0] // 2) % 2 == 0

    def weigh(matrix, use):
        return jnp.where(use, matrix, jnp.zeros_like(matrix))

    def fold(base, pieces2, rows, use, fine, half, out):
        def rows_of(n):
            return jnp.concatenate(
                [piece[32 * n : 32 * n + 32] for piece in (pieces2, other2)]
                + [piece[rows + 16 * n : rows + 16 * n + 16] for piece in (z3, s3)],
                axis=0,
            )

        fine_matrix = jnp.concatenate(
            [spread_matrix(128, 32, 4), weigh(spread_matrix(128, 32, 4), use)]
            + [weigh(spread_matrix(128, 16, 8), use)] * 2,
            axis=1,
        )
        half_matrix = jnp.concatenate(
            [spread_matrix(64, 32, 2), weigh(spread_matrix(64, 32, 2), use)]
            + [weigh(spread_matrix(64, 16, 4), use)] * 2,
            axis=1,
        )
        out[0:128] = (base[0:128].astype(F32) + dot(fine_matrix, rows_of(fine))).astype(BF16)
        out[128:192] = (base[128:192].astype(F32) + dot(half_matrix, rows_of(half))).astype(BF16)

    fold(grad_below, from2, 0, jnp.logical_not(even), 1, 0, out_below)
    fold(grad_above, to2, 32, even, 0, 1, out_above)

    row = pl.multiple_of((where[0] // 2) % 2 * 32, 32)
    own_z = z3[pl.ds(row, 32), :]
    own_s = s3[pl.ds(row, 32), :]
    matrix = jnp.concatenate([spread_matrix(BLOCK, 16, 8)] * 2, axis=1)
    totals = [
        own[BLOCK * n : BLOCK * (n + 1)]
        + dot(matrix, jnp.concatenate([x[16 * n : 16 * n + 16] for x in (own_z, own_s)], axis=0))
        for n in range(2)
    ]
    first = where[0] % 2 == 0
    keep[...] = jnp.where(first, totals[0], totals[1])
    send[...] = jnp.where(first, totals[1], totals[0])


def join_kernel(where, out_keep, out_recv, attended, qg):
    core = where[0] % 2
    mine = half_columns(core)
    other = half_columns(1 - core)
    attended[:, mine] = out_keep[:, 0:512].astype(BF16)
    attended[:, other] = out_recv[:, 0:512].astype(BF16)
    qg[:, mine] = out_keep[:, 512:1024]
    qg[:, other] = out_recv[:, 512:1024]


def final_kernel(where, keep, recv, below, above, below_recv, above_recv, kg, vg):
    core = where[0] % 2
    first = core == 0
    matrix = spread_matrix(BLOCK, 64, 2)
    sides = ((core, keep, below, above), (1 - core, recv, below_recv, above_recv))
    for half, own, low, high in sides:
        fine = jnp.where(first, low[0:128], high[0:128])
        coarse = jnp.where(first, high[128:192], low[128:192])
        total = own[...] + fine.astype(F32) + dot(matrix, coarse)
        columns = half_columns(half)
        kg[:, columns] = total[:, 0:512]
        vg[:, columns] = total[:, 512:1024]


def call(kernel, where, args, outs, scratch=(), limit=32):
    return pl.pallas_call(
        kernel,
        out_shape=[jax.ShapeDtypeStruct(shape, dtype) for shape, dtype in outs],
        in_specs=[pl.BlockSpec(memory_space=pltpu.SMEM)]
        + [pl.BlockSpec(memory_space=pltpu.VMEM)] * len(args),
        out_specs=[pl.BlockSpec(memory_space=pltpu.VMEM)] * len(outs),
        scratch_shapes=list(scratch),
        compiler_params=pltpu.CompilerParams(vmem_limit_bytes=int(limit * 1024 * 1024)),
    )(where, *args)


def sources():
    def opposite(p):
        turn = ROW // 2 + 1 if p % 2 == 0 else ROW // 2 - 1
        return p - p % ROW + (p + turn) % ROW

    return {
        "below": lambda p: p - 1,
        "above": lambda p: p + 1,
        "far2": lambda p: p + 2 if p % 2 == 0 else p - 2,
        "z3": opposite,
        "x3": lambda p: p - ROW if p % ROW < ROW // 2 else p + ROW,
        "s3": lambda p: p + 6 if p // 2 % 2 == 0 else p - 6,
    }


def on_device(query_rows, key_rows, value_rows, out_grad):
    position = lax.axis_index(AXES)
    devices = lax.axis_size(AXES)
    chips = devices // 2
    plan = sources()
    where = jnp.stack([position, jnp.int32(devices)]).astype(jnp.int32)

    def swap(x):
        return lax.ppermute(x, AXES, [(i, i ^ 1) for i in range(devices)])

    def pairs(name):
        found = []
        for chip in range(chips):
            source = plan[name](chip) % chips
            found += [(2 * source + core, 2 * chip + core) for core in range(2)]
        return found

    def fetch(x, name):
        return lax.ppermute(x, AXES, pairs(name))

    def give(x, name):
        return lax.ppermute(x, AXES, [(b, a) for a, b in pairs(name)])

    def split(a, b):
        return call(split_kernel, where, (a, b), [((BLOCK, PAIR), BF16)])[0]

    recv = swap(split(key_rows, value_rows))
    up, down = call(pool_kernel, where, (key_rows, value_rows, recv), [((192, PAIR), BF16)] * 2)
    query_rows, out_grad, up, down = lax.optimization_barrier((query_rows, out_grad, up, down))
    recv = swap(split(query_rows, out_grad))
    below = fetch(up, "below")
    above = fetch(down, "above")
    below2, above2, other2, quad3 = call(
        coarse_kernel, where, (up, down, below, above), [((64, PAIR), BF16)] * 4
    )
    z3 = fetch(quad3, "z3")
    s3 = fetch(quad3, "s3")
    s2 = fetch(other2, "far2")
    m2 = fetch(below2, "below")
    p2 = fetch(above2, "above")
    x3 = fetch(z3, "x3")
    result = call(
        attend_kernel,
        where,
        (query_rows, out_grad, recv, up, down, below, above, m2, p2, s2, z3, x3, s3),
        [
            ((BLOCK, PAIR), F32),
            ((BLOCK, PAIR), F32),
            ((2 * BLOCK, PAIR), F32),
            ((192, PAIR), BF16),
            ((192, PAIR), BF16),
        ]
        + [((64, PAIR), BF16)] * 6,
        scratch=[
            pltpu.VMEM((2 * BLOCK, HALF), BF16),
            pltpu.VMEM((2 * BLOCK, HALF), BF16),
            pltpu.VMEM((1152, PAIR), BF16),
            pltpu.VMEM((BLOCK, 64), BF16),
        ],
    )
    out_keep, out_send, grad_own, grad_below, grad_above, gm2, gp2, gs2, gz3, gx3, gs3 = result
    out_recv = swap(out_send)
    gz3, out_recv = lax.optimization_barrier((gz3 + give(gx3, "x3"), out_recv))
    back_z3 = give(gz3, "z3")
    back_s3 = give(gs3, "s3")
    back_s2 = give(gs2, "far2")
    back_m2 = give(gm2, "below")
    back_p2 = give(gp2, "above")
    attended, query_grad = call(
        join_kernel, where, (out_keep, out_recv), [((BLOCK, PAIR), BF16), ((BLOCK, PAIR), F32)]
    )
    attended, query_grad, grad_own = lax.optimization_barrier((attended, query_grad, grad_own))
    fold_below, fold_above, own_keep, own_send = call(
        fold_kernel,
        where,
        (grad_below, grad_above, grad_own, back_m2, back_p2, back_s2, back_z3, back_s3),
        [((192, PAIR), BF16)] * 2 + [((BLOCK, PAIR), F32)] * 2,
    )
    from_above = give(fold_below, "below")
    from_below = give(fold_above, "above")
    own_recv = swap(own_send)
    key_grad, value_grad = call(
        final_kernel,
        where,
        (own_keep, own_recv, from_below, from_above, swap(from_below), swap(from_above)),
        [((BLOCK, PAIR), F32)] * 2,
    )
    return attended, query_grad, key_grad, value_grad


def solution(mesh):
    spec = P(AXES, None)
    return jax.shard_map(
        on_device, mesh=mesh, in_specs=(spec,) * 4, out_specs=(spec,) * 4, check_vma=False
    )
```

```python
import math

import jax
import jax.numpy as jnp
from jax import lax
from jax.experimental import pallas as pl
from jax.experimental.pallas import tpu as pltpu
from jax.sharding import PartitionSpec as P

HEADS = 8
HEAD = 128
LEVELS = 3
BLOCK = 128
HALF = 512
PAIR = 1024
ROW = 8
AXES = ("outer", "seq")
NEGATIVE = -1e30
FACTOR = 1.0 / math.sqrt(HEAD)
FACTOR2 = FACTOR / math.log(2.0)
BF16 = jnp.bfloat16
F32 = jnp.float32


def dot(a, b, dims=((1,), (0,))):
    return lax.dot_general(a, b, (dims, ((), ())), preferred_element_type=F32)


def pool_matrix(rows, columns, span):
    i = lax.broadcasted_iota(jnp.int32, (rows, columns), 0)
    j = lax.broadcasted_iota(jnp.int32, (rows, columns), 1)
    return jnp.where(j // span == i, 1.0 / span, 0.0).astype(BF16)


def spread_matrix(rows, columns, span):
    i = lax.broadcasted_iota(jnp.int32, (rows, columns), 0)
    j = lax.broadcasted_iota(jnp.int32, (rows, columns), 1)
    return jnp.where(i // span == j, 1.0 / span, 0.0).astype(BF16)


def half_columns(core):
    return pl.ds(pl.multiple_of(core * HALF, HALF), HALF)


def block_at(core):
    return pl.ds(pl.multiple_of(core * BLOCK, BLOCK), BLOCK)


def split_kernel(where, a, b, out):
    other = half_columns(1 - where[0] % 2)
    out[:, 0:512] = a[:, other]
    out[:, 512:1024] = b[:, other]


def open_kernel(where, k, v, own, other, half_own, half_other):
    core = where[0] % 2
    halve = pool_matrix(64, BLOCK, 2)
    for half, fine, coarse in ((1 - core, other, half_other), (core, own, half_own)):
        columns = half_columns(half)
        fine[:, 0:512] = k[:, columns]
        fine[:, 512:1024] = v[:, columns]
        coarse[...] = dot(halve, fine[...]).astype(BF16)


def sides(first, own, recv, fine_same, fine_cross, half_same, half_cross):
    def pick(a, b):
        return jnp.where(first, a[...], b[...])

    return (
        pick(own, recv),
        pick(recv, own),
        pick(fine_cross, fine_same),
        pick(fine_same, fine_cross),
        pick(half_same, half_cross),
        pick(half_cross, half_same),
    )


def coarse_kernel(
    where, own, recv, fine_same, fine_cross, half_same, half_cross, below2, above2, other2, quad3
):
    even = (where[0] // 2) % 2 == 0
    first = where[0] % 2 == 0
    low, high, fine_below, fine_above, half_below, half_above = sides(
        first, own, recv, fine_same, fine_cross, half_same, half_cross
    )
    fine = jnp.concatenate([pool_matrix(32, BLOCK, 4), pool_matrix(16, BLOCK, 8)], axis=0)
    half = jnp.concatenate([pool_matrix(32, 64, 2), pool_matrix(16, 64, 4)], axis=0)
    own_low = dot(fine[32:48], low).astype(BF16)
    own_high = dot(fine[32:48], high).astype(BF16)
    below_low = dot(half, half_below).astype(BF16)
    below_high = dot(fine, fine_below).astype(BF16)
    above_low = dot(fine, fine_above).astype(BF16)
    above_high = dot(half, half_above).astype(BF16)
    b2 = jnp.concatenate([below_low[0:32], below_high[0:32]], axis=0)
    a2 = jnp.concatenate([above_low[0:32], above_high[0:32]], axis=0)
    below2[...] = b2
    above2[...] = a2
    other2[...] = jnp.where(even, a2, b2)
    own3 = jnp.concatenate([own_low, own_high], axis=0)
    b3 = jnp.concatenate([below_low[32:48], below_high[32:48]], axis=0)
    a3 = jnp.concatenate([above_low[32:48], above_high[32:48]], axis=0)
    quad3[0:32] = jnp.where(even, own3, b3)
    quad3[32:64] = jnp.where(even, a3, own3)


def attend_kernel(
    where, q, g, recv, own_kv, recv_kv, fine_same, fine_cross, half_same, half_cross,
    m2, p2, s2, z3, x3, s3,
    out_keep, out_send, grad_own, grad_below, grad_above,
    gm2, gp2, gs2, gz3, gx3, gs3,
    queries, grads, keyvals, spread, outs,
):
    chips = where[1] // 2
    core = where[0] % 2
    chip = where[0] // 2
    quad = chip // 2
    mine = half_columns(core)
    queries[block_at(core), :] = q[:, mine]
    queries[block_at(1 - core), :] = recv[:, 0:512]
    grads[block_at(core), :] = g[:, mine]
    grads[block_at(1 - core), :] = recv[:, 512:1024]
    low, high, fine_below, fine_above, half_below, half_above = sides(
        core == 0, own_kv, recv_kv, fine_same, fine_cross, half_same, half_cross
    )
    keyvals[0:128] = low
    keyvals[128:256] = high
    keyvals[256:320] = half_below
    keyvals[320:384] = half_above
    for n, piece in enumerate((m2, p2, s2, z3, x3, s3)):
        keyvals[384 + 64 * n : 448 + 64 * n] = piece[...]
    halve = pool_matrix(64, BLOCK, 2)
    keyvals[768:896] = fine_below
    keyvals[896:960] = dot(halve, fine_above).astype(BF16)
    keyvals[960:1088] = fine_above
    keyvals[1088:1152] = dot(halve, fine_below).astype(BF16)
    spread[...] = spread_matrix(BLOCK, 64, 2)

    def bias(valid, level):
        return jnp.where(valid, F32(level), F32(NEGATIVE))

    has_below = chip >= 1
    has_above = chip < chips - 1
    far2 = jnp.where(chip % 2 == 0, chip + 3, chip - 3)
    far3 = jnp.where(quad % 2 == 0, quad + 3, quad - 3)
    quads = chips // 2
    pieces = (
        (0, 256, F32(0.0)),
        (256, 64, bias(has_below, 1)),
        (320, 64, bias(has_above, 1)),
        (384, 64, bias(chip >= 2, 2)),
        (448, 64, bias(chip + 2 < chips, 2)),
        (512, 64, bias((far2 >= 0) & (far2 < chips), 2)),
        (576, 64, F32(3)),
        (640, 64, bias(jnp.where(chip % ROW < ROW // 2, chip >= ROW, chip + ROW < chips), 3)),
        (704, 64, bias((far3 >= 0) & (far3 < quads), 3)),
    )
    side = lax.broadcasted_iota(jnp.int32, (1, 256), 1) < 128
    fine_bias = jnp.where(side, bias(has_below, 0), bias(has_above, 0))
    half_bias = jnp.where(side, bias(has_above, 1), bias(has_below, 1))
    rows_bias = jnp.concatenate(
        [jnp.full((rows, 1), value, F32) for _, rows, value in pieces], axis=0
    )
    nt = ((1,), (1,))
    tn = ((0,), (0,))
    for h in range(4):
        kc = slice(h * HEAD, (h + 1) * HEAD)
        vc = slice(HALF + h * HEAD, HALF + (h + 1) * HEAD)
        qh = queries[:, kc]
        gh = grads[:, kc]
        keys = keyvals[0:768, kc]
        values = keyvals[0:768, vc]
        keys_a = keyvals[768:960, kc]
        keys_b = keyvals[960:1152, kc]
        values_a = keyvals[768:960, vc]
        values_b = keyvals[960:1152, vc]
        extra = jnp.concatenate([dot(keys_a, qh[0:128], nt), dot(keys_b, qh[128:256], nt)], axis=1)
        scores = jnp.concatenate(
            [
                dot(keys, qh, nt) * FACTOR2 + rows_bias,
                extra[0:128] * FACTOR2 + fine_bias,
                extra[128:192] * FACTOR2 + half_bias,
            ],
            axis=0,
        )
        weights = jnp.exp2(scores - jnp.max(scores, axis=0, keepdims=True))
        probs = weights * (1.0 / jnp.sum(weights, axis=0, keepdims=True))
        low = probs.astype(BF16)
        dprob = jnp.concatenate(
            [
                dot(values, gh, nt),
                jnp.concatenate(
                    [dot(values_a, gh[0:128], nt), dot(values_b, gh[128:256], nt)], axis=1
                ),
            ],
            axis=0,
        )

        def back(weight, shared, part_a, part_b):
            whole = dot(shared, weight[0:768], tn)
            edges = jnp.concatenate(
                [dot(part_a, weight[768:960, 0:128], tn), dot(part_b, weight[768:960, 128:256], tn)],
                axis=1,
            )
            return whole + edges

        attended = back(low, values, values_a, values_b)
        delta = jnp.sum(gh.astype(F32).T * attended, axis=0, keepdims=True)
        dscore = (probs * (dprob - delta)).astype(BF16)
        outs[:, kc] = attended.T
        outs[:, vc] = back(dscore, keys, keys_a, keys_b).T * FACTOR
        for columns, weight, rows, scale in ((kc, dscore, qh, FACTOR), (vc, low, gh, 1.0)):
            shared = dot(weight[0:768], rows) * scale
            part_a = dot(weight[768:960, 0:128], rows[0:128]) * scale
            part_b = dot(weight[768:960, 128:256], rows[128:256]) * scale
            grad_own[:, columns] = shared[0:256]
            terms = shared.astype(BF16)
            grad_below[0:128, columns] = (
                part_a[0:128] + dot(spread[...], part_b[128:192].astype(BF16))
            ).astype(BF16)
            grad_below[128:192, columns] = terms[256:320]
            grad_above[0:128, columns] = (
                part_b[0:128] + dot(spread[...], part_a[128:192].astype(BF16))
            ).astype(BF16)
            grad_above[128:192, columns] = terms[320:384]
            for n, piece in enumerate((gm2, gp2, gs2, gz3, gx3, gs3)):
                piece[:, columns] = terms[384 + 64 * n : 448 + 64 * n]
    out_keep[...] = outs[block_at(core), :]
    out_send[...] = outs[block_at(1 - core), :]


def fold_kernel(
    where, grad_below, grad_above, own, from2, to2, other2, z3, s3,
    out_same, out_cross, half_same, half_cross, keep, send,
):
    even = (where[0] // 2) % 2 == 0

    def weigh(matrix, use):
        return jnp.where(use, matrix, jnp.zeros_like(matrix))

    def fold(base, pieces2, rows, use, fine, half):
        def rows_of(n):
            return jnp.concatenate(
                [piece[32 * n : 32 * n + 32] for piece in (pieces2, other2)]
                + [piece[rows + 16 * n : rows + 16 * n + 16] for piece in (z3, s3)],
                axis=0,
            )

        fine_matrix = jnp.concatenate(
            [spread_matrix(128, 32, 4), weigh(spread_matrix(128, 32, 4), use)]
            + [weigh(spread_matrix(128, 16, 8), use)] * 2,
            axis=1,
        )
        half_matrix = jnp.concatenate(
            [spread_matrix(64, 32, 2), weigh(spread_matrix(64, 32, 2), use)]
            + [weigh(spread_matrix(64, 16, 4), use)] * 2,
            axis=1,
        )
        return (
            (base[0:128].astype(F32) + dot(fine_matrix, rows_of(fine))).astype(BF16),
            (base[128:192].astype(F32) + dot(half_matrix, rows_of(half))).astype(BF16),
        )

    first = where[0] % 2 == 0
    fine_below, half_below = fold(grad_below, from2, 0, jnp.logical_not(even), 1, 0)
    fine_above, half_above = fold(grad_above, to2, 32, even, 0, 1)
    out_same[...] = jnp.where(first, fine_above, fine_below)
    out_cross[...] = jnp.where(first, fine_below, fine_above)
    half_same[...] = jnp.where(first, half_below, half_above)
    half_cross[...] = jnp.where(first, half_above, half_below)

    row = pl.multiple_of((where[0] // 2) % 2 * 32, 32)
    own_z = z3[pl.ds(row, 32), :]
    own_s = s3[pl.ds(row, 32), :]
    matrix = jnp.concatenate([spread_matrix(BLOCK, 16, 8)] * 2, axis=1)
    totals = [
        own[BLOCK * n : BLOCK * (n + 1)]
        + dot(matrix, jnp.concatenate([x[16 * n : 16 * n + 16] for x in (own_z, own_s)], axis=0))
        for n in range(2)
    ]
    keep[...] = jnp.where(first, totals[0], totals[1])
    send[...] = jnp.where(first, totals[1], totals[0])


def join_kernel(where, out_keep, out_recv, attended, qg):
    core = where[0] % 2
    mine = half_columns(core)
    other = half_columns(1 - core)
    attended[:, mine] = out_keep[:, 0:512].astype(BF16)
    attended[:, other] = out_recv[:, 0:512].astype(BF16)
    qg[:, mine] = out_keep[:, 512:1024]
    qg[:, other] = out_recv[:, 512:1024]


def final_kernel(
    where, keep, recv, fine_same, fine_cross, half_same, half_cross, kg, vg
):
    core = where[0] % 2
    matrix = spread_matrix(BLOCK, 64, 2)
    for half, own, fine, coarse in (
        (core, keep, fine_same, half_same),
        (1 - core, recv, fine_cross, half_cross),
    ):
        total = own[...] + fine[...].astype(F32) + dot(matrix, coarse[...])
        columns = half_columns(half)
        kg[:, columns] = total[:, 0:512]
        vg[:, columns] = total[:, 512:1024]


def call(kernel, where, args, outs, scratch=(), limit=32):
    return pl.pallas_call(
        kernel,
        out_shape=[jax.ShapeDtypeStruct(shape, dtype) for shape, dtype in outs],
        in_specs=[pl.BlockSpec(memory_space=pltpu.SMEM)]
        + [pl.BlockSpec(memory_space=pltpu.VMEM)] * len(args),
        out_specs=[pl.BlockSpec(memory_space=pltpu.VMEM)] * len(outs),
        scratch_shapes=list(scratch),
        compiler_params=pltpu.CompilerParams(vmem_limit_bytes=int(limit * 1024 * 1024)),
    )(where, *args)


def sources():
    def opposite(p):
        turn = ROW // 2 + 1 if p % 2 == 0 else ROW // 2 - 1
        return p - p % ROW + (p + turn) % ROW

    return {
        "fine_same": lambda p, c: (p - 1, 1) if c == 1 else (p + 1, 0),
        "fine_cross": lambda p, c: (p - 1, 1) if c == 0 else (p + 1, 0),
        "half_same": lambda p, c: (p - 1, 0) if c == 0 else (p + 1, 1),
        "half_cross": lambda p, c: (p - 1, 0) if c == 1 else (p + 1, 1),
        "below": lambda p, c: (p - 1, c),
        "above": lambda p, c: (p + 1, c),
        "far2": lambda p, c: (p + 2 if p % 2 == 0 else p - 2, c),
        "z3": lambda p, c: (opposite(p), c),
        "x3": lambda p, c: (p - ROW if p % ROW < ROW // 2 else p + ROW, c),
        "s3": lambda p, c: (p + 6 if p // 2 % 2 == 0 else p - 6, c),
    }


def on_device(query_rows, key_rows, value_rows, out_grad):
    position = lax.axis_index(AXES)
    devices = lax.axis_size(AXES)
    chips = devices // 2
    plan = sources()
    where = jnp.stack([position, jnp.int32(devices)]).astype(jnp.int32)

    def swap(x):
        return lax.ppermute(x, AXES, [(i, i ^ 1) for i in range(devices)])

    def pairs(name):
        found = []
        for chip in range(chips):
            for core in range(2):
                source, side = plan[name](chip, core)
                found.append((2 * (source % chips) + side, 2 * chip + core))
        return found

    def fetch(x, name):
        return lax.ppermute(x, AXES, pairs(name))

    def give(x, name):
        return lax.ppermute(x, AXES, [(b, a) for a, b in pairs(name)])

    def split(a, b):
        return call(split_kernel, where, (a, b), [((BLOCK, PAIR), BF16)])[0]

    own_kv, other_kv, half_own, half_other = call(
        open_kernel,
        where,
        (key_rows, value_rows),
        [((BLOCK, PAIR), BF16)] * 2 + [((BLOCK // 2, PAIR), BF16)] * 2,
    )
    near = (
        fetch(own_kv, "fine_same"),
        fetch(other_kv, "fine_cross"),
        fetch(half_own, "half_same"),
        fetch(half_other, "half_cross"),
    )
    recv_kv = swap(other_kv)
    query_rows, out_grad, recv_kv = lax.optimization_barrier((query_rows, out_grad, recv_kv))
    recv = swap(split(query_rows, out_grad))
    recv, recv_kv = lax.optimization_barrier((recv, recv_kv))
    below2, above2, other2, quad3 = call(
        coarse_kernel, where, (own_kv, recv_kv, *near), [((64, PAIR), BF16)] * 4
    )
    z3 = fetch(quad3, "z3")
    s3 = fetch(quad3, "s3")
    s2 = fetch(other2, "far2")
    m2 = fetch(below2, "below")
    p2 = fetch(above2, "above")
    x3 = fetch(z3, "x3")
    result = call(
        attend_kernel,
        where,
        (query_rows, out_grad, recv, own_kv, recv_kv, *near, m2, p2, s2, z3, x3, s3),
        [
            ((BLOCK, PAIR), F32),
            ((BLOCK, PAIR), F32),
            ((2 * BLOCK, PAIR), F32),
            ((192, PAIR), BF16),
            ((192, PAIR), BF16),
        ]
        + [((64, PAIR), BF16)] * 6,
        scratch=[
            pltpu.VMEM((2 * BLOCK, HALF), BF16),
            pltpu.VMEM((2 * BLOCK, HALF), BF16),
            pltpu.VMEM((1152, PAIR), BF16),
            pltpu.VMEM((BLOCK, 64), BF16),
            pltpu.VMEM((2 * BLOCK, PAIR), F32),
        ],
    )
    out_keep, out_send, grad_own, grad_below, grad_above, gm2, gp2, gs2, gz3, gx3, gs3 = result
    out_recv = swap(out_send)
    gz3, out_recv = lax.optimization_barrier((gz3 + give(gx3, "x3"), out_recv))
    back_z3 = give(gz3, "z3")
    back_s3 = give(gs3, "s3")
    back_s2 = give(gs2, "far2")
    back_m2 = give(gm2, "below")
    back_p2 = give(gp2, "above")
    attended, query_grad = call(
        join_kernel, where, (out_keep, out_recv), [((BLOCK, PAIR), BF16), ((BLOCK, PAIR), F32)]
    )
    attended, query_grad, grad_own = lax.optimization_barrier((attended, query_grad, grad_own))
    fine_same, fine_cross, half_same, half_cross, own_keep, own_send = call(
        fold_kernel,
        where,
        (grad_below, grad_above, grad_own, back_m2, back_p2, back_s2, back_z3, back_s3),
        [((BLOCK, PAIR), BF16)] * 2
        + [((BLOCK // 2, PAIR), BF16)] * 2
        + [((BLOCK, PAIR), F32)] * 2,
    )
    fine_same = give(fine_same, "fine_same")
    fine_cross = give(fine_cross, "fine_cross")
    half_same = give(half_same, "half_same")
    half_cross = give(half_cross, "half_cross")
    own_recv = swap(own_send)
    key_grad, value_grad = call(
        final_kernel,
        where,
        (own_keep, own_recv, fine_same, fine_cross, half_same, half_cross),
        [((BLOCK, PAIR), F32)] * 2,
    )
    return attended, query_grad, key_grad, value_grad


def solution(mesh):
    spec = P(AXES, None)
    return jax.shard_map(
        on_device, mesh=mesh, in_specs=(spec,) * 4, out_specs=(spec,) * 4, check_vma=False
    )
```

```python
import math

import jax
import jax.numpy as jnp
from jax import lax
from jax.experimental import pallas as pl
from jax.experimental.pallas import tpu as pltpu
from jax.sharding import PartitionSpec as P

HEADS = 8
HEAD = 128
LEVELS = 3
BLOCK = 128
HALF = 512
PAIR = 1024
ROW = 8
AXES = ("outer", "seq")
NEGATIVE = -1e30
FACTOR = 1.0 / math.sqrt(HEAD)
FACTOR2 = FACTOR / math.log(2.0)
BF16 = jnp.bfloat16
F32 = jnp.float32


def dot(a, b, dims=((1,), (0,))):
    return lax.dot_general(a, b, (dims, ((), ())), preferred_element_type=F32)


def pool_matrix(rows, columns, span):
    i = lax.broadcasted_iota(jnp.int32, (rows, columns), 0)
    j = lax.broadcasted_iota(jnp.int32, (rows, columns), 1)
    return jnp.where(j // span == i, 1.0 / span, 0.0).astype(BF16)


def spread_matrix(rows, columns, span):
    i = lax.broadcasted_iota(jnp.int32, (rows, columns), 0)
    j = lax.broadcasted_iota(jnp.int32, (rows, columns), 1)
    return jnp.where(i // span == j, 1.0 / span, 0.0).astype(BF16)


def half_columns(core):
    return pl.ds(pl.multiple_of(core * HALF, HALF), HALF)


def block_at(core):
    return pl.ds(pl.multiple_of(core * BLOCK, BLOCK), BLOCK)


def open_kernel(where, k, v, own, other, half_own, half_other):
    core = where[0] % 2
    halve = pool_matrix(64, BLOCK, 2)
    for half, fine, coarse in ((1 - core, other, half_other), (core, own, half_own)):
        columns = half_columns(half)
        fine[:, 0:512] = k[:, columns]
        fine[:, 512:1024] = v[:, columns]
        coarse[...] = dot(halve, fine[...]).astype(BF16)


def sides(first, own, recv, fine_same, fine_cross, half_same, half_cross):
    def pick(a, b):
        return jnp.where(first, a[...], b[...])

    return (
        pick(own, recv),
        pick(recv, own),
        pick(fine_cross, fine_same),
        pick(fine_same, fine_cross),
        pick(half_same, half_cross),
        pick(half_cross, half_same),
    )


def coarse_kernel(
    where, own, recv, fine_same, fine_cross, half_same, half_cross, below2, above2, other2, quad3
):
    even = (where[0] // 2) % 2 == 0
    first = where[0] % 2 == 0
    low, high, fine_below, fine_above, half_below, half_above = sides(
        first, own, recv, fine_same, fine_cross, half_same, half_cross
    )
    fine = jnp.concatenate([pool_matrix(32, BLOCK, 4), pool_matrix(16, BLOCK, 8)], axis=0)
    half = jnp.concatenate([pool_matrix(32, 64, 2), pool_matrix(16, 64, 4)], axis=0)
    own_low = dot(fine[32:48], low).astype(BF16)
    own_high = dot(fine[32:48], high).astype(BF16)
    below_low = dot(half, half_below).astype(BF16)
    below_high = dot(fine, fine_below).astype(BF16)
    above_low = dot(fine, fine_above).astype(BF16)
    above_high = dot(half, half_above).astype(BF16)
    b2 = jnp.concatenate([below_low[0:32], below_high[0:32]], axis=0)
    a2 = jnp.concatenate([above_low[0:32], above_high[0:32]], axis=0)
    below2[...] = b2
    above2[...] = a2
    other2[...] = jnp.where(even, a2, b2)
    own3 = jnp.concatenate([own_low, own_high], axis=0)
    b3 = jnp.concatenate([below_low[32:48], below_high[32:48]], axis=0)
    a3 = jnp.concatenate([above_low[32:48], above_high[32:48]], axis=0)
    quad3[0:32] = jnp.where(even, own3, b3)
    quad3[32:64] = jnp.where(even, a3, own3)


def attend_kernel(
    where, q, g, recv_q, recv_g, own_kv, recv_kv, fine_same, fine_cross, half_same, half_cross,
    m2, p2, s2, z3, x3, s3,
    out_keep, out_send, grad_own, grad_below, grad_above,
    gm2, gp2, gs2, gz3, gx3, gs3,
    queries, grads, keyvals, spread, outs,
):
    chips = where[1] // 2
    core = where[0] % 2
    chip = where[0] // 2
    quad = chip // 2
    mine = half_columns(core)
    queries[block_at(core), :] = q[:, mine]
    queries[block_at(1 - core), :] = recv_q[:, mine]
    grads[block_at(core), :] = g[:, mine]
    grads[block_at(1 - core), :] = recv_g[:, mine]
    low, high, fine_below, fine_above, half_below, half_above = sides(
        core == 0, own_kv, recv_kv, fine_same, fine_cross, half_same, half_cross
    )
    keyvals[0:128] = low
    keyvals[128:256] = high
    keyvals[256:320] = half_below
    keyvals[320:384] = half_above
    for n, piece in enumerate((m2, p2, s2, z3, x3, s3)):
        keyvals[384 + 64 * n : 448 + 64 * n] = piece[...]
    halve = pool_matrix(64, BLOCK, 2)
    keyvals[768:896] = fine_below
    keyvals[896:960] = dot(halve, fine_above).astype(BF16)
    keyvals[960:1088] = fine_above
    keyvals[1088:1152] = dot(halve, fine_below).astype(BF16)
    spread[...] = spread_matrix(BLOCK, 64, 2)

    def bias(valid, level):
        return jnp.where(valid, F32(level), F32(NEGATIVE))

    has_below = chip >= 1
    has_above = chip < chips - 1
    far2 = jnp.where(chip % 2 == 0, chip + 3, chip - 3)
    far3 = jnp.where(quad % 2 == 0, quad + 3, quad - 3)
    quads = chips // 2
    pieces = (
        (0, 256, F32(0.0)),
        (256, 64, bias(has_below, 1)),
        (320, 64, bias(has_above, 1)),
        (384, 64, bias(chip >= 2, 2)),
        (448, 64, bias(chip + 2 < chips, 2)),
        (512, 64, bias((far2 >= 0) & (far2 < chips), 2)),
        (576, 64, F32(3)),
        (640, 64, bias(jnp.where(chip % ROW < ROW // 2, chip >= ROW, chip + ROW < chips), 3)),
        (704, 64, bias((far3 >= 0) & (far3 < quads), 3)),
    )
    side = lax.broadcasted_iota(jnp.int32, (1, 256), 1) < 128
    fine_bias = jnp.where(side, bias(has_below, 0), bias(has_above, 0))
    half_bias = jnp.where(side, bias(has_above, 1), bias(has_below, 1))
    rows_bias = jnp.concatenate(
        [jnp.full((rows, 1), value, F32) for _, rows, value in pieces], axis=0
    )
    nt = ((1,), (1,))
    tn = ((0,), (0,))
    for h in range(4):
        kc = slice(h * HEAD, (h + 1) * HEAD)
        vc = slice(HALF + h * HEAD, HALF + (h + 1) * HEAD)
        qh = queries[:, kc]
        gh = grads[:, kc]
        keys = keyvals[0:768, kc]
        values = keyvals[0:768, vc]
        keys_a = keyvals[768:960, kc]
        keys_b = keyvals[960:1152, kc]
        values_a = keyvals[768:960, vc]
        values_b = keyvals[960:1152, vc]
        extra = jnp.concatenate([dot(keys_a, qh[0:128], nt), dot(keys_b, qh[128:256], nt)], axis=1)
        scores = jnp.concatenate(
            [
                dot(keys, qh, nt) * FACTOR2 + rows_bias,
                extra[0:128] * FACTOR2 + fine_bias,
                extra[128:192] * FACTOR2 + half_bias,
            ],
            axis=0,
        )
        weights = jnp.exp2(scores - jnp.max(scores, axis=0, keepdims=True))
        probs = weights * (1.0 / jnp.sum(weights, axis=0, keepdims=True))
        low = probs.astype(BF16)
        dprob = jnp.concatenate(
            [
                dot(values, gh, nt),
                jnp.concatenate(
                    [dot(values_a, gh[0:128], nt), dot(values_b, gh[128:256], nt)], axis=1
                ),
            ],
            axis=0,
        )

        def back(weight, shared, part_a, part_b):
            whole = dot(shared, weight[0:768], tn)
            edges = jnp.concatenate(
                [dot(part_a, weight[768:960, 0:128], tn), dot(part_b, weight[768:960, 128:256], tn)],
                axis=1,
            )
            return whole + edges

        attended = back(low, values, values_a, values_b)
        delta = jnp.sum(gh.astype(F32).T * attended, axis=0, keepdims=True)
        dscore = (probs * (dprob - delta)).astype(BF16)
        outs[:, kc] = attended.T
        outs[:, vc] = back(dscore, keys, keys_a, keys_b).T * FACTOR
        for columns, weight, rows, scale in ((kc, dscore, qh, FACTOR), (vc, low, gh, 1.0)):
            shared = dot(weight[0:768], rows) * scale
            part_a = dot(weight[768:960, 0:128], rows[0:128]) * scale
            part_b = dot(weight[768:960, 128:256], rows[128:256]) * scale
            grad_own[:, columns] = shared[0:256]
            terms = shared.astype(BF16)
            grad_below[0:128, columns] = (
                part_a[0:128] + dot(spread[...], part_b[128:192].astype(BF16))
            ).astype(BF16)
            grad_below[128:192, columns] = terms[256:320]
            grad_above[0:128, columns] = (
                part_b[0:128] + dot(spread[...], part_a[128:192].astype(BF16))
            ).astype(BF16)
            grad_above[128:192, columns] = terms[320:384]
            for n, piece in enumerate((gm2, gp2, gs2, gz3, gx3, gs3)):
                piece[:, columns] = terms[384 + 64 * n : 448 + 64 * n]
    out_keep[...] = outs[block_at(core), :]
    out_send[...] = outs[block_at(1 - core), :]


def fold_kernel(
    where, grad_below, grad_above, own, s3, z3, from2, to2, other2,
    out_same, out_cross, half_same, half_cross, keep, send,
):
    even = (where[0] // 2) % 2 == 0

    def weigh(matrix, use):
        return jnp.where(use, matrix, jnp.zeros_like(matrix))

    def fold(base, pieces2, rows, use, fine, half):
        def rows_of(n):
            return jnp.concatenate(
                [piece[32 * n : 32 * n + 32] for piece in (pieces2, other2)]
                + [piece[rows + 16 * n : rows + 16 * n + 16] for piece in (z3, s3)],
                axis=0,
            )

        fine_matrix = jnp.concatenate(
            [spread_matrix(128, 32, 4), weigh(spread_matrix(128, 32, 4), use)]
            + [weigh(spread_matrix(128, 16, 8), use)] * 2,
            axis=1,
        )
        half_matrix = jnp.concatenate(
            [spread_matrix(64, 32, 2), weigh(spread_matrix(64, 32, 2), use)]
            + [weigh(spread_matrix(64, 16, 4), use)] * 2,
            axis=1,
        )
        return (
            (base[0:128].astype(F32) + dot(fine_matrix, rows_of(fine))).astype(BF16),
            (base[128:192].astype(F32) + dot(half_matrix, rows_of(half))).astype(BF16),
        )

    first = where[0] % 2 == 0
    fine_below, half_below = fold(grad_below, from2, 0, jnp.logical_not(even), 1, 0)
    fine_above, half_above = fold(grad_above, to2, 32, even, 0, 1)
    out_same[...] = jnp.where(first, fine_above, fine_below)
    out_cross[...] = jnp.where(first, fine_below, fine_above)
    half_same[...] = jnp.where(first, half_below, half_above)
    half_cross[...] = jnp.where(first, half_above, half_below)

    row = pl.multiple_of((where[0] // 2) % 2 * 32, 32)
    own_z = z3[pl.ds(row, 32), :]
    own_s = s3[pl.ds(row, 32), :]
    matrix = jnp.concatenate([spread_matrix(BLOCK, 16, 8)] * 2, axis=1)
    totals = [
        own[BLOCK * n : BLOCK * (n + 1)]
        + dot(matrix, jnp.concatenate([x[16 * n : 16 * n + 16] for x in (own_z, own_s)], axis=0))
        for n in range(2)
    ]
    keep[...] = jnp.where(first, totals[0], totals[1])
    send[...] = jnp.where(first, totals[1], totals[0])


def join_kernel(where, out_keep, out_recv, attended, qg):
    core = where[0] % 2
    mine = half_columns(core)
    other = half_columns(1 - core)
    attended[:, mine] = out_keep[:, 0:512].astype(BF16)
    attended[:, other] = out_recv[:, 0:512].astype(BF16)
    qg[:, mine] = out_keep[:, 512:1024]
    qg[:, other] = out_recv[:, 512:1024]


def final_kernel(
    where, keep, recv, fine_same, fine_cross, half_same, half_cross, kg, vg
):
    core = where[0] % 2
    matrix = spread_matrix(BLOCK, 64, 2)
    for half, own, fine, coarse in (
        (core, keep, fine_same, half_same),
        (1 - core, recv, fine_cross, half_cross),
    ):
        total = own[...] + fine[...].astype(F32) + dot(matrix, coarse[...])
        columns = half_columns(half)
        kg[:, columns] = total[:, 0:512]
        vg[:, columns] = total[:, 512:1024]


def call(kernel, where, args, outs, scratch=(), limit=32):
    return pl.pallas_call(
        kernel,
        out_shape=[jax.ShapeDtypeStruct(shape, dtype) for shape, dtype in outs],
        in_specs=[pl.BlockSpec(memory_space=pltpu.SMEM)]
        + [pl.BlockSpec(memory_space=pltpu.VMEM)] * len(args),
        out_specs=[pl.BlockSpec(memory_space=pltpu.VMEM)] * len(outs),
        scratch_shapes=list(scratch),
        compiler_params=pltpu.CompilerParams(vmem_limit_bytes=int(limit * 1024 * 1024)),
    )(where, *args)


def sources():
    def opposite(p):
        turn = ROW // 2 + 1 if p % 2 == 0 else ROW // 2 - 1
        return p - p % ROW + (p + turn) % ROW

    return {
        "fine_same": lambda p, c: (p - 1, 1) if c == 1 else (p + 1, 0),
        "fine_cross": lambda p, c: (p - 1, 1) if c == 0 else (p + 1, 0),
        "half_same": lambda p, c: (p - 1, 0) if c == 0 else (p + 1, 1),
        "half_cross": lambda p, c: (p - 1, 0) if c == 1 else (p + 1, 1),
        "below": lambda p, c: (p - 1, c),
        "above": lambda p, c: (p + 1, c),
        "far2": lambda p, c: (p + 2 if p % 2 == 0 else p - 2, c),
        "z3": lambda p, c: (opposite(p), c),
        "x3": lambda p, c: (p - ROW if p % ROW < ROW // 2 else p + ROW, c),
        "s3": lambda p, c: (p + 6 if p // 2 % 2 == 0 else p - 6, c),
    }


def on_device(query_rows, key_rows, value_rows, out_grad):
    position = lax.axis_index(AXES)
    devices = lax.axis_size(AXES)
    chips = devices // 2
    plan = sources()
    where = jnp.stack([position, jnp.int32(devices)]).astype(jnp.int32)

    def swap(x):
        return lax.ppermute(x, AXES, [(i, i ^ 1) for i in range(devices)])

    def pairs(name):
        found = []
        for chip in range(chips):
            for core in range(2):
                source, side = plan[name](chip, core)
                found.append((2 * (source % chips) + side, 2 * chip + core))
        return found

    def fetch(x, name):
        return lax.ppermute(x, AXES, pairs(name))

    def give(x, name):
        return lax.ppermute(x, AXES, [(b, a) for a, b in pairs(name)])

    recv_q = swap(query_rows)
    recv_g = swap(out_grad)
    own_kv, other_kv, half_own, half_other = call(
        open_kernel,
        where,
        (key_rows, value_rows),
        [((BLOCK, PAIR), BF16)] * 2 + [((BLOCK // 2, PAIR), BF16)] * 2,
    )
    recv_q, recv_g, own_kv, other_kv, half_own, half_other = lax.optimization_barrier(
        (recv_q, recv_g, own_kv, other_kv, half_own, half_other)
    )
    fine_same = fetch(own_kv, "fine_same")
    fine_cross = fetch(other_kv, "fine_cross")
    half_same = fetch(half_own, "half_same")
    half_cross = fetch(half_other, "half_cross")
    recv_kv = swap(other_kv)
    near = (fine_same, fine_cross, half_same, half_cross)
    below2, above2, other2, quad3 = call(
        coarse_kernel, where, (own_kv, recv_kv, *near), [((64, PAIR), BF16)] * 4
    )
    z3 = fetch(quad3, "z3")
    s3 = fetch(quad3, "s3")
    s2 = fetch(other2, "far2")
    m2 = fetch(below2, "below")
    p2 = fetch(above2, "above")
    x3 = fetch(z3, "x3")
    result = call(
        attend_kernel,
        where,
        (query_rows, out_grad, recv_q, recv_g, own_kv, recv_kv, *near, m2, p2, s2, z3, x3, s3),
        [
            ((BLOCK, PAIR), F32),
            ((BLOCK, PAIR), F32),
            ((2 * BLOCK, PAIR), F32),
            ((192, PAIR), BF16),
            ((192, PAIR), BF16),
        ]
        + [((64, PAIR), BF16)] * 6,
        scratch=[
            pltpu.VMEM((2 * BLOCK, HALF), BF16),
            pltpu.VMEM((2 * BLOCK, HALF), BF16),
            pltpu.VMEM((1152, PAIR), BF16),
            pltpu.VMEM((BLOCK, 64), BF16),
            pltpu.VMEM((2 * BLOCK, PAIR), F32),
        ],
    )
    out_keep, out_send, grad_own, grad_below, grad_above, gm2, gp2, gs2, gz3, gx3, gs3 = result
    out_recv = swap(out_send)
    back_s3 = give(gs3, "s3")
    gz3, out_recv, gs2, gp2 = lax.optimization_barrier(
        (gz3 + give(gx3, "x3"), out_recv, gs2, gp2)
    )
    back_z3 = give(gz3, "z3")
    back_s2 = give(gs2, "far2")
    back_m2 = give(gm2, "below")
    back_p2 = give(gp2, "above")
    attended, query_grad = call(
        join_kernel, where, (out_keep, out_recv), [((BLOCK, PAIR), BF16), ((BLOCK, PAIR), F32)]
    )
    attended, query_grad, grad_own = lax.optimization_barrier((attended, query_grad, grad_own))
    fine_same, fine_cross, half_same, half_cross, own_keep, own_send = call(
        fold_kernel,
        where,
        (grad_below, grad_above, grad_own, back_s3, back_z3, back_m2, back_p2, back_s2),
        [((BLOCK, PAIR), BF16)] * 2
        + [((BLOCK // 2, PAIR), BF16)] * 2
        + [((BLOCK, PAIR), F32)] * 2,
    )
    fine_same = give(fine_same, "fine_same")
    fine_cross = give(fine_cross, "fine_cross")
    half_same = give(half_same, "half_same")
    half_cross = give(half_cross, "half_cross")
    own_recv = swap(own_send)
    key_grad, value_grad = call(
        final_kernel,
        where,
        (own_keep, own_recv, fine_same, fine_cross, half_same, half_cross),
        [((BLOCK, PAIR), F32)] * 2,
    )
    return attended, query_grad, key_grad, value_grad


def solution(mesh):
    spec = P(AXES, None)
    return jax.shard_map(
        on_device, mesh=mesh, in_specs=(spec,) * 4, out_specs=(spec,) * 4, check_vma=False
    )
```

```python
import math

import jax
import jax.numpy as jnp
from jax import lax
from jax.experimental import pallas as pl
from jax.experimental.pallas import tpu as pltpu
from jax.sharding import PartitionSpec as P

HEADS = 8
HEAD = 128
LEVELS = 3
BLOCK = 128
HALF = 512
PAIR = 1024
ROW = 8
AXES = ("outer", "seq")
NEGATIVE = -1e30
FACTOR = 1.0 / math.sqrt(HEAD)
FACTOR2 = FACTOR / math.log(2.0)
BF16 = jnp.bfloat16
F32 = jnp.float32


def dot(a, b, dims=((1,), (0,))):
    return lax.dot_general(a, b, (dims, ((), ())), preferred_element_type=F32)


def pool_matrix(rows, columns, span):
    i = lax.broadcasted_iota(jnp.int32, (rows, columns), 0)
    j = lax.broadcasted_iota(jnp.int32, (rows, columns), 1)
    return jnp.where(j // span == i, 1.0 / span, 0.0).astype(BF16)


def spread_matrix(rows, columns, span):
    i = lax.broadcasted_iota(jnp.int32, (rows, columns), 0)
    j = lax.broadcasted_iota(jnp.int32, (rows, columns), 1)
    return jnp.where(i // span == j, 1.0 / span, 0.0).astype(BF16)


def half_columns(core):
    return pl.ds(pl.multiple_of(core * HALF, HALF), HALF)


def block_at(core):
    return pl.ds(pl.multiple_of(core * BLOCK, BLOCK), BLOCK)


def open_kernel(where, k, v, own, other, half_own, half_other):
    core = where[0] % 2
    halve = pool_matrix(64, BLOCK, 2)
    for half, fine, coarse in ((1 - core, other, half_other), (core, own, half_own)):
        columns = half_columns(half)
        fine[:, 0:512] = k[:, columns]
        fine[:, 512:1024] = v[:, columns]
        coarse[...] = dot(halve, fine[...]).astype(BF16)


def sides(first, own, recv, fine_same, fine_cross, half_same, half_cross):
    def pick(a, b):
        return jnp.where(first, a[...], b[...])

    return (
        pick(own, recv),
        pick(recv, own),
        pick(fine_cross, fine_same),
        pick(fine_same, fine_cross),
        pick(half_same, half_cross),
        pick(half_cross, half_same),
    )


def coarse_kernel(
    where, own, recv, fine_same, fine_cross, half_same, half_cross, same2, cross2, other2, quad3
):
    even = (where[0] // 2) % 2 == 0
    first = where[0] % 2 == 0
    low, high, fine_below, fine_above, half_below, half_above = sides(
        first, own, recv, fine_same, fine_cross, half_same, half_cross
    )
    fine = jnp.concatenate([pool_matrix(32, BLOCK, 4), pool_matrix(16, BLOCK, 8)], axis=0)
    half = jnp.concatenate([pool_matrix(32, 64, 2), pool_matrix(16, 64, 4)], axis=0)
    own_low = dot(fine[32:48], low).astype(BF16)
    own_high = dot(fine[32:48], high).astype(BF16)
    below_low = dot(half, half_below).astype(BF16)
    below_high = dot(fine, fine_below).astype(BF16)
    above_low = dot(fine, fine_above).astype(BF16)
    above_high = dot(half, half_above).astype(BF16)
    b2 = jnp.concatenate([below_low[0:32], below_high[0:32]], axis=0)
    a2 = jnp.concatenate([above_low[0:32], above_high[0:32]], axis=0)
    same2[...] = jnp.where(first, b2, a2)
    cross2[...] = jnp.where(first, a2, b2)
    other2[...] = jnp.where(even, a2, b2)
    own3 = jnp.concatenate([own_low, own_high], axis=0)
    b3 = jnp.concatenate([below_low[32:48], below_high[32:48]], axis=0)
    a3 = jnp.concatenate([above_low[32:48], above_high[32:48]], axis=0)
    quad3[0:32] = jnp.where(even, own3, b3)
    quad3[32:64] = jnp.where(even, a3, own3)


def attend_kernel(
    where, q, g, recv_q, recv_g, own_kv, recv_kv, fine_same, fine_cross, half_same, half_cross,
    m2, p2, s2, z3, x3, s3,
    out_keep, out_send, grad_own, grad_below, grad_above,
    gm2, gp2, gs2, gz3, gx3, gs3,
    queries, grads, keyvals, spread, outs,
):
    chips = where[1] // 2
    core = where[0] % 2
    chip = where[0] // 2
    quad = chip // 2
    mine = half_columns(core)
    queries[block_at(core), :] = q[:, mine]
    queries[block_at(1 - core), :] = recv_q[:, mine]
    grads[block_at(core), :] = g[:, mine]
    grads[block_at(1 - core), :] = recv_g[:, mine]
    low, high, fine_below, fine_above, half_below, half_above = sides(
        core == 0, own_kv, recv_kv, fine_same, fine_cross, half_same, half_cross
    )
    keyvals[0:128] = low
    keyvals[128:256] = high
    keyvals[256:320] = half_below
    keyvals[320:384] = half_above
    for n, piece in enumerate((m2, p2, s2, z3, x3, s3)):
        keyvals[384 + 64 * n : 448 + 64 * n] = piece[...]
    halve = pool_matrix(64, BLOCK, 2)
    keyvals[768:896] = fine_below
    keyvals[896:960] = dot(halve, fine_above).astype(BF16)
    keyvals[960:1088] = fine_above
    keyvals[1088:1152] = dot(halve, fine_below).astype(BF16)
    spread[...] = spread_matrix(BLOCK, 64, 2)

    def bias(valid, level):
        return jnp.where(valid, F32(level), F32(NEGATIVE))

    has_below = chip >= 1
    has_above = chip < chips - 1
    far2 = jnp.where(chip % 2 == 0, chip + 3, chip - 3)
    far3 = jnp.where(quad % 2 == 0, quad + 3, quad - 3)
    quads = chips // 2
    pieces = (
        (0, 256, F32(0.0)),
        (256, 64, bias(has_below, 1)),
        (320, 64, bias(has_above, 1)),
        (384, 64, bias(jnp.where(core == 0, chip >= 2, chip + 2 < chips), 2)),
        (448, 64, bias(jnp.where(core == 0, chip + 2 < chips, chip >= 2), 2)),
        (512, 64, bias((far2 >= 0) & (far2 < chips), 2)),
        (576, 64, F32(3)),
        (640, 64, bias(jnp.where(chip % ROW < ROW // 2, chip >= ROW, chip + ROW < chips), 3)),
        (704, 64, bias((far3 >= 0) & (far3 < quads), 3)),
    )
    side = lax.broadcasted_iota(jnp.int32, (1, 256), 1) < 128
    fine_bias = jnp.where(side, bias(has_below, 0), bias(has_above, 0))
    half_bias = jnp.where(side, bias(has_above, 1), bias(has_below, 1))
    rows_bias = jnp.concatenate(
        [jnp.full((rows, 1), value, F32) for _, rows, value in pieces], axis=0
    )
    nt = ((1,), (1,))
    tn = ((0,), (0,))
    for h in range(4):
        kc = slice(h * HEAD, (h + 1) * HEAD)
        vc = slice(HALF + h * HEAD, HALF + (h + 1) * HEAD)
        qh = queries[:, kc]
        gh = grads[:, kc]
        keys = keyvals[0:768, kc]
        values = keyvals[0:768, vc]
        keys_a = keyvals[768:960, kc]
        keys_b = keyvals[960:1152, kc]
        values_a = keyvals[768:960, vc]
        values_b = keyvals[960:1152, vc]
        extra = jnp.concatenate([dot(keys_a, qh[0:128], nt), dot(keys_b, qh[128:256], nt)], axis=1)
        scores = jnp.concatenate(
            [
                dot(keys, qh, nt) * FACTOR2 + rows_bias,
                extra[0:128] * FACTOR2 + fine_bias,
                extra[128:192] * FACTOR2 + half_bias,
            ],
            axis=0,
        )
        weights = jnp.exp2(scores - jnp.max(scores, axis=0, keepdims=True))
        probs = weights * (1.0 / jnp.sum(weights, axis=0, keepdims=True))
        low = probs.astype(BF16)
        dprob = jnp.concatenate(
            [
                dot(values, gh, nt),
                jnp.concatenate(
                    [dot(values_a, gh[0:128], nt), dot(values_b, gh[128:256], nt)], axis=1
                ),
            ],
            axis=0,
        )

        def back(weight, shared, part_a, part_b):
            whole = dot(shared, weight[0:768], tn)
            edges = jnp.concatenate(
                [dot(part_a, weight[768:960, 0:128], tn), dot(part_b, weight[768:960, 128:256], tn)],
                axis=1,
            )
            return whole + edges

        attended = back(low, values, values_a, values_b)
        delta = jnp.sum(gh.astype(F32).T * attended, axis=0, keepdims=True)
        dscore = (probs * (dprob - delta)).astype(BF16)
        outs[:, kc] = attended.T
        outs[:, vc] = back(dscore, keys, keys_a, keys_b).T * FACTOR
        for columns, weight, rows, scale in ((kc, dscore, qh, FACTOR), (vc, low, gh, 1.0)):
            shared = dot(weight[0:768], rows) * scale
            part_a = dot(weight[768:960, 0:128], rows[0:128]) * scale
            part_b = dot(weight[768:960, 128:256], rows[128:256]) * scale
            grad_own[:, columns] = shared[0:256]
            terms = shared.astype(BF16)
            grad_below[0:128, columns] = (
                part_a[0:128] + dot(spread[...], part_b[128:192].astype(BF16))
            ).astype(BF16)
            grad_below[128:192, columns] = terms[256:320]
            grad_above[0:128, columns] = (
                part_b[0:128] + dot(spread[...], part_a[128:192].astype(BF16))
            ).astype(BF16)
            grad_above[128:192, columns] = terms[320:384]
            for n, piece in enumerate((gm2, gp2, gs2, gz3, gx3, gs3)):
                piece[:, columns] = terms[384 + 64 * n : 448 + 64 * n]
    out_keep[...] = outs[block_at(core), :]
    out_send[...] = outs[block_at(1 - core), :]


def fold_kernel(
    where, grad_below, grad_above, own, s3, z3, same2, cross2, other2,
    out_same, out_cross, half_same, half_cross, keep, send,
):
    even = (where[0] // 2) % 2 == 0

    def weigh(matrix, use):
        return jnp.where(use, matrix, jnp.zeros_like(matrix))

    def fold(base, pieces2, rows, use, fine, half):
        def rows_of(n):
            return jnp.concatenate(
                [piece[32 * n : 32 * n + 32] for piece in (pieces2, other2)]
                + [piece[rows + 16 * n : rows + 16 * n + 16] for piece in (z3, s3)],
                axis=0,
            )

        fine_matrix = jnp.concatenate(
            [spread_matrix(128, 32, 4), weigh(spread_matrix(128, 32, 4), use)]
            + [weigh(spread_matrix(128, 16, 8), use)] * 2,
            axis=1,
        )
        half_matrix = jnp.concatenate(
            [spread_matrix(64, 32, 2), weigh(spread_matrix(64, 32, 2), use)]
            + [weigh(spread_matrix(64, 16, 4), use)] * 2,
            axis=1,
        )
        return (
            (base[0:128].astype(F32) + dot(fine_matrix, rows_of(fine))).astype(BF16),
            (base[128:192].astype(F32) + dot(half_matrix, rows_of(half))).astype(BF16),
        )

    first = where[0] % 2 == 0
    from2 = jnp.where(first, same2[...], cross2[...])
    to2 = jnp.where(first, cross2[...], same2[...])
    fine_below, half_below = fold(grad_below, from2, 0, jnp.logical_not(even), 1, 0)
    fine_above, half_above = fold(grad_above, to2, 32, even, 0, 1)
    out_same[...] = jnp.where(first, fine_above, fine_below)
    out_cross[...] = jnp.where(first, fine_below, fine_above)
    half_same[...] = jnp.where(first, half_below, half_above)
    half_cross[...] = jnp.where(first, half_above, half_below)

    row = pl.multiple_of((where[0] // 2) % 2 * 32, 32)
    own_z = z3[pl.ds(row, 32), :]
    own_s = s3[pl.ds(row, 32), :]
    matrix = jnp.concatenate([spread_matrix(BLOCK, 16, 8)] * 2, axis=1)
    totals = [
        own[BLOCK * n : BLOCK * (n + 1)]
        + dot(matrix, jnp.concatenate([x[16 * n : 16 * n + 16] for x in (own_z, own_s)], axis=0))
        for n in range(2)
    ]
    keep[...] = jnp.where(first, totals[0], totals[1])
    send[...] = jnp.where(first, totals[1], totals[0])


def join_kernel(where, out_keep, out_recv, attended, qg):
    core = where[0] % 2
    mine = half_columns(core)
    other = half_columns(1 - core)
    attended[:, mine] = out_keep[:, 0:512].astype(BF16)
    attended[:, other] = out_recv[:, 0:512].astype(BF16)
    qg[:, mine] = out_keep[:, 512:1024]
    qg[:, other] = out_recv[:, 512:1024]


def final_kernel(
    where, keep, recv, fine_same, fine_cross, half_same, half_cross, kg, vg
):
    core = where[0] % 2
    matrix = spread_matrix(BLOCK, 64, 2)
    for half, own, fine, coarse in (
        (core, keep, fine_same, half_same),
        (1 - core, recv, fine_cross, half_cross),
    ):
        total = own[...] + fine[...].astype(F32) + dot(matrix, coarse[...])
        columns = half_columns(half)
        kg[:, columns] = total[:, 0:512]
        vg[:, columns] = total[:, 512:1024]


def call(kernel, where, args, outs, scratch=(), limit=32):
    return pl.pallas_call(
        kernel,
        out_shape=[jax.ShapeDtypeStruct(shape, dtype) for shape, dtype in outs],
        in_specs=[pl.BlockSpec(memory_space=pltpu.SMEM)]
        + [pl.BlockSpec(memory_space=pltpu.VMEM)] * len(args),
        out_specs=[pl.BlockSpec(memory_space=pltpu.VMEM)] * len(outs),
        scratch_shapes=list(scratch),
        compiler_params=pltpu.CompilerParams(vmem_limit_bytes=int(limit * 1024 * 1024)),
    )(where, *args)


def sources(chips):
    def opposite(p):
        turn = ROW // 2 + 1 if p % 2 == 0 else ROW // 2 - 1
        return p - p % ROW + (p + turn) % ROW

    near = {
        "fine_same": lambda p, c: (p - 1, 1) if c == 1 else (p + 1, 0),
        "fine_cross": lambda p, c: (p - 1, 1) if c == 0 else (p + 1, 0),
        "half_same": lambda p, c: (p - 1, 0) if c == 0 else (p + 1, 1),
        "half_cross": lambda p, c: (p - 1, 0) if c == 1 else (p + 1, 1),
        "far2": lambda p, c: (p + 2 if p % 2 == 0 else p - 2, c),
        "z3": lambda p, c: (opposite(p), c),
        "x3": lambda p, c: (p - ROW if p % ROW < ROW // 2 else p + ROW, c),
        "s3": lambda p, c: (p + 6 if p // 2 % 2 == 0 else p - 6, c),
    }
    closing = {
        "fine_same": lambda p, c: (p, 1 - c),
        "fine_cross": lambda p, c: (p, c),
        "half_same": lambda p, c: (p, 1 - c),
        "half_cross": lambda p, c: (p, c),
        "far2": lambda p, c: (p ^ 1, c),
        "x3": lambda p, c: (p - p % ROW + ROW - 1 - p % ROW, c),
        "s3": lambda p, c: (p, c),
    }

    def source(name, p, c):
        found = near[name](p, c)
        return found if 0 <= found[0] < chips else closing[name](p, c)

    return source


def on_device(query_rows, key_rows, value_rows, out_grad):
    position = lax.axis_index(AXES)
    devices = lax.axis_size(AXES)
    chips = devices // 2
    plan = sources(chips)
    where = jnp.stack([position, jnp.int32(devices)]).astype(jnp.int32)

    def swap(x):
        return lax.ppermute(x, AXES, [(i, i ^ 1) for i in range(devices)])

    def pairs(name):
        found = []
        for chip in range(chips):
            for core in range(2):
                source, side = plan(name, chip, core)
                found.append((2 * source + side, 2 * chip + core))
        return found

    def fetch(x, name):
        return lax.ppermute(x, AXES, pairs(name))

    def give(x, name):
        return lax.ppermute(x, AXES, [(b, a) for a, b in pairs(name)])

    recv_q = swap(query_rows)
    recv_g = swap(out_grad)
    own_kv, other_kv, half_own, half_other = call(
        open_kernel,
        where,
        (key_rows, value_rows),
        [((BLOCK, PAIR), BF16)] * 2 + [((BLOCK // 2, PAIR), BF16)] * 2,
    )
    recv_q, recv_g, own_kv, other_kv, half_own, half_other = lax.optimization_barrier(
        (recv_q, recv_g, own_kv, other_kv, half_own, half_other)
    )
    fine_same = fetch(own_kv, "fine_same")
    fine_cross = fetch(other_kv, "fine_cross")
    half_same = fetch(half_own, "half_same")
    half_cross = fetch(half_other, "half_cross")
    recv_kv = swap(other_kv)
    near = (fine_same, fine_cross, half_same, half_cross)
    same2, cross2, other2, quad3 = call(
        coarse_kernel, where, (own_kv, recv_kv, *near), [((64, PAIR), BF16)] * 4
    )
    z3 = fetch(quad3, "z3")
    s3 = fetch(quad3, "s3")
    s2 = fetch(other2, "far2")
    same2 = fetch(same2, "half_same")
    cross2 = fetch(cross2, "fine_same")
    x3 = fetch(z3, "x3")
    result = call(
        attend_kernel,
        where,
        (query_rows, out_grad, recv_q, recv_g, own_kv, recv_kv, *near, same2, cross2, s2, z3, x3, s3),
        [
            ((BLOCK, PAIR), F32),
            ((BLOCK, PAIR), F32),
            ((2 * BLOCK, PAIR), F32),
            ((192, PAIR), BF16),
            ((192, PAIR), BF16),
        ]
        + [((64, PAIR), BF16)] * 6,
        scratch=[
            pltpu.VMEM((2 * BLOCK, HALF), BF16),
            pltpu.VMEM((2 * BLOCK, HALF), BF16),
            pltpu.VMEM((1152, PAIR), BF16),
            pltpu.VMEM((BLOCK, 64), BF16),
            pltpu.VMEM((2 * BLOCK, PAIR), F32),
        ],
    )
    out_keep, out_send, grad_own, grad_below, grad_above, gm2, gp2, gs2, gz3, gx3, gs3 = result
    out_recv = swap(out_send)
    back_s3 = give(gs3, "s3")
    gz3, out_recv, gs2, gp2 = lax.optimization_barrier(
        (gz3 + give(gx3, "x3"), out_recv, gs2, gp2)
    )
    back_z3 = give(gz3, "z3")
    back_s2 = give(gs2, "far2")
    back_m2 = give(gm2, "half_same")
    back_p2 = give(gp2, "fine_same")
    attended, query_grad = call(
        join_kernel, where, (out_keep, out_recv), [((BLOCK, PAIR), BF16), ((BLOCK, PAIR), F32)]
    )
    attended, query_grad, grad_own = lax.optimization_barrier((attended, query_grad, grad_own))
    fine_same, fine_cross, half_same, half_cross, own_keep, own_send = call(
        fold_kernel,
        where,
        (grad_below, grad_above, grad_own, back_s3, back_z3, back_m2, back_p2, back_s2),
        [((BLOCK, PAIR), BF16)] * 2
        + [((BLOCK // 2, PAIR), BF16)] * 2
        + [((BLOCK, PAIR), F32)] * 2,
    )
    fine_same = give(fine_same, "fine_same")
    fine_cross = give(fine_cross, "fine_cross")
    half_same = give(half_same, "half_same")
    half_cross = give(half_cross, "half_cross")
    own_recv = swap(own_send)
    key_grad, value_grad = call(
        final_kernel,
        where,
        (own_keep, own_recv, fine_same, fine_cross, half_same, half_cross),
        [((BLOCK, PAIR), F32)] * 2,
    )
    return attended, query_grad, key_grad, value_grad


def solution(mesh):
    spec = P(AXES, None)
    return jax.shard_map(
        on_device, mesh=mesh, in_specs=(spec,) * 4, out_specs=(spec,) * 4, check_vma=False
    )
```

```python
import math

import jax
import jax.numpy as jnp
from jax import lax
from jax.experimental import pallas as pl
from jax.experimental.pallas import tpu as pltpu
from jax.sharding import PartitionSpec as P

HEADS = 8
HEAD = 128
LEVELS = 3
BLOCK = 128
HALF = 512
PAIR = 1024
ROW = 8
AXES = ("outer", "seq")
NEGATIVE = -1e30
FACTOR = 1.0 / math.sqrt(HEAD)
FACTOR2 = FACTOR / math.log(2.0)
BF16 = jnp.bfloat16
F32 = jnp.float32


def dot(a, b, dims=((1,), (0,))):
    return lax.dot_general(a, b, (dims, ((), ())), preferred_element_type=F32)


def pool_matrix(rows, columns, span):
    i = lax.broadcasted_iota(jnp.int32, (rows, columns), 0)
    j = lax.broadcasted_iota(jnp.int32, (rows, columns), 1)
    return jnp.where(j // span == i, 1.0 / span, 0.0).astype(BF16)


def spread_matrix(rows, columns, span):
    i = lax.broadcasted_iota(jnp.int32, (rows, columns), 0)
    j = lax.broadcasted_iota(jnp.int32, (rows, columns), 1)
    return jnp.where(i // span == j, 1.0 / span, 0.0).astype(BF16)


def half_columns(core):
    return pl.ds(pl.multiple_of(core * HALF, HALF), HALF)


def block_at(core):
    return pl.ds(pl.multiple_of(core * BLOCK, BLOCK), BLOCK)


def open_kernel(where, k, v, own, other, half_own, half_other):
    core = where[0] % 2
    halve = pool_matrix(64, BLOCK, 2)
    for half, fine, coarse in ((1 - core, other, half_other), (core, own, half_own)):
        columns = half_columns(half)
        fine[:, 0:512] = k[:, columns]
        fine[:, 512:1024] = v[:, columns]
        coarse[...] = dot(halve, fine[...]).astype(BF16)


def sides(first, own, recv, fine_same, fine_cross, half_same, half_cross):
    def pick(a, b):
        return jnp.where(first, a[...], b[...])

    return (
        pick(own, recv),
        pick(recv, own),
        pick(fine_cross, fine_same),
        pick(fine_same, fine_cross),
        pick(half_same, half_cross),
        pick(half_cross, half_same),
    )


def coarse_kernel(
    where, own, recv, fine_same, fine_cross, half_same, half_cross, same2, cross2, other2, quad3
):
    even = (where[0] // 2) % 2 == 0
    first = where[0] % 2 == 0
    low, high, fine_below, fine_above, half_below, half_above = sides(
        first, own, recv, fine_same, fine_cross, half_same, half_cross
    )
    fine = jnp.concatenate([pool_matrix(32, BLOCK, 4), pool_matrix(16, BLOCK, 8)], axis=0)
    half = jnp.concatenate([pool_matrix(32, 64, 2), pool_matrix(16, 64, 4)], axis=0)
    own_low = dot(fine[32:48], low).astype(BF16)
    own_high = dot(fine[32:48], high).astype(BF16)
    below_low = dot(half, half_below).astype(BF16)
    below_high = dot(fine, fine_below).astype(BF16)
    above_low = dot(fine, fine_above).astype(BF16)
    above_high = dot(half, half_above).astype(BF16)
    b2 = jnp.concatenate([below_low[0:32], below_high[0:32]], axis=0)
    a2 = jnp.concatenate([above_low[0:32], above_high[0:32]], axis=0)
    same2[...] = jnp.where(first, b2, a2)
    cross2[...] = jnp.where(first, a2, b2)
    other2[...] = jnp.where(even, a2, b2)
    own3 = jnp.concatenate([own_low, own_high], axis=0)
    b3 = jnp.concatenate([below_low[32:48], below_high[32:48]], axis=0)
    a3 = jnp.concatenate([above_low[32:48], above_high[32:48]], axis=0)
    quad3[0:32] = jnp.where(even, own3, b3)
    quad3[32:64] = jnp.where(even, a3, own3)


def attend_kernel(
    where, q, g, recv_q, recv_g, own_kv, recv_kv, fine_same, fine_cross, half_same, half_cross,
    m2, p2, s2, z3, x3, s3,
    out_keep, out_send, grad_own, grad_below, grad_above,
    gm2, gp2, gs2, gz3, gx3, gs3,
    queries, grads, keyvals, spread, outs,
):
    chips = where[1] // 2
    core = where[0] % 2
    chip = where[0] // 2
    quad = chip // 2
    mine = half_columns(core)
    queries[block_at(core), :] = q[:, mine]
    queries[block_at(1 - core), :] = recv_q[:, mine]
    grads[block_at(core), :] = g[:, mine]
    grads[block_at(1 - core), :] = recv_g[:, mine]
    low, high, fine_below, fine_above, half_below, half_above = sides(
        core == 0, own_kv, recv_kv, fine_same, fine_cross, half_same, half_cross
    )
    keyvals[0:128] = low
    keyvals[128:256] = high
    keyvals[256:320] = half_below
    keyvals[320:384] = half_above
    for n, piece in enumerate((m2, p2, s2, z3, x3, s3)):
        keyvals[384 + 64 * n : 448 + 64 * n] = piece[...]
    halve = pool_matrix(64, BLOCK, 2)
    keyvals[768:896] = fine_below
    keyvals[896:960] = dot(halve, fine_above).astype(BF16)
    keyvals[960:1088] = fine_above
    keyvals[1088:1152] = dot(halve, fine_below).astype(BF16)
    spread[...] = spread_matrix(BLOCK, 64, 2)

    def bias(valid, level):
        return jnp.where(valid, F32(level), F32(NEGATIVE))

    has_below = chip >= 1
    has_above = chip < chips - 1
    far2 = jnp.where(chip % 2 == 0, chip + 3, chip - 3)
    far3 = jnp.where(quad % 2 == 0, quad + 3, quad - 3)
    quads = chips // 2
    pieces = (
        (0, 256, F32(0.0)),
        (256, 64, bias(has_below, 1)),
        (320, 64, bias(has_above, 1)),
        (384, 64, bias(jnp.where(core == 0, chip >= 2, chip + 2 < chips), 2)),
        (448, 64, bias(jnp.where(core == 0, chip + 2 < chips, chip >= 2), 2)),
        (512, 64, bias((far2 >= 0) & (far2 < chips), 2)),
        (576, 64, F32(3)),
        (640, 64, bias(jnp.where(chip % ROW < ROW // 2, chip >= ROW, chip + ROW < chips), 3)),
        (704, 64, bias((far3 >= 0) & (far3 < quads), 3)),
    )
    side = lax.broadcasted_iota(jnp.int32, (1, 256), 1) < 128
    fine_bias = jnp.where(side, bias(has_below, 0), bias(has_above, 0))
    half_bias = jnp.where(side, bias(has_above, 1), bias(has_below, 1))
    rows_bias = jnp.concatenate(
        [jnp.full((rows, 1), value, F32) for _, rows, value in pieces], axis=0
    )
    nt = ((1,), (1,))
    tn = ((0,), (0,))
    for h in range(4):
        kc = slice(h * HEAD, (h + 1) * HEAD)
        vc = slice(HALF + h * HEAD, HALF + (h + 1) * HEAD)
        qh = queries[:, kc]
        gh = grads[:, kc]
        keys = keyvals[0:768, kc]
        values = keyvals[0:768, vc]
        keys_a = keyvals[768:960, kc]
        keys_b = keyvals[960:1152, kc]
        values_a = keyvals[768:960, vc]
        values_b = keyvals[960:1152, vc]
        extra = jnp.concatenate([dot(keys_a, qh[0:128], nt), dot(keys_b, qh[128:256], nt)], axis=1)
        scores = jnp.concatenate(
            [
                dot(keys, qh, nt) * FACTOR2 + rows_bias,
                extra[0:128] * FACTOR2 + fine_bias,
                extra[128:192] * FACTOR2 + half_bias,
            ],
            axis=0,
        )
        weights = jnp.exp2(scores - jnp.max(scores, axis=0, keepdims=True))
        probs = weights * (1.0 / jnp.sum(weights, axis=0, keepdims=True))
        low = probs.astype(BF16)
        dprob = jnp.concatenate(
            [
                dot(values, gh, nt),
                jnp.concatenate(
                    [dot(values_a, gh[0:128], nt), dot(values_b, gh[128:256], nt)], axis=1
                ),
            ],
            axis=0,
        )

        def back(weight, shared, part_a, part_b):
            whole = dot(shared, weight[0:768], tn)
            edges = jnp.concatenate(
                [dot(part_a, weight[768:960, 0:128], tn), dot(part_b, weight[768:960, 128:256], tn)],
                axis=1,
            )
            return whole + edges

        attended = back(low, values, values_a, values_b)
        delta = jnp.sum(gh.astype(F32).T * attended, axis=0, keepdims=True)
        dscore = (probs * (dprob - delta)).astype(BF16)
        outs[:, kc] = attended.T
        outs[:, vc] = back(dscore, keys, keys_a, keys_b).T * FACTOR
        for columns, weight, rows, scale in ((kc, dscore, qh, FACTOR), (vc, low, gh, 1.0)):
            shared = dot(weight[0:768], rows) * scale
            part_a = dot(weight[768:960, 0:128], rows[0:128]) * scale
            part_b = dot(weight[768:960, 128:256], rows[128:256]) * scale
            grad_own[:, columns] = shared[0:256]
            terms = shared.astype(BF16)
            grad_below[0:128, columns] = (
                part_a[0:128] + dot(spread[...], part_b[128:192].astype(BF16))
            ).astype(BF16)
            grad_below[128:192, columns] = terms[256:320]
            grad_above[0:128, columns] = (
                part_b[0:128] + dot(spread[...], part_a[128:192].astype(BF16))
            ).astype(BF16)
            grad_above[128:192, columns] = terms[320:384]
            for n, piece in enumerate((gm2, gp2, gs2, gz3, gx3, gs3)):
                piece[:, columns] = terms[384 + 64 * n : 448 + 64 * n]
    out_keep[...] = outs[block_at(core), :]
    out_send[...] = outs[block_at(1 - core), :]


def fold_kernel(
    where, grad_below, grad_above, own, s3, z3, same2, cross2, other2,
    out_same, out_cross, half_same, half_cross, keep, send,
):
    even = (where[0] // 2) % 2 == 0

    def weigh(matrix, use):
        return jnp.where(use, matrix, jnp.zeros_like(matrix))

    def fold(base, pieces2, rows, use, fine, half):
        def rows_of(n):
            return jnp.concatenate(
                [piece[32 * n : 32 * n + 32] for piece in (pieces2, other2)]
                + [piece[rows + 16 * n : rows + 16 * n + 16] for piece in (z3, s3)],
                axis=0,
            )

        fine_matrix = jnp.concatenate(
            [spread_matrix(128, 32, 4), weigh(spread_matrix(128, 32, 4), use)]
            + [weigh(spread_matrix(128, 16, 8), use)] * 2,
            axis=1,
        )
        half_matrix = jnp.concatenate(
            [spread_matrix(64, 32, 2), weigh(spread_matrix(64, 32, 2), use)]
            + [weigh(spread_matrix(64, 16, 4), use)] * 2,
            axis=1,
        )
        return (
            (base[0:128].astype(F32) + dot(fine_matrix, rows_of(fine))).astype(BF16),
            (base[128:192].astype(F32) + dot(half_matrix, rows_of(half))).astype(BF16),
        )

    first = where[0] % 2 == 0
    from2 = jnp.where(first, same2[...], cross2[...])
    to2 = jnp.where(first, cross2[...], same2[...])
    fine_below, half_below = fold(grad_below, from2, 0, jnp.logical_not(even), 1, 0)
    fine_above, half_above = fold(grad_above, to2, 32, even, 0, 1)
    out_same[...] = jnp.where(first, fine_above, fine_below)
    out_cross[...] = jnp.where(first, fine_below, fine_above)
    half_same[...] = jnp.where(first, half_below, half_above)
    half_cross[...] = jnp.where(first, half_above, half_below)

    row = pl.multiple_of((where[0] // 2) % 2 * 32, 32)
    own_z = z3[pl.ds(row, 32), :]
    own_s = s3[pl.ds(row, 32), :]
    matrix = jnp.concatenate([spread_matrix(BLOCK, 16, 8)] * 2, axis=1)
    totals = [
        own[BLOCK * n : BLOCK * (n + 1)]
        + dot(matrix, jnp.concatenate([x[16 * n : 16 * n + 16] for x in (own_z, own_s)], axis=0))
        for n in range(2)
    ]
    keep[...] = jnp.where(first, totals[0], totals[1])
    send[...] = jnp.where(first, totals[1], totals[0])


def join_kernel(where, out_keep, out_recv, attended, qg):
    core = where[0] % 2
    mine = half_columns(core)
    other = half_columns(1 - core)
    attended[:, mine] = out_keep[:, 0:512].astype(BF16)
    attended[:, other] = out_recv[:, 0:512].astype(BF16)
    qg[:, mine] = out_keep[:, 512:1024]
    qg[:, other] = out_recv[:, 512:1024]


def final_kernel(
    where, keep, recv, fine_same, fine_cross, half_same, half_cross, kg, vg
):
    core = where[0] % 2
    matrix = spread_matrix(BLOCK, 64, 2)
    for half, own, fine, coarse in (
        (core, keep, fine_same, half_same),
        (1 - core, recv, fine_cross, half_cross),
    ):
        total = own[...] + fine[...].astype(F32) + dot(matrix, coarse[...])
        columns = half_columns(half)
        kg[:, columns] = total[:, 0:512]
        vg[:, columns] = total[:, 512:1024]


def call(kernel, where, args, outs, scratch=(), limit=32):
    return pl.pallas_call(
        kernel,
        out_shape=[jax.ShapeDtypeStruct(shape, dtype) for shape, dtype in outs],
        in_specs=[pl.BlockSpec(memory_space=pltpu.SMEM)]
        + [pl.BlockSpec(memory_space=pltpu.VMEM)] * len(args),
        out_specs=[pl.BlockSpec(memory_space=pltpu.VMEM)] * len(outs),
        scratch_shapes=list(scratch),
        compiler_params=pltpu.CompilerParams(vmem_limit_bytes=int(limit * 1024 * 1024)),
    )(where, *args)


def sources(chips):
    def opposite(p):
        turn = ROW // 2 + 1 if p % 2 == 0 else ROW // 2 - 1
        return p - p % ROW + (p + turn) % ROW

    near = {
        "fine_same": lambda p, c: (p - 1, 1) if c == 1 else (p + 1, 0),
        "half_same": lambda p, c: (p - 1, 0) if c == 0 else (p + 1, 1),
        "far2": lambda p, c: (p + 2 if p % 2 == 0 else p - 2, c),
        "z3": lambda p, c: (opposite(p), c),
        "x3": lambda p, c: (p - ROW if p % ROW < ROW // 2 else p + ROW, c),
        "s3": lambda p, c: (p + 6 if p // 2 % 2 == 0 else p - 6, c),
    }
    closing = {
        "fine_same": lambda p, c: (p, 1 - c),
        "half_same": lambda p, c: (p, 1 - c),
        "far2": lambda p, c: (p ^ 1, c),
        "x3": lambda p, c: (p - p % ROW + ROW - 1 - p % ROW, c),
        "s3": lambda p, c: (p ^ 1, c),
    }

    def source(name, p, c):
        found = near[name](p, c)
        return found if 0 <= found[0] < chips else closing[name](p, c)

    return source


def on_device(query_rows, key_rows, value_rows, out_grad):
    position = lax.axis_index(AXES)
    devices = lax.axis_size(AXES)
    chips = devices // 2
    plan = sources(chips)
    where = jnp.stack([position, jnp.int32(devices)]).astype(jnp.int32)

    def swap(x):
        return lax.ppermute(x, AXES, [(i, i ^ 1) for i in range(devices)])

    def pairs(name):
        found = []
        for chip in range(chips):
            for core in range(2):
                source, side = plan(name, chip, core)
                found.append((2 * source + side, 2 * chip + core))
        return found

    def fetch(x, name):
        return lax.ppermute(x, AXES, pairs(name))

    def give(x, name):
        return lax.ppermute(x, AXES, [(b, a) for a, b in pairs(name)])

    recv_q = swap(query_rows)
    recv_g = swap(out_grad)
    own_kv, other_kv, half_own, half_other = call(
        open_kernel,
        where,
        (key_rows, value_rows),
        [((BLOCK, PAIR), BF16)] * 2 + [((BLOCK // 2, PAIR), BF16)] * 2,
    )
    recv_q, recv_g, own_kv, other_kv, half_own, half_other = lax.optimization_barrier(
        (recv_q, recv_g, own_kv, other_kv, half_own, half_other)
    )
    fine_cross = swap(fetch(other_kv, "fine_same"))
    half_cross = swap(fetch(half_other, "half_same"))
    fine_same = fetch(own_kv, "fine_same")
    half_same = fetch(half_own, "half_same")
    recv_kv = swap(other_kv)
    near = (fine_same, fine_cross, half_same, half_cross)
    same2, cross2, other2, quad3 = call(
        coarse_kernel, where, (own_kv, recv_kv, *near), [((64, PAIR), BF16)] * 4
    )
    z3 = fetch(quad3, "z3")
    s3 = fetch(quad3, "s3")
    s2 = fetch(other2, "far2")
    same2 = fetch(same2, "half_same")
    cross2 = fetch(cross2, "fine_same")
    x3 = fetch(z3, "x3")
    result = call(
        attend_kernel,
        where,
        (query_rows, out_grad, recv_q, recv_g, own_kv, recv_kv, *near, same2, cross2, s2, z3, x3, s3),
        [
            ((BLOCK, PAIR), F32),
            ((BLOCK, PAIR), F32),
            ((2 * BLOCK, PAIR), F32),
            ((192, PAIR), BF16),
            ((192, PAIR), BF16),
        ]
        + [((64, PAIR), BF16)] * 6,
        scratch=[
            pltpu.VMEM((2 * BLOCK, HALF), BF16),
            pltpu.VMEM((2 * BLOCK, HALF), BF16),
            pltpu.VMEM((1152, PAIR), BF16),
            pltpu.VMEM((BLOCK, 64), BF16),
            pltpu.VMEM((2 * BLOCK, PAIR), F32),
        ],
    )
    out_keep, out_send, grad_own, grad_below, grad_above, gm2, gp2, gs2, gz3, gx3, gs3 = result
    out_recv = swap(out_send)
    back_s3 = give(gs3, "s3")
    gz3, out_recv, gs2, gp2 = lax.optimization_barrier(
        (gz3 + give(gx3, "x3"), out_recv, gs2, gp2)
    )
    back_z3 = give(gz3, "z3")
    back_s2 = give(gs2, "far2")
    back_m2 = give(gm2, "half_same")
    back_p2 = give(gp2, "fine_same")
    attended, query_grad = call(
        join_kernel, where, (out_keep, out_recv), [((BLOCK, PAIR), BF16), ((BLOCK, PAIR), F32)]
    )
    attended, query_grad, grad_own = lax.optimization_barrier((attended, query_grad, grad_own))
    fine_same, fine_cross, half_same, half_cross, own_keep, own_send = call(
        fold_kernel,
        where,
        (grad_below, grad_above, grad_own, back_s3, back_z3, back_m2, back_p2, back_s2),
        [((BLOCK, PAIR), BF16)] * 2
        + [((BLOCK // 2, PAIR), BF16)] * 2
        + [((BLOCK, PAIR), F32)] * 2,
    )
    fine_same = give(fine_same, "fine_same")
    fine_cross = give(swap(fine_cross), "fine_same")
    half_same = give(half_same, "half_same")
    half_cross = give(swap(half_cross), "half_same")
    own_recv = swap(own_send)
    key_grad, value_grad = call(
        final_kernel,
        where,
        (own_keep, own_recv, fine_same, fine_cross, half_same, half_cross),
        [((BLOCK, PAIR), F32)] * 2,
    )
    return attended, query_grad, key_grad, value_grad


def solution(mesh):
    spec = P(AXES, None)
    return jax.shard_map(
        on_device, mesh=mesh, in_specs=(spec,) * 4, out_specs=(spec,) * 4, check_vma=False
    )
```

```python
import math

import jax
import jax.numpy as jnp
from jax import lax
from jax.experimental import pallas as pl
from jax.experimental.pallas import tpu as pltpu
from jax.sharding import PartitionSpec as P

HEADS = 8
HEAD = 128
LEVELS = 3
BLOCK = 128
HALF = 512
PAIR = 1024
ROW = 8
AXES = ("outer", "seq")
NEGATIVE = -1e30
FACTOR = 1.0 / math.sqrt(HEAD)
FACTOR2 = FACTOR / math.log(2.0)
BF16 = jnp.bfloat16
F32 = jnp.float32


def dot(a, b, dims=((1,), (0,))):
    return lax.dot_general(a, b, (dims, ((), ())), preferred_element_type=F32)


def pool_matrix(rows, columns, span):
    i = lax.broadcasted_iota(jnp.int32, (rows, columns), 0)
    j = lax.broadcasted_iota(jnp.int32, (rows, columns), 1)
    return jnp.where(j // span == i, 1.0 / span, 0.0).astype(BF16)


def spread_matrix(rows, columns, span):
    i = lax.broadcasted_iota(jnp.int32, (rows, columns), 0)
    j = lax.broadcasted_iota(jnp.int32, (rows, columns), 1)
    return jnp.where(i // span == j, 1.0 / span, 0.0).astype(BF16)


def half_columns(core):
    return pl.ds(pl.multiple_of(core * HALF, HALF), HALF)


def block_at(core):
    return pl.ds(pl.multiple_of(core * BLOCK, BLOCK), BLOCK)


def open_kernel(where, k, v, own, other, half_own, half_other):
    core = where[0] % 2
    halve = pool_matrix(64, BLOCK, 2)
    for half, fine, coarse in ((1 - core, other, half_other), (core, own, half_own)):
        columns = half_columns(half)
        fine[:, 0:512] = k[:, columns]
        fine[:, 512:1024] = v[:, columns]
        coarse[...] = dot(halve, fine[...]).astype(BF16)


def sides(first, own, recv, fine_same, fine_cross, half_same, half_cross):
    def pick(a, b):
        return jnp.where(first, a[...], b[...])

    return (
        pick(own, recv),
        pick(recv, own),
        pick(fine_cross, fine_same),
        pick(fine_same, fine_cross),
        pick(half_same, half_cross),
        pick(half_cross, half_same),
    )


def coarse_kernel(
    where, own, recv, fine_same, fine_cross, half_same, half_cross, cross2, pair2, own3, quad3
):
    even = (where[0] // 2) % 2 == 0
    first = where[0] % 2 == 0
    low, high, fine_below, fine_above, half_below, half_above = sides(
        first, own, recv, fine_same, fine_cross, half_same, half_cross
    )
    fine = jnp.concatenate([pool_matrix(32, BLOCK, 4), pool_matrix(16, BLOCK, 8)], axis=0)
    half = jnp.concatenate([pool_matrix(32, 64, 2), pool_matrix(16, 64, 4)], axis=0)
    own_low = dot(fine[32:48], low).astype(BF16)
    own_high = dot(fine[32:48], high).astype(BF16)
    below_low = dot(half, half_below).astype(BF16)
    below_high = dot(fine, fine_below).astype(BF16)
    above_low = dot(fine, fine_above).astype(BF16)
    above_high = dot(half, half_above).astype(BF16)
    b2 = jnp.concatenate([below_low[0:32], below_high[0:32]], axis=0)
    a2 = jnp.concatenate([above_low[0:32], above_high[0:32]], axis=0)
    cross2[...] = jnp.where(even, a2, b2)
    pair2[...] = jnp.where(even, b2, a2)
    mine3 = jnp.concatenate([own_low, own_high], axis=0)
    own3[...] = mine3
    b3 = jnp.concatenate([below_low[32:48], below_high[32:48]], axis=0)
    a3 = jnp.concatenate([above_low[32:48], above_high[32:48]], axis=0)
    quad3[0:32] = jnp.where(even, mine3, b3)
    quad3[32:64] = jnp.where(even, a3, mine3)


def attend_kernel(
    where, q, g, recv_q, recv_g, own_kv, recv_kv, fine_same, fine_cross, half_same, half_cross,
    c2, b2, f2, z3, x3, s3, t3,
    out_keep, out_send, grad_own, grad_below, grad_above,
    gc2, gb2, gz3, gx3, gs3, gmix,
    queries, grads, keyvals, spread, outs,
):
    chips = where[1] // 2
    core = where[0] % 2
    chip = where[0] // 2
    quad = chip // 2
    mine = half_columns(core)
    queries[block_at(core), :] = q[:, mine]
    queries[block_at(1 - core), :] = recv_q[:, mine]
    grads[block_at(core), :] = g[:, mine]
    grads[block_at(1 - core), :] = recv_g[:, mine]
    low, high, fine_below, fine_above, half_below, half_above = sides(
        core == 0, own_kv, recv_kv, fine_same, fine_cross, half_same, half_cross
    )
    keyvals[0:128] = low
    keyvals[128:256] = high
    keyvals[256:320] = half_below
    keyvals[320:384] = half_above
    for n, piece in enumerate((c2, b2, f2, z3, x3)):
        keyvals[384 + 64 * n : 448 + 64 * n] = piece[...]
    keyvals[704:736] = s3[...]
    keyvals[736:768] = t3[...]
    halve = pool_matrix(64, BLOCK, 2)
    keyvals[768:896] = fine_below
    keyvals[896:960] = dot(halve, fine_above).astype(BF16)
    keyvals[960:1088] = fine_above
    keyvals[1088:1152] = dot(halve, fine_below).astype(BF16)
    spread[...] = spread_matrix(BLOCK, 64, 2)

    def bias(valid, level):
        return jnp.where(valid, F32(level), F32(NEGATIVE))

    has_below = chip >= 1
    has_above = chip < chips - 1
    far2 = jnp.where(chip % 2 == 0, chip + 3, chip - 3)
    far3 = jnp.where(quad % 2 == 0, quad + 3, quad - 3)
    quads = chips // 2
    pieces = (
        (0, 256, F32(0.0)),
        (256, 64, bias(has_below, 1)),
        (320, 64, bias(has_above, 1)),
        (384, 64, bias(jnp.where(chip % 2 == 0, chip >= 2, chip + 2 < chips), 2)),
        (448, 64, bias(jnp.where(chip % 2 == 0, chip + 2 < chips, chip >= 2), 2)),
        (512, 64, bias((far2 >= 0) & (far2 < chips), 2)),
        (576, 64, F32(3)),
        (640, 64, bias(jnp.where(chip % ROW < ROW // 2, chip >= ROW, chip + ROW < chips), 3)),
        (704, 64, bias((far3 >= 0) & (far3 < quads), 3)),
    )
    side = lax.broadcasted_iota(jnp.int32, (1, 256), 1) < 128
    fine_bias = jnp.where(side, bias(has_below, 0), bias(has_above, 0))
    half_bias = jnp.where(side, bias(has_above, 1), bias(has_below, 1))
    rows_bias = jnp.concatenate(
        [jnp.full((rows, 1), value, F32) for _, rows, value in pieces], axis=0
    )
    nt = ((1,), (1,))
    tn = ((0,), (0,))
    for h in range(4):
        kc = slice(h * HEAD, (h + 1) * HEAD)
        vc = slice(HALF + h * HEAD, HALF + (h + 1) * HEAD)
        qh = queries[:, kc]
        gh = grads[:, kc]
        keys = keyvals[0:768, kc]
        values = keyvals[0:768, vc]
        keys_a = keyvals[768:960, kc]
        keys_b = keyvals[960:1152, kc]
        values_a = keyvals[768:960, vc]
        values_b = keyvals[960:1152, vc]
        extra = jnp.concatenate([dot(keys_a, qh[0:128], nt), dot(keys_b, qh[128:256], nt)], axis=1)
        scores = jnp.concatenate(
            [
                dot(keys, qh, nt) * FACTOR2 + rows_bias,
                extra[0:128] * FACTOR2 + fine_bias,
                extra[128:192] * FACTOR2 + half_bias,
            ],
            axis=0,
        )
        weights = jnp.exp2(scores - jnp.max(scores, axis=0, keepdims=True))
        probs = weights * (1.0 / jnp.sum(weights, axis=0, keepdims=True))
        low = probs.astype(BF16)
        dprob = jnp.concatenate(
            [
                dot(values, gh, nt),
                jnp.concatenate(
                    [dot(values_a, gh[0:128], nt), dot(values_b, gh[128:256], nt)], axis=1
                ),
            ],
            axis=0,
        )

        def back(weight, shared, part_a, part_b):
            whole = dot(shared, weight[0:768], tn)
            edges = jnp.concatenate(
                [dot(part_a, weight[768:960, 0:128], tn), dot(part_b, weight[768:960, 128:256], tn)],
                axis=1,
            )
            return whole + edges

        attended = back(low, values, values_a, values_b)
        delta = jnp.sum(gh.astype(F32).T * attended, axis=0, keepdims=True)
        dscore = (probs * (dprob - delta)).astype(BF16)
        outs[:, kc] = attended.T
        outs[:, vc] = back(dscore, keys, keys_a, keys_b).T * FACTOR
        for columns, weight, rows, scale in ((kc, dscore, qh, FACTOR), (vc, low, gh, 1.0)):
            shared = dot(weight[0:768], rows) * scale
            part_a = dot(weight[768:960, 0:128], rows[0:128]) * scale
            part_b = dot(weight[768:960, 128:256], rows[128:256]) * scale
            grad_own[:, columns] = shared[0:256]
            terms = shared.astype(BF16)
            grad_below[0:128, columns] = (
                part_a[0:128] + dot(spread[...], part_b[128:192].astype(BF16))
            ).astype(BF16)
            grad_below[128:192, columns] = terms[256:320]
            grad_above[0:128, columns] = (
                part_b[0:128] + dot(spread[...], part_a[128:192].astype(BF16))
            ).astype(BF16)
            grad_above[128:192, columns] = terms[320:384]
            gc2[:, columns] = terms[384:448]
            gb2[:, columns] = terms[448:512]
            gz3[:, columns] = terms[576:640]
            gx3[:, columns] = terms[640:704]
            gs3[:, columns] = terms[704:736]
            gmix[0:64, columns] = terms[512:576]
            gmix[64:96, columns] = terms[736:768]
    out_keep[...] = outs[block_at(core), :]
    out_send[...] = outs[block_at(1 - core), :]


def fold_kernel(
    where, grad_below, grad_above, own, s3, z3, cross2, pair2,
    out_same, out_cross, half_same, half_cross, keep, send,
):
    even = (where[0] // 2) % 2 == 0

    def weigh(matrix, use):
        return jnp.where(use, matrix, jnp.zeros_like(matrix))

    def fold(base, pieces2, rows, use, fine, half):
        def rows_of(n):
            return jnp.concatenate(
                [pieces2[32 * n : 32 * n + 32], z3[rows + 16 * n : rows + 16 * n + 16]], axis=0
            )

        fine_matrix = jnp.concatenate(
            [spread_matrix(128, 32, 4), weigh(spread_matrix(128, 16, 8), use)], axis=1
        )
        half_matrix = jnp.concatenate(
            [spread_matrix(64, 32, 2), weigh(spread_matrix(64, 16, 4), use)], axis=1
        )
        return (
            (base[0:128].astype(F32) + dot(fine_matrix, rows_of(fine))).astype(BF16),
            (base[128:192].astype(F32) + dot(half_matrix, rows_of(half))).astype(BF16),
        )

    first = where[0] % 2 == 0
    from2 = jnp.where(even, pair2[...], cross2[...])
    to2 = jnp.where(even, cross2[...], pair2[...])
    fine_below, half_below = fold(grad_below, from2, 0, jnp.logical_not(even), 1, 0)
    fine_above, half_above = fold(grad_above, to2, 32, even, 0, 1)
    out_same[...] = jnp.where(first, fine_above, fine_below)
    out_cross[...] = jnp.where(first, fine_below, fine_above)
    half_same[...] = jnp.where(first, half_below, half_above)
    half_cross[...] = jnp.where(first, half_above, half_below)

    row = pl.multiple_of((where[0] // 2) % 2 * 32, 32)
    own_z = z3[pl.ds(row, 32), :]
    own_s = s3[...]
    matrix = jnp.concatenate([spread_matrix(BLOCK, 16, 8)] * 2, axis=1)
    totals = [
        own[BLOCK * n : BLOCK * (n + 1)]
        + dot(matrix, jnp.concatenate([x[16 * n : 16 * n + 16] for x in (own_z, own_s)], axis=0))
        for n in range(2)
    ]
    keep[...] = jnp.where(first, totals[0], totals[1])
    send[...] = jnp.where(first, totals[1], totals[0])


def join_kernel(where, out_keep, out_recv, attended, qg):
    core = where[0] % 2
    mine = half_columns(core)
    other = half_columns(1 - core)
    attended[:, mine] = out_keep[:, 0:512].astype(BF16)
    attended[:, other] = out_recv[:, 0:512].astype(BF16)
    qg[:, mine] = out_keep[:, 512:1024]
    qg[:, other] = out_recv[:, 512:1024]


def final_kernel(
    where, keep, recv, fine_same, fine_cross, half_same, half_cross, kg, vg
):
    core = where[0] % 2
    matrix = spread_matrix(BLOCK, 64, 2)
    for half, own, fine, coarse in (
        (core, keep, fine_same, half_same),
        (1 - core, recv, fine_cross, half_cross),
    ):
        total = own[...] + fine[...].astype(F32) + dot(matrix, coarse[...])
        columns = half_columns(half)
        kg[:, columns] = total[:, 0:512]
        vg[:, columns] = total[:, 512:1024]


def call(kernel, where, args, outs, scratch=(), limit=32):
    return pl.pallas_call(
        kernel,
        out_shape=[jax.ShapeDtypeStruct(shape, dtype) for shape, dtype in outs],
        in_specs=[pl.BlockSpec(memory_space=pltpu.SMEM)]
        + [pl.BlockSpec(memory_space=pltpu.VMEM)] * len(args),
        out_specs=[pl.BlockSpec(memory_space=pltpu.VMEM)] * len(outs),
        scratch_shapes=list(scratch),
        compiler_params=pltpu.CompilerParams(vmem_limit_bytes=int(limit * 1024 * 1024)),
    )(where, *args)


def sources(chips):
    def opposite(p):
        turn = ROW // 2 + 1 if p % 2 == 0 else ROW // 2 - 1
        return p - p % ROW + (p + turn) % ROW

    near = {
        "fine_same": lambda p, c: (p - 1, 1) if c == 1 else (p + 1, 0),
        "half_same": lambda p, c: (p - 1, 0) if c == 0 else (p + 1, 1),
        "cross": lambda p, c: (p - 1 if p % 2 == 0 else p + 1, c),
        "pair": lambda p, c: (p ^ 1, c),
        "z3": lambda p, c: (opposite(p), c),
        "x3": lambda p, c: (p - ROW if p % ROW < ROW // 2 else p + ROW, c),
        "s3": lambda p, c: (p + 6 if p // 2 % 2 == 0 else p - 6, c),
    }
    closing = {
        "fine_same": lambda p, c: (p, 1 - c),
        "half_same": lambda p, c: (p, 1 - c),
        "cross": lambda p, c: (p, 1 - c),
        "x3": lambda p, c: (p - p % ROW + ROW - 1 - p % ROW, c),
        "s3": lambda p, c: (p ^ 1, c),
    }

    def source(name, p, c):
        found = near[name](p, c)
        return found if 0 <= found[0] < chips else closing[name](p, c)

    return source


def on_device(query_rows, key_rows, value_rows, out_grad):
    position = lax.axis_index(AXES)
    devices = lax.axis_size(AXES)
    chips = devices // 2
    plan = sources(chips)
    where = jnp.stack([position, jnp.int32(devices)]).astype(jnp.int32)

    def swap(x):
        return lax.ppermute(x, AXES, [(i, i ^ 1) for i in range(devices)])

    def pairs(name):
        found = []
        for chip in range(chips):
            for core in range(2):
                source, side = plan(name, chip, core)
                found.append((2 * source + side, 2 * chip + core))
        return found

    def fetch(x, name):
        return lax.ppermute(x, AXES, pairs(name))

    def give(x, name):
        return lax.ppermute(x, AXES, [(b, a) for a, b in pairs(name)])

    recv_q = swap(query_rows)
    recv_g = swap(out_grad)
    own_kv, other_kv, half_own, half_other = call(
        open_kernel,
        where,
        (key_rows, value_rows),
        [((BLOCK, PAIR), BF16)] * 2 + [((BLOCK // 2, PAIR), BF16)] * 2,
    )
    recv_q, recv_g, own_kv, other_kv, half_own, half_other = lax.optimization_barrier(
        (recv_q, recv_g, own_kv, other_kv, half_own, half_other)
    )
    fine_cross = swap(fetch(other_kv, "fine_same"))
    half_cross = swap(fetch(half_other, "half_same"))
    fine_same = fetch(own_kv, "fine_same")
    half_same = fetch(half_own, "half_same")
    recv_kv = swap(other_kv)
    near = (fine_same, fine_cross, half_same, half_cross)
    cross2, pair2, own3, quad3 = call(
        coarse_kernel,
        where,
        (own_kv, recv_kv, *near),
        [((64, PAIR), BF16)] * 2 + [((32, PAIR), BF16), ((64, PAIR), BF16)],
    )
    z3 = fetch(quad3, "z3")
    c2 = fetch(cross2, "cross")
    s3 = fetch(own3, "s3")
    b2 = fetch(pair2, "pair")
    f2 = fetch(c2, "pair")
    t3 = fetch(s3, "pair")
    x3 = fetch(z3, "x3")
    result = call(
        attend_kernel,
        where,
        (query_rows, out_grad, recv_q, recv_g, own_kv, recv_kv, *near, c2, b2, f2, z3, x3, s3, t3),
        [
            ((BLOCK, PAIR), F32),
            ((BLOCK, PAIR), F32),
            ((2 * BLOCK, PAIR), F32),
            ((192, PAIR), BF16),
            ((192, PAIR), BF16),
        ]
        + [((64, PAIR), BF16)] * 4
        + [((32, PAIR), BF16), ((96, PAIR), BF16)],
        scratch=[
            pltpu.VMEM((2 * BLOCK, HALF), BF16),
            pltpu.VMEM((2 * BLOCK, HALF), BF16),
            pltpu.VMEM((1152, PAIR), BF16),
            pltpu.VMEM((BLOCK, 64), BF16),
            pltpu.VMEM((2 * BLOCK, PAIR), F32),
        ],
    )
    out_keep, out_send, grad_own, grad_below, grad_above, gc2, gb2, gz3, gx3, gs3, gmix = result
    out_recv = swap(out_send)
    mixed = fetch(gmix, "pair")
    gz3, out_recv = lax.optimization_barrier((gz3 + give(gx3, "x3"), out_recv))
    back_z3 = give(gz3, "z3")
    back_s3 = give(gs3 + mixed[64:96], "s3")
    back_c2 = give(gc2 + mixed[0:64], "cross")
    back_b2 = give(gb2, "pair")
    attended, query_grad = call(
        join_kernel, where, (out_keep, out_recv), [((BLOCK, PAIR), BF16), ((BLOCK, PAIR), F32)]
    )
    attended, query_grad, grad_own = lax.optimization_barrier((attended, query_grad, grad_own))
    fine_same, fine_cross, half_same, half_cross, own_keep, own_send = call(
        fold_kernel,
        where,
        (grad_below, grad_above, grad_own, back_s3, back_z3, back_c2, back_b2),
        [((BLOCK, PAIR), BF16)] * 2
        + [((BLOCK // 2, PAIR), BF16)] * 2
        + [((BLOCK, PAIR), F32)] * 2,
    )
    fine_same = give(fine_same, "fine_same")
    fine_cross = give(swap(fine_cross), "fine_same")
    half_same = give(half_same, "half_same")
    half_cross = give(swap(half_cross), "half_same")
    own_recv = swap(own_send)
    key_grad, value_grad = call(
        final_kernel,
        where,
        (own_keep, own_recv, fine_same, fine_cross, half_same, half_cross),
        [((BLOCK, PAIR), F32)] * 2,
    )
    return attended, query_grad, key_grad, value_grad


def solution(mesh):
    spec = P(AXES, None)
    return jax.shard_map(
        on_device, mesh=mesh, in_specs=(spec,) * 4, out_specs=(spec,) * 4, check_vma=False
    )
```

```python
import math

import jax
import jax.numpy as jnp
from jax import lax
from jax.experimental import pallas as pl
from jax.experimental.pallas import tpu as pltpu
from jax.sharding import PartitionSpec as P

HEADS = 8
HEAD = 128
LEVELS = 3
BLOCK = 128
HALF = 512
PAIR = 1024
ROW = 8
AXES = ("outer", "seq")
NEGATIVE = -1e30
FACTOR = 1.0 / math.sqrt(HEAD)
FACTOR2 = FACTOR / math.log(2.0)
BF16 = jnp.bfloat16
F32 = jnp.float32


def dot(a, b, dims=((1,), (0,))):
    return lax.dot_general(a, b, (dims, ((), ())), preferred_element_type=F32)


def pool_matrix(rows, columns, span):
    i = lax.broadcasted_iota(jnp.int32, (rows, columns), 0)
    j = lax.broadcasted_iota(jnp.int32, (rows, columns), 1)
    return jnp.where(j // span == i, 1.0 / span, 0.0).astype(BF16)


def spread_matrix(rows, columns, span):
    i = lax.broadcasted_iota(jnp.int32, (rows, columns), 0)
    j = lax.broadcasted_iota(jnp.int32, (rows, columns), 1)
    return jnp.where(i // span == j, 1.0 / span, 0.0).astype(BF16)


def half_columns(core):
    return pl.ds(pl.multiple_of(core * HALF, HALF), HALF)


def block_at(core):
    return pl.ds(pl.multiple_of(core * BLOCK, BLOCK), BLOCK)


def open_kernel(where, k, v, fine, coarse):
    core = where[0] % 2
    halve = pool_matrix(64, BLOCK, 2)
    for n, half in enumerate((core, 1 - core)):
        columns = half_columns(half)
        fine[128 * n : 128 * n + 128, 0:512] = k[:, columns]
        fine[128 * n : 128 * n + 128, 512:1024] = v[:, columns]
        coarse[64 * n : 64 * n + 64] = dot(halve, fine[128 * n : 128 * n + 128]).astype(BF16)


def sides(first, own, recv, fine_same, fine_cross, half_same, half_cross):
    def pick(a, b):
        return jnp.where(first, a, b)

    own, recv = own[0:128], recv[128:256]
    fine_same, fine_cross = fine_same[0:128], fine_cross[128:256]
    half_same, half_cross = half_same[0:64], half_cross[64:128]
    return (
        pick(own, recv),
        pick(recv, own),
        pick(fine_cross, fine_same),
        pick(fine_same, fine_cross),
        pick(half_same, half_cross),
        pick(half_cross, half_same),
    )


def coarse_kernel(
    where, own, recv, fine_same, fine_cross, half_same, half_cross, same2, cross2, other2, quad3
):
    even = (where[0] // 2) % 2 == 0
    first = where[0] % 2 == 0
    low, high, fine_below, fine_above, half_below, half_above = sides(
        first, own, recv, fine_same, fine_cross, half_same, half_cross
    )
    fine = jnp.concatenate([pool_matrix(32, BLOCK, 4), pool_matrix(16, BLOCK, 8)], axis=0)
    half = jnp.concatenate([pool_matrix(32, 64, 2), pool_matrix(16, 64, 4)], axis=0)
    own_low = dot(fine[32:48], low).astype(BF16)
    own_high = dot(fine[32:48], high).astype(BF16)
    below_low = dot(half, half_below).astype(BF16)
    below_high = dot(fine, fine_below).astype(BF16)
    above_low = dot(fine, fine_above).astype(BF16)
    above_high = dot(half, half_above).astype(BF16)
    b2 = jnp.concatenate([below_low[0:32], below_high[0:32]], axis=0)
    a2 = jnp.concatenate([above_low[0:32], above_high[0:32]], axis=0)
    same2[...] = jnp.where(first, b2, a2)
    cross2[...] = jnp.where(first, a2, b2)
    other2[...] = jnp.where(even, a2, b2)
    own3 = jnp.concatenate([own_low, own_high], axis=0)
    b3 = jnp.concatenate([below_low[32:48], below_high[32:48]], axis=0)
    a3 = jnp.concatenate([above_low[32:48], above_high[32:48]], axis=0)
    quad3[0:32] = jnp.where(even, own3, b3)
    quad3[32:64] = jnp.where(even, a3, own3)


def attend_kernel(
    where, q, g, recv_q, recv_g, own_kv, recv_kv, fine_same, fine_cross, half_same, half_cross,
    m2, p2, s2, z3, x3, s3,
    out_keep, out_send, grad_own, grad_below, grad_above,
    gm2, gp2, gs2, gz3, gx3, gs3,
    queries, grads, keyvals, spread, outs,
):
    chips = where[1] // 2
    core = where[0] % 2
    chip = where[0] // 2
    quad = chip // 2
    mine = half_columns(core)
    queries[block_at(core), :] = q[:, mine]
    queries[block_at(1 - core), :] = recv_q[:, mine]
    grads[block_at(core), :] = g[:, mine]
    grads[block_at(1 - core), :] = recv_g[:, mine]
    low, high, fine_below, fine_above, half_below, half_above = sides(
        core == 0, own_kv, recv_kv, fine_same, fine_cross, half_same, half_cross
    )
    keyvals[0:128] = low
    keyvals[128:256] = high
    keyvals[256:320] = half_below
    keyvals[320:384] = half_above
    for n, piece in enumerate((m2, p2, s2, z3, x3, s3)):
        keyvals[384 + 64 * n : 448 + 64 * n] = piece[...]
    halve = pool_matrix(64, BLOCK, 2)
    keyvals[768:896] = fine_below
    keyvals[896:960] = dot(halve, fine_above).astype(BF16)
    keyvals[960:1088] = fine_above
    keyvals[1088:1152] = dot(halve, fine_below).astype(BF16)
    spread[...] = spread_matrix(BLOCK, 64, 2)

    def bias(valid, level):
        return jnp.where(valid, F32(level), F32(NEGATIVE))

    has_below = chip >= 1
    has_above = chip < chips - 1
    far2 = jnp.where(chip % 2 == 0, chip + 3, chip - 3)
    far3 = jnp.where(quad % 2 == 0, quad + 3, quad - 3)
    quads = chips // 2
    pieces = (
        (0, 256, F32(0.0)),
        (256, 64, bias(has_below, 1)),
        (320, 64, bias(has_above, 1)),
        (384, 64, bias(jnp.where(core == 0, chip >= 2, chip + 2 < chips), 2)),
        (448, 64, bias(jnp.where(core == 0, chip + 2 < chips, chip >= 2), 2)),
        (512, 64, bias((far2 >= 0) & (far2 < chips), 2)),
        (576, 64, F32(3)),
        (640, 64, bias(jnp.where(chip % ROW < ROW // 2, chip >= ROW, chip + ROW < chips), 3)),
        (704, 64, bias((far3 >= 0) & (far3 < quads), 3)),
    )
    side = lax.broadcasted_iota(jnp.int32, (1, 256), 1) < 128
    fine_bias = jnp.where(side, bias(has_below, 0), bias(has_above, 0))
    half_bias = jnp.where(side, bias(has_above, 1), bias(has_below, 1))
    rows_bias = jnp.concatenate(
        [jnp.full((rows, 1), value, F32) for _, rows, value in pieces], axis=0
    )
    nt = ((1,), (1,))
    tn = ((0,), (0,))
    for h in range(4):
        kc = slice(h * HEAD, (h + 1) * HEAD)
        vc = slice(HALF + h * HEAD, HALF + (h + 1) * HEAD)
        qh = queries[:, kc]
        gh = grads[:, kc]
        keys = keyvals[0:768, kc]
        values = keyvals[0:768, vc]
        keys_a = keyvals[768:960, kc]
        keys_b = keyvals[960:1152, kc]
        values_a = keyvals[768:960, vc]
        values_b = keyvals[960:1152, vc]
        extra = jnp.concatenate([dot(keys_a, qh[0:128], nt), dot(keys_b, qh[128:256], nt)], axis=1)
        scores = jnp.concatenate(
            [
                dot(keys, qh, nt) * FACTOR2 + rows_bias,
                extra[0:128] * FACTOR2 + fine_bias,
                extra[128:192] * FACTOR2 + half_bias,
            ],
            axis=0,
        )
        weights = jnp.exp2(scores - jnp.max(scores, axis=0, keepdims=True))
        probs = weights * (1.0 / jnp.sum(weights, axis=0, keepdims=True))
        low = probs.astype(BF16)
        dprob = jnp.concatenate(
            [
                dot(values, gh, nt),
                jnp.concatenate(
                    [dot(values_a, gh[0:128], nt), dot(values_b, gh[128:256], nt)], axis=1
                ),
            ],
            axis=0,
        )

        def back(weight, shared, part_a, part_b):
            whole = dot(shared, weight[0:768], tn)
            edges = jnp.concatenate(
                [dot(part_a, weight[768:960, 0:128], tn), dot(part_b, weight[768:960, 128:256], tn)],
                axis=1,
            )
            return whole + edges

        attended = back(low, values, values_a, values_b)
        delta = jnp.sum(gh.astype(F32).T * attended, axis=0, keepdims=True)
        dscore = (probs * (dprob - delta)).astype(BF16)
        outs[:, kc] = attended.T
        outs[:, vc] = back(dscore, keys, keys_a, keys_b).T * FACTOR
        for columns, weight, rows, scale in ((kc, dscore, qh, FACTOR), (vc, low, gh, 1.0)):
            shared = dot(weight[0:768], rows) * scale
            part_a = dot(weight[768:960, 0:128], rows[0:128]) * scale
            part_b = dot(weight[768:960, 128:256], rows[128:256]) * scale
            grad_own[:, columns] = shared[0:256]
            terms = shared.astype(BF16)
            grad_below[0:128, columns] = (
                part_a[0:128] + dot(spread[...], part_b[128:192].astype(BF16))
            ).astype(BF16)
            grad_below[128:192, columns] = terms[256:320]
            grad_above[0:128, columns] = (
                part_b[0:128] + dot(spread[...], part_a[128:192].astype(BF16))
            ).astype(BF16)
            grad_above[128:192, columns] = terms[320:384]
            for n, piece in enumerate((gm2, gp2, gs2, gz3, gx3, gs3)):
                piece[:, columns] = terms[384 + 64 * n : 448 + 64 * n]
    out_keep[...] = outs[block_at(core), :]
    out_send[...] = outs[block_at(1 - core), :]


def fold_kernel(
    where, grad_below, grad_above, own, s3, z3, same2, cross2, other2,
    out_same, out_cross, keep, send,
):
    even = (where[0] // 2) % 2 == 0

    def weigh(matrix, use):
        return jnp.where(use, matrix, jnp.zeros_like(matrix))

    def fold(base, pieces2, rows, use, fine, half):
        def rows_of(n):
            return jnp.concatenate(
                [piece[32 * n : 32 * n + 32] for piece in (pieces2, other2)]
                + [piece[rows + 16 * n : rows + 16 * n + 16] for piece in (z3, s3)],
                axis=0,
            )

        fine_matrix = jnp.concatenate(
            [spread_matrix(128, 32, 4), weigh(spread_matrix(128, 32, 4), use)]
            + [weigh(spread_matrix(128, 16, 8), use)] * 2,
            axis=1,
        )
        half_matrix = jnp.concatenate(
            [spread_matrix(64, 32, 2), weigh(spread_matrix(64, 32, 2), use)]
            + [weigh(spread_matrix(64, 16, 4), use)] * 2,
            axis=1,
        )
        matrix = (fine_matrix, rows_of(fine)), (half_matrix, rows_of(half))
        folded = jnp.concatenate([dot(*pair) for pair in matrix], axis=0)
        return (base[...].astype(F32) + folded).astype(BF16)

    first = where[0] % 2 == 0
    from2 = jnp.where(first, same2[...], cross2[...])
    to2 = jnp.where(first, cross2[...], same2[...])
    below = fold(grad_below, from2, 0, jnp.logical_not(even), 1, 0)
    above = fold(grad_above, to2, 32, even, 0, 1)
    out_same[...] = jnp.where(first, above, below)
    out_cross[...] = jnp.where(first, below, above)

    row = pl.multiple_of((where[0] // 2) % 2 * 32, 32)
    own_z = z3[pl.ds(row, 32), :]
    own_s = s3[pl.ds(row, 32), :]
    matrix = jnp.concatenate([spread_matrix(BLOCK, 16, 8)] * 2, axis=1)
    totals = [
        own[BLOCK * n : BLOCK * (n + 1)]
        + dot(matrix, jnp.concatenate([x[16 * n : 16 * n + 16] for x in (own_z, own_s)], axis=0))
        for n in range(2)
    ]
    keep[...] = jnp.where(first, totals[0], totals[1])
    send[...] = jnp.where(first, totals[1], totals[0])


def join_kernel(where, out_keep, out_recv, attended, qg):
    core = where[0] % 2
    mine = half_columns(core)
    other = half_columns(1 - core)
    attended[:, mine] = out_keep[:, 0:512].astype(BF16)
    attended[:, other] = out_recv[:, 0:512].astype(BF16)
    qg[:, mine] = out_keep[:, 512:1024]
    qg[:, other] = out_recv[:, 512:1024]


def final_kernel(where, keep, recv, same, cross, same_recv, cross_recv, kg, vg):
    core = where[0] % 2
    matrix = spread_matrix(BLOCK, 64, 2)
    for half, own, fine, coarse in (
        (core, keep, same, cross),
        (1 - core, recv, cross_recv, same_recv),
    ):
        total = own[...] + fine[0:128].astype(F32) + dot(matrix, coarse[128:192])
        columns = half_columns(half)
        kg[:, columns] = total[:, 0:512]
        vg[:, columns] = total[:, 512:1024]


def call(kernel, where, args, outs, scratch=(), limit=32):
    return pl.pallas_call(
        kernel,
        out_shape=[jax.ShapeDtypeStruct(shape, dtype) for shape, dtype in outs],
        in_specs=[pl.BlockSpec(memory_space=pltpu.SMEM)]
        + [pl.BlockSpec(memory_space=pltpu.VMEM)] * len(args),
        out_specs=[pl.BlockSpec(memory_space=pltpu.VMEM)] * len(outs),
        scratch_shapes=list(scratch),
        compiler_params=pltpu.CompilerParams(vmem_limit_bytes=int(limit * 1024 * 1024)),
    )(where, *args)


def sources(chips):
    def opposite(p):
        turn = ROW // 2 + 1 if p % 2 == 0 else ROW // 2 - 1
        return p - p % ROW + (p + turn) % ROW

    near = {
        "fine_same": lambda p, c: (p - 1, 1) if c == 1 else (p + 1, 0),
        "half_same": lambda p, c: (p - 1, 0) if c == 0 else (p + 1, 1),
        "far2": lambda p, c: (p + 2 if p % 2 == 0 else p - 2, c),
        "z3": lambda p, c: (opposite(p), c),
        "x3": lambda p, c: (p - ROW if p % ROW < ROW // 2 else p + ROW, c),
        "s3": lambda p, c: (p + 6 if p // 2 % 2 == 0 else p - 6, c),
    }
    closing = {
        "fine_same": lambda p, c: (p, 1 - c),
        "half_same": lambda p, c: (p, 1 - c),
        "far2": lambda p, c: (p ^ 1, c),
        "x3": lambda p, c: (p - p % ROW + ROW - 1 - p % ROW, c),
        "s3": lambda p, c: (p ^ 1, c),
    }

    def source(name, p, c):
        found = near[name](p, c)
        return found if 0 <= found[0] < chips else closing[name](p, c)

    return source


def on_device(query_rows, key_rows, value_rows, out_grad):
    position = lax.axis_index(AXES)
    devices = lax.axis_size(AXES)
    chips = devices // 2
    plan = sources(chips)
    where = jnp.stack([position, jnp.int32(devices)]).astype(jnp.int32)

    def swap(x):
        return lax.ppermute(x, AXES, [(i, i ^ 1) for i in range(devices)])

    def pairs(name):
        found = []
        for chip in range(chips):
            for core in range(2):
                source, side = plan(name, chip, core)
                found.append((2 * source + side, 2 * chip + core))
        return found

    def fetch(x, name):
        return lax.ppermute(x, AXES, pairs(name))

    def give(x, name):
        return lax.ppermute(x, AXES, [(b, a) for a, b in pairs(name)])

    recv_q = swap(query_rows)
    recv_g = swap(out_grad)
    own_kv, half_kv = call(
        open_kernel,
        where,
        (key_rows, value_rows),
        [((2 * BLOCK, PAIR), BF16), ((BLOCK, PAIR), BF16)],
    )
    recv_q, recv_g, own_kv, half_kv = lax.optimization_barrier((recv_q, recv_g, own_kv, half_kv))
    fine_same = fetch(own_kv, "fine_same")
    half_same = fetch(half_kv, "half_same")
    recv_kv = swap(own_kv)
    fine_cross = swap(fine_same)
    half_cross = swap(half_same)
    near = (fine_same, fine_cross, half_same, half_cross)
    same2, cross2, other2, quad3 = call(
        coarse_kernel, where, (own_kv, recv_kv, *near), [((64, PAIR), BF16)] * 4
    )
    z3 = fetch(quad3, "z3")
    s3 = fetch(quad3, "s3")
    s2 = fetch(other2, "far2")
    same2 = fetch(same2, "half_same")
    cross2 = fetch(cross2, "fine_same")
    x3 = fetch(z3, "x3")
    result = call(
        attend_kernel,
        where,
        (query_rows, out_grad, recv_q, recv_g, own_kv, recv_kv, *near, same2, cross2, s2, z3, x3, s3),
        [
            ((BLOCK, PAIR), F32),
            ((BLOCK, PAIR), F32),
            ((2 * BLOCK, PAIR), F32),
            ((192, PAIR), BF16),
            ((192, PAIR), BF16),
        ]
        + [((64, PAIR), BF16)] * 6,
        scratch=[
            pltpu.VMEM((2 * BLOCK, HALF), BF16),
            pltpu.VMEM((2 * BLOCK, HALF), BF16),
            pltpu.VMEM((1152, PAIR), BF16),
            pltpu.VMEM((BLOCK, 64), BF16),
            pltpu.VMEM((2 * BLOCK, PAIR), F32),
        ],
    )
    out_keep, out_send, grad_own, grad_below, grad_above, gm2, gp2, gs2, gz3, gx3, gs3 = result
    out_recv = swap(out_send)
    back_s3 = give(gs3, "s3")
    gz3, out_recv, gs2, gp2 = lax.optimization_barrier(
        (gz3 + give(gx3, "x3"), out_recv, gs2, gp2)
    )
    back_z3 = give(gz3, "z3")
    back_s2 = give(gs2, "far2")
    back_m2 = give(gm2, "half_same")
    back_p2 = give(gp2, "fine_same")
    attended, query_grad = call(
        join_kernel, where, (out_keep, out_recv), [((BLOCK, PAIR), BF16), ((BLOCK, PAIR), F32)]
    )
    attended, query_grad, grad_own = lax.optimization_barrier((attended, query_grad, grad_own))
    same, cross, own_keep, own_send = call(
        fold_kernel,
        where,
        (grad_below, grad_above, grad_own, back_s3, back_z3, back_m2, back_p2, back_s2),
        [((192, PAIR), BF16)] * 2 + [((BLOCK, PAIR), F32)] * 2,
    )
    same = give(same, "fine_same")
    cross = give(cross, "half_same")
    own_recv = swap(own_send)
    key_grad, value_grad = call(
        final_kernel,
        where,
        (own_keep, own_recv, same, cross, swap(same), swap(cross)),
        [((BLOCK, PAIR), F32)] * 2,
    )
    return attended, query_grad, key_grad, value_grad


def solution(mesh):
    spec = P(AXES, None)
    return jax.shard_map(
        on_device, mesh=mesh, in_specs=(spec,) * 4, out_specs=(spec,) * 4, check_vma=False
    )
```

```python
import math

import jax
import jax.numpy as jnp
from jax import lax
from jax.experimental import pallas as pl
from jax.experimental.pallas import tpu as pltpu
from jax.sharding import PartitionSpec as P

HEADS = 8
HEAD = 128
LEVELS = 3
BLOCK = 128
HALF = 512
PAIR = 1024
ROW = 8
AXES = ("outer", "seq")
NEGATIVE = -1e30
FACTOR = 1.0 / math.sqrt(HEAD)
FACTOR2 = FACTOR / math.log(2.0)
BF16 = jnp.bfloat16
F32 = jnp.float32


def dot(a, b, dims=((1,), (0,))):
    return lax.dot_general(a, b, (dims, ((), ())), preferred_element_type=F32)


def pool_matrix(rows, columns, span):
    i = lax.broadcasted_iota(jnp.int32, (rows, columns), 0)
    j = lax.broadcasted_iota(jnp.int32, (rows, columns), 1)
    return jnp.where(j // span == i, 1.0 / span, 0.0).astype(BF16)


def spread_matrix(rows, columns, span):
    i = lax.broadcasted_iota(jnp.int32, (rows, columns), 0)
    j = lax.broadcasted_iota(jnp.int32, (rows, columns), 1)
    return jnp.where(i // span == j, 1.0 / span, 0.0).astype(BF16)


def half_columns(core):
    return pl.ds(pl.multiple_of(core * HALF, HALF), HALF)


def block_at(core):
    return pl.ds(pl.multiple_of(core * BLOCK, BLOCK), BLOCK)


def open_kernel(where, k, v, own, other, half_own, half_other):
    core = where[0] % 2
    halve = pool_matrix(64, BLOCK, 2)
    for half, fine, coarse in ((1 - core, other, half_other), (core, own, half_own)):
        columns = half_columns(half)
        fine[:, 0:512] = k[:, columns]
        fine[:, 512:1024] = v[:, columns]
        coarse[...] = dot(halve, fine[...]).astype(BF16)


def sides(first, own, recv, fine_same, fine_cross, half_same, half_cross):
    def pick(a, b):
        return jnp.where(first, a[...], b[...])

    return (
        pick(own, recv),
        pick(recv, own),
        pick(fine_cross, fine_same),
        pick(fine_same, fine_cross),
        pick(half_same, half_cross),
        pick(half_cross, half_same),
    )


def coarse_kernel(
    where, own, recv, fine_same, fine_cross, half_same, half_cross, same2, cross2, other2, quad3
):
    even = (where[0] // 2) % 2 == 0
    first = where[0] % 2 == 0
    low, high, fine_below, fine_above, half_below, half_above = sides(
        first, own, recv, fine_same, fine_cross, half_same, half_cross
    )
    fine = jnp.concatenate([pool_matrix(32, BLOCK, 4), pool_matrix(16, BLOCK, 8)], axis=0)
    half = jnp.concatenate([pool_matrix(32, 64, 2), pool_matrix(16, 64, 4)], axis=0)
    own_low = dot(fine[32:48], low).astype(BF16)
    own_high = dot(fine[32:48], high).astype(BF16)
    below_low = dot(half, half_below).astype(BF16)
    below_high = dot(fine, fine_below).astype(BF16)
    above_low = dot(fine, fine_above).astype(BF16)
    above_high = dot(half, half_above).astype(BF16)
    b2 = jnp.concatenate([below_low[0:32], below_high[0:32]], axis=0)
    a2 = jnp.concatenate([above_low[0:32], above_high[0:32]], axis=0)
    same2[...] = jnp.where(first, b2, a2)
    cross2[...] = jnp.where(first, a2, b2)
    other2[...] = jnp.where(even, a2, b2)
    own3 = jnp.concatenate([own_low, own_high], axis=0)
    b3 = jnp.concatenate([below_low[32:48], below_high[32:48]], axis=0)
    a3 = jnp.concatenate([above_low[32:48], above_high[32:48]], axis=0)
    quad3[0:32] = jnp.where(even, own3, b3)
    quad3[32:64] = jnp.where(even, a3, own3)


NEAR = 576
FAR = 384
NT = ((1,), (1,))
TN = ((0,), (0,))


def bias(valid, level):
    return jnp.where(valid, F32(level), F32(NEGATIVE))


def row_bias(pieces):
    return jnp.concatenate([jnp.full((rows, 1), value, F32) for rows, value in pieces], axis=0)


def columns_of(h):
    return (
        slice(h * HEAD, (h + 1) * HEAD),
        slice(HALF + h * HEAD, HALF + (h + 1) * HEAD),
    )


def near_kernel(
    where, q, g, recv_q, recv_g, own_kv, recv_kv, fine_same, fine_cross, half_same, half_cross,
    queries, grads, keyvals, weights, dprobs, stats,
):
    chips = where[1] // 2
    core = where[0] % 2
    chip = where[0] // 2
    mine = half_columns(core)
    queries[block_at(core), :] = q[:, mine]
    queries[block_at(1 - core), :] = recv_q[:, mine]
    grads[block_at(core), :] = g[:, mine]
    grads[block_at(1 - core), :] = recv_g[:, mine]
    low, high, fine_below, fine_above, half_below, half_above = sides(
        core == 0, own_kv, recv_kv, fine_same, fine_cross, half_same, half_cross
    )
    halve = pool_matrix(64, BLOCK, 2)
    keyvals[0:128] = low
    keyvals[128:256] = high
    keyvals[256:320] = half_below
    keyvals[320:384] = half_above
    keyvals[384:512] = fine_below
    keyvals[512:576] = dot(halve, fine_above).astype(BF16)
    keyvals[576:704] = fine_above
    keyvals[704:768] = dot(halve, fine_below).astype(BF16)
    has_below = chip >= 1
    has_above = chip < chips - 1
    side = lax.broadcasted_iota(jnp.int32, (1, 256), 1) < 128
    fine_bias = jnp.where(side, bias(has_below, 0), bias(has_above, 0))
    half_bias = jnp.where(side, bias(has_above, 1), bias(has_below, 1))
    rows_bias = row_bias(((256, F32(0.0)), (64, bias(has_below, 1)), (64, bias(has_above, 1))))

    def product(columns, rows):
        shared = dot(keyvals[0:384, columns], rows, NT)
        edges = jnp.concatenate(
            [
                dot(keyvals[384:576, columns], rows[0:128], NT),
                dot(keyvals[576:768, columns], rows[128:256], NT),
            ],
            axis=1,
        )
        return shared, edges

    for h in range(4):
        kc, vc = columns_of(h)
        at = NEAR * h
        shared, edges = product(kc, queries[:, kc])
        scores = jnp.concatenate(
            [
                shared * FACTOR2 + rows_bias,
                edges[0:128] * FACTOR2 + fine_bias,
                edges[128:192] * FACTOR2 + half_bias,
            ],
            axis=0,
        )
        highest = jnp.max(scores, axis=0, keepdims=True)
        weight = jnp.exp2(scores - highest)
        weights[at : at + NEAR] = weight
        stats[h : h + 1] = highest
        stats[4 + h : 5 + h] = jnp.sum(weight, axis=0, keepdims=True)
        shared, edges = product(vc, grads[:, kc])
        dprobs[at : at + 384] = shared
        dprobs[at + 384 : at + NEAR] = edges


def back(weight, near, columns):
    edges = jnp.concatenate(
        [
            dot(near[384:576, columns], weight[384:576, 0:128], TN),
            dot(near[576:768, columns], weight[384:576, 128:256], TN),
        ],
        axis=1,
    )
    return dot(near[0:384, columns], weight[0:384], TN) + edges


def main_kernel(
    where, queries, grads, near, weights, dprobs, stats, m2, p2, s2, z3, x3, s3,
    output, low_near, dscores, gm2, gp2, gs2, gz3, gx3, gs3,
    far,
):
    chips = where[1] // 2
    core = where[0] % 2
    chip = where[0] // 2
    quad = chip // 2
    for n, piece in enumerate((m2, p2, s2, z3, x3, s3)):
        far[64 * n : 64 * n + 64] = piece[...]
    far2 = jnp.where(chip % 2 == 0, chip + 3, chip - 3)
    far3 = jnp.where(quad % 2 == 0, quad + 3, quad - 3)
    quads = chips // 2
    rows_bias = row_bias(
        (
            (64, bias(jnp.where(core == 0, chip >= 2, chip + 2 < chips), 2)),
            (64, bias(jnp.where(core == 0, chip + 2 < chips, chip >= 2), 2)),
            (64, bias((far2 >= 0) & (far2 < chips), 2)),
            (64, F32(3)),
            (64, bias(jnp.where(chip % ROW < ROW // 2, chip >= ROW, chip + ROW < chips), 3)),
            (64, bias((far3 >= 0) & (far3 < quads), 3)),
        )
    )
    for h in range(4):
        kc, vc = columns_of(h)
        at = NEAR * h
        qh = queries[:, kc]
        gh = grads[:, kc]
        scores = dot(far[:, kc], qh, NT) * FACTOR2 + rows_bias
        before = stats[h : h + 1]
        highest = jnp.maximum(before, jnp.max(scores, axis=0, keepdims=True))
        weight = jnp.exp2(scores - highest)
        shrink = jnp.exp2(before - highest)
        total = stats[4 + h : 5 + h] * shrink + jnp.sum(weight, axis=0, keepdims=True)
        inverse = 1.0 / total
        probs_far = weight * inverse
        low_far = probs_far.astype(BF16)
        probs_near = weights[at : at + NEAR] * (shrink * inverse)
        low = probs_near.astype(BF16)
        low_near[at : at + NEAR] = low
        attended = back(low, near, vc) + dot(far[:, vc], low_far, TN)
        delta = jnp.sum(gh.astype(F32).T * attended, axis=0, keepdims=True)
        output[:, kc] = attended.T
        dscore_far = (probs_far * (dot(far[:, vc], gh, NT) - delta)).astype(BF16)
        base = (NEAR + FAR) * h
        dscores[base : base + NEAR] = (
            probs_near * (dprobs[at : at + NEAR] - delta)
        ).astype(BF16)
        dscores[base + NEAR : base + NEAR + FAR] = dscore_far
        terms_k = (dot(dscore_far, qh) * FACTOR).astype(BF16)
        terms_v = dot(low_far, gh).astype(BF16)
        for n, piece in enumerate((gm2, gp2, gs2, gz3, gx3, gs3)):
            piece[:, kc] = terms_k[64 * n : 64 * n + 64]
            piece[:, vc] = terms_v[64 * n : 64 * n + 64]


def rest_kernel(
    where, queries, grads, near, low_near, dscores, output, m2, p2, s2, z3, x3, s3,
    out_keep, out_send, grad_own, grad_below, grad_above,
    outs,
):
    core = where[0] % 2
    spread = spread_matrix(BLOCK, 64, 2)
    for h in range(4):
        kc, vc = columns_of(h)
        base = (NEAR + FAR) * h
        dscore = dscores[base : base + NEAR]
        far = jnp.concatenate([piece[:, kc] for piece in (m2, p2, s2, z3, x3, s3)], axis=0)
        query_grad = back(dscore, near, kc) + dot(
            far, dscores[base + NEAR : base + NEAR + FAR], TN
        )
        outs[:, kc] = output[:, kc]
        outs[:, vc] = query_grad.T * FACTOR
        low = low_near[NEAR * h : NEAR * h + NEAR]
        for columns, weight, rows, scale in (
            (kc, dscore, queries[:, kc], FACTOR),
            (vc, low, grads[:, kc], 1.0),
        ):
            shared = dot(weight[0:384], rows) * scale
            part_a = dot(weight[384:576, 0:128], rows[0:128]) * scale
            part_b = dot(weight[384:576, 128:256], rows[128:256]) * scale
            grad_own[:, columns] = shared[0:256]
            terms = shared[256:384].astype(BF16)
            grad_below[0:128, columns] = (
                part_a[0:128] + dot(spread, part_b[128:192].astype(BF16))
            ).astype(BF16)
            grad_below[128:192, columns] = terms[0:64]
            grad_above[0:128, columns] = (
                part_b[0:128] + dot(spread, part_a[128:192].astype(BF16))
            ).astype(BF16)
            grad_above[128:192, columns] = terms[64:128]
    out_keep[...] = outs[block_at(core), :]
    out_send[...] = outs[block_at(1 - core), :]


def fold_kernel(
    where, grad_below, grad_above, own, s3, z3, same2, cross2, other2,
    out_same, out_cross, half_same, half_cross, keep, send,
):
    even = (where[0] // 2) % 2 == 0

    def weigh(matrix, use):
        return jnp.where(use, matrix, jnp.zeros_like(matrix))

    def fold(base, pieces2, rows, use, fine, half):
        def rows_of(n):
            return jnp.concatenate(
                [piece[32 * n : 32 * n + 32] for piece in (pieces2, other2)]
                + [piece[rows + 16 * n : rows + 16 * n + 16] for piece in (z3, s3)],
                axis=0,
            )

        fine_matrix = jnp.concatenate(
            [spread_matrix(128, 32, 4), weigh(spread_matrix(128, 32, 4), use)]
            + [weigh(spread_matrix(128, 16, 8), use)] * 2,
            axis=1,
        )
        half_matrix = jnp.concatenate(
            [spread_matrix(64, 32, 2), weigh(spread_matrix(64, 32, 2), use)]
            + [weigh(spread_matrix(64, 16, 4), use)] * 2,
            axis=1,
        )
        return (
            (base[0:128].astype(F32) + dot(fine_matrix, rows_of(fine))).astype(BF16),
            (base[128:192].astype(F32) + dot(half_matrix, rows_of(half))).astype(BF16),
        )

    first = where[0] % 2 == 0
    from2 = jnp.where(first, same2[...], cross2[...])
    to2 = jnp.where(first, cross2[...], same2[...])
    fine_below, half_below = fold(grad_below, from2, 0, jnp.logical_not(even), 1, 0)
    fine_above, half_above = fold(grad_above, to2, 32, even, 0, 1)
    out_same[...] = jnp.where(first, fine_above, fine_below)
    out_cross[...] = jnp.where(first, fine_below, fine_above)
    half_same[...] = jnp.where(first, half_below, half_above)
    half_cross[...] = jnp.where(first, half_above, half_below)

    row = pl.multiple_of((where[0] // 2) % 2 * 32, 32)
    own_z = z3[pl.ds(row, 32), :]
    own_s = s3[pl.ds(row, 32), :]
    matrix = jnp.concatenate([spread_matrix(BLOCK, 16, 8)] * 2, axis=1)
    totals = [
        own[BLOCK * n : BLOCK * (n + 1)]
        + dot(matrix, jnp.concatenate([x[16 * n : 16 * n + 16] for x in (own_z, own_s)], axis=0))
        for n in range(2)
    ]
    keep[...] = jnp.where(first, totals[0], totals[1])
    send[...] = jnp.where(first, totals[1], totals[0])


def join_kernel(where, out_keep, out_recv, attended, qg):
    core = where[0] % 2
    mine = half_columns(core)
    other = half_columns(1 - core)
    attended[:, mine] = out_keep[:, 0:512].astype(BF16)
    attended[:, other] = out_recv[:, 0:512].astype(BF16)
    qg[:, mine] = out_keep[:, 512:1024]
    qg[:, other] = out_recv[:, 512:1024]


def final_kernel(
    where, keep, recv, fine_same, fine_cross, half_same, half_cross, kg, vg
):
    core = where[0] % 2
    matrix = spread_matrix(BLOCK, 64, 2)
    for half, own, fine, coarse in (
        (core, keep, fine_same, half_same),
        (1 - core, recv, fine_cross, half_cross),
    ):
        total = own[...] + fine[...].astype(F32) + dot(matrix, coarse[...])
        columns = half_columns(half)
        kg[:, columns] = total[:, 0:512]
        vg[:, columns] = total[:, 512:1024]


def call(kernel, where, args, outs, scratch=(), limit=32):
    return pl.pallas_call(
        kernel,
        out_shape=[jax.ShapeDtypeStruct(shape, dtype) for shape, dtype in outs],
        in_specs=[pl.BlockSpec(memory_space=pltpu.SMEM)]
        + [pl.BlockSpec(memory_space=pltpu.VMEM)] * len(args),
        out_specs=[pl.BlockSpec(memory_space=pltpu.VMEM)] * len(outs),
        scratch_shapes=list(scratch),
        compiler_params=pltpu.CompilerParams(vmem_limit_bytes=int(limit * 1024 * 1024)),
    )(where, *args)


def sources(chips):
    def opposite(p):
        turn = ROW // 2 + 1 if p % 2 == 0 else ROW // 2 - 1
        return p - p % ROW + (p + turn) % ROW

    near = {
        "fine_same": lambda p, c: (p - 1, 1) if c == 1 else (p + 1, 0),
        "half_same": lambda p, c: (p - 1, 0) if c == 0 else (p + 1, 1),
        "far2": lambda p, c: (p + 2 if p % 2 == 0 else p - 2, c),
        "z3": lambda p, c: (opposite(p), c),
        "x3": lambda p, c: (p - ROW if p % ROW < ROW // 2 else p + ROW, c),
        "s3": lambda p, c: (p + 6 if p // 2 % 2 == 0 else p - 6, c),
    }
    closing = {
        "fine_same": lambda p, c: (p, 1 - c),
        "half_same": lambda p, c: (p, 1 - c),
        "far2": lambda p, c: (p ^ 1, c),
        "x3": lambda p, c: (p - p % ROW + ROW - 1 - p % ROW, c),
        "s3": lambda p, c: (p ^ 1, c),
    }

    def source(name, p, c):
        found = near[name](p, c)
        return found if 0 <= found[0] < chips else closing[name](p, c)

    return source


def on_device(query_rows, key_rows, value_rows, out_grad):
    position = lax.axis_index(AXES)
    devices = lax.axis_size(AXES)
    chips = devices // 2
    plan = sources(chips)
    where = jnp.stack([position, jnp.int32(devices)]).astype(jnp.int32)

    def swap(x):
        return lax.ppermute(x, AXES, [(i, i ^ 1) for i in range(devices)])

    def pairs(name):
        found = []
        for chip in range(chips):
            for core in range(2):
                source, side = plan(name, chip, core)
                found.append((2 * source + side, 2 * chip + core))
        return found

    def fetch(x, name):
        return lax.ppermute(x, AXES, pairs(name))

    def give(x, name):
        return lax.ppermute(x, AXES, [(b, a) for a, b in pairs(name)])

    recv_q = swap(query_rows)
    recv_g = swap(out_grad)
    own_kv, other_kv, half_own, half_other = call(
        open_kernel,
        where,
        (key_rows, value_rows),
        [((BLOCK, PAIR), BF16)] * 2 + [((BLOCK // 2, PAIR), BF16)] * 2,
    )
    recv_q, recv_g, own_kv, other_kv, half_own, half_other = lax.optimization_barrier(
        (recv_q, recv_g, own_kv, other_kv, half_own, half_other)
    )
    fine_cross = swap(fetch(other_kv, "fine_same"))
    half_cross = swap(fetch(half_other, "half_same"))
    fine_same = fetch(own_kv, "fine_same")
    half_same = fetch(half_own, "half_same")
    recv_kv = swap(other_kv)
    near = (fine_same, fine_cross, half_same, half_cross)
    same2, cross2, other2, quad3 = call(
        coarse_kernel, where, (own_kv, recv_kv, *near), [((64, PAIR), BF16)] * 4
    )
    z3 = fetch(quad3, "z3")
    s3 = fetch(quad3, "s3")
    s2 = fetch(other2, "far2")
    same2 = fetch(same2, "half_same")
    cross2 = fetch(cross2, "fine_same")
    x3 = fetch(z3, "x3")
    queries, grads, near_kv, weights, dprobs, stats = call(
        near_kernel,
        where,
        (query_rows, out_grad, recv_q, recv_g, own_kv, recv_kv, *near),
        [
            ((2 * BLOCK, HALF), BF16),
            ((2 * BLOCK, HALF), BF16),
            ((768, PAIR), BF16),
            ((4 * NEAR, 2 * BLOCK), F32),
            ((4 * NEAR, 2 * BLOCK), F32),
            ((8, 2 * BLOCK), F32),
        ],
    )
    far = (same2, cross2, s2, z3, x3, s3)
    output, low_near, dscores, gm2, gp2, gs2, gz3, gx3, gs3 = call(
        main_kernel,
        where,
        (queries, grads, near_kv, weights, dprobs, stats, *far),
        [
            ((2 * BLOCK, HALF), F32),
            ((4 * NEAR, 2 * BLOCK), BF16),
            ((4 * (NEAR + FAR), 2 * BLOCK), BF16),
        ]
        + [((64, PAIR), BF16)] * 6,
        scratch=[pltpu.VMEM((FAR, PAIR), BF16)],
    )
    back_s3 = give(gs3, "s3")
    gz3, gs2, gp2, dscores = lax.optimization_barrier(
        (gz3 + give(gx3, "x3"), gs2, gp2, dscores)
    )
    back_z3 = give(gz3, "z3")
    back_s2 = give(gs2, "far2")
    back_m2 = give(gm2, "half_same")
    back_p2 = give(gp2, "fine_same")
    out_keep, out_send, grad_own, grad_below, grad_above = call(
        rest_kernel,
        where,
        (queries, grads, near_kv, low_near, dscores, output, *far),
        [
            ((BLOCK, PAIR), F32),
            ((BLOCK, PAIR), F32),
            ((2 * BLOCK, PAIR), F32),
            ((192, PAIR), BF16),
            ((192, PAIR), BF16),
        ],
        scratch=[pltpu.VMEM((2 * BLOCK, PAIR), F32)],
    )
    out_recv = swap(out_send)
    fine_same, fine_cross, half_same, half_cross, own_keep, own_send = call(
        fold_kernel,
        where,
        (grad_below, grad_above, grad_own, back_s3, back_z3, back_m2, back_p2, back_s2),
        [((BLOCK, PAIR), BF16)] * 2
        + [((BLOCK // 2, PAIR), BF16)] * 2
        + [((BLOCK, PAIR), F32)] * 2,
    )
    fine_same = give(fine_same, "fine_same")
    fine_cross = give(swap(fine_cross), "fine_same")
    half_same = give(half_same, "half_same")
    half_cross = give(swap(half_cross), "half_same")
    own_recv = swap(own_send)
    attended, query_grad = call(
        join_kernel, where, (out_keep, out_recv), [((BLOCK, PAIR), BF16), ((BLOCK, PAIR), F32)]
    )
    attended, query_grad, own_keep = lax.optimization_barrier((attended, query_grad, own_keep))
    key_grad, value_grad = call(
        final_kernel,
        where,
        (own_keep, own_recv, fine_same, fine_cross, half_same, half_cross),
        [((BLOCK, PAIR), F32)] * 2,
    )
    return attended, query_grad, key_grad, value_grad


def solution(mesh):
    spec = P(AXES, None)
    return jax.shard_map(
        on_device, mesh=mesh, in_specs=(spec,) * 4, out_specs=(spec,) * 4, check_vma=False
    )
```

```python
import math

import jax
import jax.numpy as jnp
from jax import lax
from jax.experimental import pallas as pl
from jax.experimental.pallas import tpu as pltpu
from jax.sharding import PartitionSpec as P

HEADS = 8
HEAD = 128
LEVELS = 3
BLOCK = 128
HALF = 512
PAIR = 1024
ROW = 8
AXES = ("outer", "seq")
NEGATIVE = -1e30
FACTOR = 1.0 / math.sqrt(HEAD)
FACTOR2 = FACTOR / math.log(2.0)
BF16 = jnp.bfloat16
F32 = jnp.float32


def dot(a, b, dims=((1,), (0,))):
    return lax.dot_general(a, b, (dims, ((), ())), preferred_element_type=F32)


def pool_matrix(rows, columns, span):
    i = lax.broadcasted_iota(jnp.int32, (rows, columns), 0)
    j = lax.broadcasted_iota(jnp.int32, (rows, columns), 1)
    return jnp.where(j // span == i, 1.0 / span, 0.0).astype(BF16)


def spread_matrix(rows, columns, span):
    i = lax.broadcasted_iota(jnp.int32, (rows, columns), 0)
    j = lax.broadcasted_iota(jnp.int32, (rows, columns), 1)
    return jnp.where(i // span == j, 1.0 / span, 0.0).astype(BF16)


def half_columns(core):
    return pl.ds(pl.multiple_of(core * HALF, HALF), HALF)


def block_at(core):
    return pl.ds(pl.multiple_of(core * BLOCK, BLOCK), BLOCK)


def open_kernel(where, k, v, own, other, coarse):
    core = where[0] % 2
    halve = pool_matrix(64, BLOCK, 2)
    for n, half, fine in ((1, 1 - core, other), (0, core, own)):
        columns = half_columns(half)
        fine[:, 0:512] = k[:, columns]
        fine[:, 512:1024] = v[:, columns]
        coarse[64 * n : 64 * n + 64] = dot(halve, fine[...]).astype(BF16)


def sides(first, own, recv, fine_same, fine_cross, half_same, half_cross):
    def pick(a, b):
        return jnp.where(first, a[...], b[...])

    return (
        pick(own, recv),
        pick(recv, own),
        pick(fine_cross, fine_same),
        pick(fine_same, fine_cross),
        pick(half_same[0:64], half_cross[64:128]),
        pick(half_cross[64:128], half_same[0:64]),
    )


def coarse_kernel(
    where, own, recv, fine_same, fine_cross, half_same, half_cross, same2, cross2, other2, quad3
):
    even = (where[0] // 2) % 2 == 0
    first = where[0] % 2 == 0
    low, high, fine_below, fine_above, half_below, half_above = sides(
        first, own, recv, fine_same, fine_cross, half_same, half_cross
    )
    fine = jnp.concatenate([pool_matrix(32, BLOCK, 4), pool_matrix(16, BLOCK, 8)], axis=0)
    half = jnp.concatenate([pool_matrix(32, 64, 2), pool_matrix(16, 64, 4)], axis=0)
    own_low = dot(fine[32:48], low).astype(BF16)
    own_high = dot(fine[32:48], high).astype(BF16)
    below_low = dot(half, half_below).astype(BF16)
    below_high = dot(fine, fine_below).astype(BF16)
    above_low = dot(fine, fine_above).astype(BF16)
    above_high = dot(half, half_above).astype(BF16)
    b2 = jnp.concatenate([below_low[0:32], below_high[0:32]], axis=0)
    a2 = jnp.concatenate([above_low[0:32], above_high[0:32]], axis=0)
    same2[...] = jnp.where(first, b2, a2)
    cross2[...] = jnp.where(first, a2, b2)
    other2[...] = jnp.where(even, a2, b2)
    own3 = jnp.concatenate([own_low, own_high], axis=0)
    b3 = jnp.concatenate([below_low[32:48], below_high[32:48]], axis=0)
    a3 = jnp.concatenate([above_low[32:48], above_high[32:48]], axis=0)
    quad3[0:32] = jnp.where(even, own3, b3)
    quad3[32:64] = jnp.where(even, a3, own3)


NEAR = 576
FAR = 384
NT = ((1,), (1,))
TN = ((0,), (0,))


def bias(valid, level):
    return jnp.where(valid, F32(level), F32(NEGATIVE))


def row_bias(pieces):
    return jnp.concatenate([jnp.full((rows, 1), value, F32) for rows, value in pieces], axis=0)


def columns_of(h):
    return (
        slice(h * HEAD, (h + 1) * HEAD),
        slice(HALF + h * HEAD, HALF + (h + 1) * HEAD),
    )


def back(weight, near, columns):
    edges = jnp.concatenate(
        [
            dot(near[384:576, columns], weight[384:576, 0:128], TN),
            dot(near[576:768, columns], weight[384:576, 128:256], TN),
        ],
        axis=1,
    )
    return dot(near[0:384, columns], weight[0:384], TN) + edges


def near_kernel(
    where, q, g, recv_q, recv_g, own_kv, recv_kv, fine_same, fine_cross, half_same, half_cross,
    queries, grads, keyvals, weights, dprobs, stats, outputs,
):
    chips = where[1] // 2
    core = where[0] % 2
    chip = where[0] // 2
    mine = half_columns(core)
    queries[block_at(core), :] = q[:, mine]
    queries[block_at(1 - core), :] = recv_q[:, mine]
    grads[block_at(core), :] = g[:, mine]
    grads[block_at(1 - core), :] = recv_g[:, mine]
    low, high, fine_below, fine_above, half_below, half_above = sides(
        core == 0, own_kv, recv_kv, fine_same, fine_cross, half_same, half_cross
    )
    halve = pool_matrix(64, BLOCK, 2)
    keyvals[0:128] = low
    keyvals[128:256] = high
    keyvals[256:320] = half_below
    keyvals[320:384] = half_above
    keyvals[384:512] = fine_below
    keyvals[512:576] = dot(halve, fine_above).astype(BF16)
    keyvals[576:704] = fine_above
    keyvals[704:768] = dot(halve, fine_below).astype(BF16)
    has_below = chip >= 1
    has_above = chip < chips - 1
    side = lax.broadcasted_iota(jnp.int32, (1, 256), 1) < 128
    fine_bias = jnp.where(side, bias(has_below, 0), bias(has_above, 0))
    half_bias = jnp.where(side, bias(has_above, 1), bias(has_below, 1))
    rows_bias = row_bias(((256, F32(0.0)), (64, bias(has_below, 1)), (64, bias(has_above, 1))))

    def product(columns, rows):
        shared = dot(keyvals[0:384, columns], rows, NT)
        edges = jnp.concatenate(
            [
                dot(keyvals[384:576, columns], rows[0:128], NT),
                dot(keyvals[576:768, columns], rows[128:256], NT),
            ],
            axis=1,
        )
        return shared, edges

    for h in range(4):
        kc, vc = columns_of(h)
        at = NEAR * h
        shared, edges = product(kc, queries[:, kc])
        scores = jnp.concatenate(
            [
                shared * FACTOR2 + rows_bias,
                edges[0:128] * FACTOR2 + fine_bias,
                edges[128:192] * FACTOR2 + half_bias,
            ],
            axis=0,
        )
        highest = jnp.max(scores, axis=0, keepdims=True)
        weight = jnp.exp2(scores - highest)
        weights[at : at + NEAR] = weight
        stats[h : h + 1] = highest
        stats[4 + h : 5 + h] = jnp.sum(weight, axis=0, keepdims=True)
        outputs[HEAD * h : HEAD * h + HEAD] = back(weight.astype(BF16), keyvals, vc)
        shared, edges = product(vc, grads[:, kc])
        dprobs[at : at + 384] = shared
        dprobs[at + 384 : at + NEAR] = edges


def main_kernel(
    where, queries, grads, outputs, stats, m2, p2, s2, z3, x3, s3,
    output, scales, dscores, gm2, gp2, gs2, gz3, gx3, gs3,
    far,
):
    chips = where[1] // 2
    core = where[0] % 2
    chip = where[0] // 2
    quad = chip // 2
    for n, piece in enumerate((m2, p2, s2, z3, x3, s3)):
        far[64 * n : 64 * n + 64] = piece[...]
    far2 = jnp.where(chip % 2 == 0, chip + 3, chip - 3)
    far3 = jnp.where(quad % 2 == 0, quad + 3, quad - 3)
    quads = chips // 2
    rows_bias = row_bias(
        (
            (64, bias(jnp.where(core == 0, chip >= 2, chip + 2 < chips), 2)),
            (64, bias(jnp.where(core == 0, chip + 2 < chips, chip >= 2), 2)),
            (64, bias((far2 >= 0) & (far2 < chips), 2)),
            (64, F32(3)),
            (64, bias(jnp.where(chip % ROW < ROW // 2, chip >= ROW, chip + ROW < chips), 3)),
            (64, bias((far3 >= 0) & (far3 < quads), 3)),
        )
    )
    for h in range(4):
        kc, vc = columns_of(h)
        qh = queries[:, kc]
        gh = grads[:, kc]
        scores = dot(far[:, kc], qh, NT) * FACTOR2 + rows_bias
        before = stats[h : h + 1]
        highest = jnp.maximum(before, jnp.max(scores, axis=0, keepdims=True))
        weight = jnp.exp2(scores - highest)
        shrink = jnp.exp2(before - highest)
        total = stats[4 + h : 5 + h] * shrink + jnp.sum(weight, axis=0, keepdims=True)
        inverse = 1.0 / total
        scale = shrink * inverse
        probs_far = weight * inverse
        low_far = probs_far.astype(BF16)
        attended = outputs[HEAD * h : HEAD * h + HEAD] * scale + dot(far[:, vc], low_far, TN)
        delta = jnp.sum(gh.astype(F32).T * attended, axis=0, keepdims=True)
        output[:, kc] = attended.T
        scales[h : h + 1] = scale
        scales[4 + h : 5 + h] = delta
        dscore_far = (probs_far * (dot(far[:, vc], gh, NT) - delta)).astype(BF16)
        dscores[FAR * h : FAR * h + FAR] = dscore_far
        terms_k = (dot(dscore_far, qh) * FACTOR).astype(BF16)
        terms_v = dot(low_far, gh).astype(BF16)
        for n, piece in enumerate((gm2, gp2, gs2, gz3, gx3, gs3)):
            piece[:, kc] = terms_k[64 * n : 64 * n + 64]
            piece[:, vc] = terms_v[64 * n : 64 * n + 64]


def rest_kernel(
    where, queries, grads, near, weights, dprobs, scales, dscores, output,
    m2, p2, s2, z3, x3, s3,
    out_keep, out_send, grad_own, grad_below, grad_above,
    outs,
):
    core = where[0] % 2
    spread = spread_matrix(BLOCK, 64, 2)
    for h in range(4):
        kc, vc = columns_of(h)
        at = NEAR * h
        probs = weights[at : at + NEAR] * scales[h : h + 1]
        low = probs.astype(BF16)
        dscore = (probs * (dprobs[at : at + NEAR] - scales[4 + h : 5 + h])).astype(BF16)
        far = jnp.concatenate([piece[:, kc] for piece in (m2, p2, s2, z3, x3, s3)], axis=0)
        query_grad = back(dscore, near, kc) + dot(far, dscores[FAR * h : FAR * h + FAR], TN)
        outs[:, kc] = output[:, kc]
        outs[:, vc] = query_grad.T * FACTOR
        for columns, weight, rows, scale in (
            (kc, dscore, queries[:, kc], FACTOR),
            (vc, low, grads[:, kc], 1.0),
        ):
            shared = dot(weight[0:384], rows) * scale
            part_a = dot(weight[384:576, 0:128], rows[0:128]) * scale
            part_b = dot(weight[384:576, 128:256], rows[128:256]) * scale
            grad_own[:, columns] = shared[0:256]
            terms = shared[256:384].astype(BF16)
            grad_below[0:128, columns] = (
                part_a[0:128] + dot(spread, part_b[128:192].astype(BF16))
            ).astype(BF16)
            grad_below[128:192, columns] = terms[0:64]
            grad_above[0:128, columns] = (
                part_b[0:128] + dot(spread, part_a[128:192].astype(BF16))
            ).astype(BF16)
            grad_above[128:192, columns] = terms[64:128]
    out_keep[...] = outs[block_at(core), :]
    out_send[...] = outs[block_at(1 - core), :]


def fold_kernel(
    where, grad_below, grad_above, own, s3, z3, same2, cross2, other2,
    out_same, out_cross, half_same, half_cross, keep, send,
):
    even = (where[0] // 2) % 2 == 0

    def weigh(matrix, use):
        return jnp.where(use, matrix, jnp.zeros_like(matrix))

    def fold(base, pieces2, rows, use, fine, half):
        def rows_of(n):
            return jnp.concatenate(
                [piece[32 * n : 32 * n + 32] for piece in (pieces2, other2)]
                + [piece[rows + 16 * n : rows + 16 * n + 16] for piece in (z3, s3)],
                axis=0,
            )

        fine_matrix = jnp.concatenate(
            [spread_matrix(128, 32, 4), weigh(spread_matrix(128, 32, 4), use)]
            + [weigh(spread_matrix(128, 16, 8), use)] * 2,
            axis=1,
        )
        half_matrix = jnp.concatenate(
            [spread_matrix(64, 32, 2), weigh(spread_matrix(64, 32, 2), use)]
            + [weigh(spread_matrix(64, 16, 4), use)] * 2,
            axis=1,
        )
        return (
            (base[0:128].astype(F32) + dot(fine_matrix, rows_of(fine))).astype(BF16),
            (base[128:192].astype(F32) + dot(half_matrix, rows_of(half))).astype(BF16),
        )

    first = where[0] % 2 == 0
    from2 = jnp.where(first, same2[...], cross2[...])
    to2 = jnp.where(first, cross2[...], same2[...])
    fine_below, half_below = fold(grad_below, from2, 0, jnp.logical_not(even), 1, 0)
    fine_above, half_above = fold(grad_above, to2, 32, even, 0, 1)
    out_same[...] = jnp.where(first, fine_above, fine_below)
    out_cross[...] = jnp.where(first, fine_below, fine_above)
    half_same[...] = jnp.where(first, half_below, half_above)
    half_cross[...] = jnp.where(first, half_above, half_below)

    row = pl.multiple_of((where[0] // 2) % 2 * 32, 32)
    own_z = z3[pl.ds(row, 32), :]
    own_s = s3[pl.ds(row, 32), :]
    matrix = jnp.concatenate([spread_matrix(BLOCK, 16, 8)] * 2, axis=1)
    totals = [
        own[BLOCK * n : BLOCK * (n + 1)]
        + dot(matrix, jnp.concatenate([x[16 * n : 16 * n + 16] for x in (own_z, own_s)], axis=0))
        for n in range(2)
    ]
    keep[...] = jnp.where(first, totals[0], totals[1])
    send[...] = jnp.where(first, totals[1], totals[0])


def join_kernel(where, out_keep, out_recv, attended, qg):
    core = where[0] % 2
    mine = half_columns(core)
    other = half_columns(1 - core)
    attended[:, mine] = out_keep[:, 0:512].astype(BF16)
    attended[:, other] = out_recv[:, 0:512].astype(BF16)
    qg[:, mine] = out_keep[:, 512:1024]
    qg[:, other] = out_recv[:, 512:1024]


def final_kernel(
    where, keep, recv, fine_same, fine_cross, half_same, half_cross, kg, vg
):
    core = where[0] % 2
    matrix = spread_matrix(BLOCK, 64, 2)
    for half, own, fine, coarse in (
        (core, keep, fine_same, half_same),
        (1 - core, recv, fine_cross, half_cross),
    ):
        total = own[...] + fine[...].astype(F32) + dot(matrix, coarse[...])
        columns = half_columns(half)
        kg[:, columns] = total[:, 0:512]
        vg[:, columns] = total[:, 512:1024]


def call(kernel, where, args, outs, scratch=(), limit=32):
    return pl.pallas_call(
        kernel,
        out_shape=[jax.ShapeDtypeStruct(shape, dtype) for shape, dtype in outs],
        in_specs=[pl.BlockSpec(memory_space=pltpu.SMEM)]
        + [pl.BlockSpec(memory_space=pltpu.VMEM)] * len(args),
        out_specs=[pl.BlockSpec(memory_space=pltpu.VMEM)] * len(outs),
        scratch_shapes=list(scratch),
        compiler_params=pltpu.CompilerParams(vmem_limit_bytes=int(limit * 1024 * 1024)),
    )(where, *args)


def sources(chips):
    def opposite(p):
        turn = ROW // 2 + 1 if p % 2 == 0 else ROW // 2 - 1
        return p - p % ROW + (p + turn) % ROW

    near = {
        "fine_same": lambda p, c: (p - 1, 1) if c == 1 else (p + 1, 0),
        "half_same": lambda p, c: (p - 1, 0) if c == 0 else (p + 1, 1),
        "far2": lambda p, c: (p + 2 if p % 2 == 0 else p - 2, c),
        "z3": lambda p, c: (opposite(p), c),
        "x3": lambda p, c: (p - ROW if p % ROW < ROW // 2 else p + ROW, c),
        "s3": lambda p, c: (p + 6 if p // 2 % 2 == 0 else p - 6, c),
    }
    closing = {
        "fine_same": lambda p, c: (p, 1 - c),
        "half_same": lambda p, c: (p, 1 - c),
        "far2": lambda p, c: (p ^ 1, c),
        "x3": lambda p, c: (p - p % ROW + ROW - 1 - p % ROW, c),
        "s3": lambda p, c: (p ^ 1, c),
    }

    def source(name, p, c):
        found = near[name](p, c)
        return found if 0 <= found[0] < chips else closing[name](p, c)

    return source


def on_device(query_rows, key_rows, value_rows, out_grad):
    position = lax.axis_index(AXES)
    devices = lax.axis_size(AXES)
    chips = devices // 2
    plan = sources(chips)
    where = jnp.stack([position, jnp.int32(devices)]).astype(jnp.int32)

    def swap(x):
        return lax.ppermute(x, AXES, [(i, i ^ 1) for i in range(devices)])

    def pairs(name):
        found = []
        for chip in range(chips):
            for core in range(2):
                source, side = plan(name, chip, core)
                found.append((2 * source + side, 2 * chip + core))
        return found

    def fetch(x, name):
        return lax.ppermute(x, AXES, pairs(name))

    def give(x, name):
        return lax.ppermute(x, AXES, [(b, a) for a, b in pairs(name)])

    recv_q = swap(query_rows)
    recv_g = swap(out_grad)
    own_kv, other_kv, half_kv = call(
        open_kernel, where, (key_rows, value_rows), [((BLOCK, PAIR), BF16)] * 3
    )
    recv_q, recv_g, own_kv, other_kv, half_kv = lax.optimization_barrier(
        (recv_q, recv_g, own_kv, other_kv, half_kv)
    )
    fine_cross = swap(fetch(other_kv, "fine_same"))
    half_same = fetch(half_kv, "half_same")
    half_cross = swap(half_same)
    fine_same = fetch(own_kv, "fine_same")
    recv_kv = swap(other_kv)
    near = (fine_same, fine_cross, half_same, half_cross)
    same2, cross2, other2, quad3 = call(
        coarse_kernel, where, (own_kv, recv_kv, *near), [((64, PAIR), BF16)] * 4
    )
    z3 = fetch(quad3, "z3")
    s3 = fetch(quad3, "s3")
    s2 = fetch(other2, "far2")
    same2 = fetch(same2, "half_same")
    cross2 = fetch(cross2, "fine_same")
    x3 = fetch(z3, "x3")
    queries, grads, near_kv, weights, dprobs, stats, outputs = call(
        near_kernel,
        where,
        (query_rows, out_grad, recv_q, recv_g, own_kv, recv_kv, *near),
        [
            ((2 * BLOCK, HALF), BF16),
            ((2 * BLOCK, HALF), BF16),
            ((768, PAIR), BF16),
            ((4 * NEAR, 2 * BLOCK), F32),
            ((4 * NEAR, 2 * BLOCK), F32),
            ((8, 2 * BLOCK), F32),
            ((4 * HEAD, 2 * BLOCK), F32),
        ],
    )
    far = (same2, cross2, s2, z3, x3, s3)
    output, scales, dscores, gm2, gp2, gs2, gz3, gx3, gs3 = call(
        main_kernel,
        where,
        (queries, grads, outputs, stats, *far),
        [
            ((2 * BLOCK, HALF), F32),
            ((8, 2 * BLOCK), F32),
            ((4 * FAR, 2 * BLOCK), BF16),
        ]
        + [((64, PAIR), BF16)] * 6,
        scratch=[pltpu.VMEM((FAR, PAIR), BF16)],
    )
    back_s3 = give(gs3, "s3")
    gz3, gs2, gp2, scales = lax.optimization_barrier((gz3 + give(gx3, "x3"), gs2, gp2, scales))
    back_z3 = give(gz3, "z3")
    back_s2 = give(gs2, "far2")
    back_m2 = give(gm2, "half_same")
    back_p2 = give(gp2, "fine_same")
    out_keep, out_send, grad_own, grad_below, grad_above = call(
        rest_kernel,
        where,
        (queries, grads, near_kv, weights, dprobs, scales, dscores, output, *far),
        [
            ((BLOCK, PAIR), F32),
            ((BLOCK, PAIR), F32),
            ((2 * BLOCK, PAIR), F32),
            ((192, PAIR), BF16),
            ((192, PAIR), BF16),
        ],
        scratch=[pltpu.VMEM((2 * BLOCK, PAIR), F32)],
    )
    out_recv = swap(out_send)
    fine_same, fine_cross, half_same, half_cross, own_keep, own_send = call(
        fold_kernel,
        where,
        (grad_below, grad_above, grad_own, back_s3, back_z3, back_m2, back_p2, back_s2),
        [((BLOCK, PAIR), BF16)] * 2
        + [((BLOCK // 2, PAIR), BF16)] * 2
        + [((BLOCK, PAIR), F32)] * 2,
    )
    fine_same = give(fine_same, "fine_same")
    fine_cross = give(swap(fine_cross), "fine_same")
    half_same = give(half_same, "half_same")
    half_cross = give(swap(half_cross), "half_same")
    own_recv = swap(own_send)
    attended, query_grad = call(
        join_kernel, where, (out_keep, out_recv), [((BLOCK, PAIR), BF16), ((BLOCK, PAIR), F32)]
    )
    attended, query_grad, own_keep = lax.optimization_barrier((attended, query_grad, own_keep))
    key_grad, value_grad = call(
        final_kernel,
        where,
        (own_keep, own_recv, fine_same, fine_cross, half_same, half_cross),
        [((BLOCK, PAIR), F32)] * 2,
    )
    return attended, query_grad, key_grad, value_grad


def solution(mesh):
    spec = P(AXES, None)
    return jax.shard_map(
        on_device, mesh=mesh, in_specs=(spec,) * 4, out_specs=(spec,) * 4, check_vma=False
    )
```

```python
import math

import jax
import jax.numpy as jnp
from jax import lax
from jax.experimental import pallas as pl
from jax.experimental.pallas import tpu as pltpu
from jax.sharding import PartitionSpec as P

HEADS = 8
HEAD = 128
LEVELS = 3
BLOCK = 128
HALF = 512
PAIR = 1024
ROW = 8
AXES = ("outer", "seq")
NEGATIVE = -1e30
FACTOR = 1.0 / math.sqrt(HEAD)
FACTOR2 = FACTOR / math.log(2.0)
BF16 = jnp.bfloat16
F32 = jnp.float32


def dot(a, b, dims=((1,), (0,))):
    return lax.dot_general(a, b, (dims, ((), ())), preferred_element_type=F32)


def pool_matrix(rows, columns, span):
    i = lax.broadcasted_iota(jnp.int32, (rows, columns), 0)
    j = lax.broadcasted_iota(jnp.int32, (rows, columns), 1)
    return jnp.where(j // span == i, 1.0 / span, 0.0).astype(BF16)


def spread_matrix(rows, columns, span):
    i = lax.broadcasted_iota(jnp.int32, (rows, columns), 0)
    j = lax.broadcasted_iota(jnp.int32, (rows, columns), 1)
    return jnp.where(i // span == j, 1.0 / span, 0.0).astype(BF16)


def half_columns(core):
    return pl.ds(pl.multiple_of(core * HALF, HALF), HALF)


def block_at(core):
    return pl.ds(pl.multiple_of(core * BLOCK, BLOCK), BLOCK)


def open_kernel(where, k, v, own, other, coarse):
    core = where[0] % 2
    halve = pool_matrix(64, BLOCK, 2)
    for n, half, fine in ((1, 1 - core, other), (0, core, own)):
        columns = half_columns(half)
        fine[:, 0:512] = k[:, columns]
        fine[:, 512:1024] = v[:, columns]
        coarse[64 * n : 64 * n + 64] = dot(halve, fine[...]).astype(BF16)


def sides(first, own, recv, fine_same, fine_cross, half_same, half_cross):
    def pick(a, b):
        return jnp.where(first, a[...], b[...])

    return (
        pick(own, recv),
        pick(recv, own),
        pick(fine_cross, fine_same),
        pick(fine_same, fine_cross),
        pick(half_same[0:64], half_cross[64:128]),
        pick(half_cross[64:128], half_same[0:64]),
    )


def coarse_kernel(
    where, own, recv, fine_same, fine_cross, half_same, half_cross, same2, cross2, other2, quad3
):
    even = (where[0] // 2) % 2 == 0
    first = where[0] % 2 == 0
    low, high, fine_below, fine_above, half_below, half_above = sides(
        first, own, recv, fine_same, fine_cross, half_same, half_cross
    )
    fine = jnp.concatenate([pool_matrix(32, BLOCK, 4), pool_matrix(16, BLOCK, 8)], axis=0)
    half = jnp.concatenate([pool_matrix(32, 64, 2), pool_matrix(16, 64, 4)], axis=0)
    own_low = dot(fine[32:48], low).astype(BF16)
    own_high = dot(fine[32:48], high).astype(BF16)
    below_low = dot(half, half_below).astype(BF16)
    below_high = dot(fine, fine_below).astype(BF16)
    above_low = dot(fine, fine_above).astype(BF16)
    above_high = dot(half, half_above).astype(BF16)
    b2 = jnp.concatenate([below_low[0:32], below_high[0:32]], axis=0)
    a2 = jnp.concatenate([above_low[0:32], above_high[0:32]], axis=0)
    same2[...] = jnp.where(first, b2, a2)
    cross2[...] = jnp.where(first, a2, b2)
    other2[...] = jnp.where(even, a2, b2)
    own3 = jnp.concatenate([own_low, own_high], axis=0)
    b3 = jnp.concatenate([below_low[32:48], below_high[32:48]], axis=0)
    a3 = jnp.concatenate([above_low[32:48], above_high[32:48]], axis=0)
    quad3[0:32] = jnp.where(even, own3, b3)
    quad3[32:64] = jnp.where(even, a3, own3)


NEAR = 576
FAR = 384
NT = ((1,), (1,))
TN = ((0,), (0,))


def bias(valid, level):
    return jnp.where(valid, F32(level), F32(NEGATIVE))


def row_bias(pieces):
    return jnp.concatenate([jnp.full((rows, 1), value, F32) for rows, value in pieces], axis=0)


def columns_of(h):
    return (
        slice(h * HEAD, (h + 1) * HEAD),
        slice(HALF + h * HEAD, HALF + (h + 1) * HEAD),
    )


def back(weight, near, columns):
    edges = jnp.concatenate(
        [
            dot(near[384:576, columns], weight[384:576, 0:128], TN),
            dot(near[576:768, columns], weight[384:576, 128:256], TN),
        ],
        axis=1,
    )
    return dot(near[0:384, columns], weight[0:384], TN) + edges


def near_kernel(
    where, q, g, recv_q, recv_g, own_kv, recv_kv, fine_same, fine_cross, half_same, half_cross,
    queries, grads, keyvals, weights, dprobs, stats, outputs,
):
    chips = where[1] // 2
    core = where[0] % 2
    chip = where[0] // 2
    mine = half_columns(core)
    queries[block_at(core), :] = q[:, mine]
    queries[block_at(1 - core), :] = recv_q[:, mine]
    grads[block_at(core), :] = g[:, mine]
    grads[block_at(1 - core), :] = recv_g[:, mine]
    low, high, fine_below, fine_above, half_below, half_above = sides(
        core == 0, own_kv, recv_kv, fine_same, fine_cross, half_same, half_cross
    )
    halve = pool_matrix(64, BLOCK, 2)
    keyvals[0:128] = low
    keyvals[128:256] = high
    keyvals[256:320] = half_below
    keyvals[320:384] = half_above
    keyvals[384:512] = fine_below
    keyvals[512:576] = dot(halve, fine_above).astype(BF16)
    keyvals[576:704] = fine_above
    keyvals[704:768] = dot(halve, fine_below).astype(BF16)
    has_below = chip >= 1
    has_above = chip < chips - 1
    side = lax.broadcasted_iota(jnp.int32, (1, 256), 1) < 128
    fine_bias = jnp.where(side, bias(has_below, 0), bias(has_above, 0))
    half_bias = jnp.where(side, bias(has_above, 1), bias(has_below, 1))
    rows_bias = row_bias(((256, F32(0.0)), (64, bias(has_below, 1)), (64, bias(has_above, 1))))

    def product(columns, rows):
        shared = dot(keyvals[0:384, columns], rows, NT)
        edges = jnp.concatenate(
            [
                dot(keyvals[384:576, columns], rows[0:128], NT),
                dot(keyvals[576:768, columns], rows[128:256], NT),
            ],
            axis=1,
        )
        return shared, edges

    for h in range(4):
        kc, vc = columns_of(h)
        at = NEAR * h
        shared, edges = product(kc, queries[:, kc])
        scores = jnp.concatenate(
            [
                shared * FACTOR2 + rows_bias,
                edges[0:128] * FACTOR2 + fine_bias,
                edges[128:192] * FACTOR2 + half_bias,
            ],
            axis=0,
        )
        highest = jnp.max(scores, axis=0, keepdims=True)
        weight = jnp.exp2(scores - highest)
        weights[at : at + NEAR] = weight
        stats[h : h + 1] = highest
        stats[4 + h : 5 + h] = jnp.sum(weight, axis=0, keepdims=True)
        outputs[HEAD * h : HEAD * h + HEAD] = back(weight.astype(BF16), keyvals, vc)
        shared, edges = product(vc, grads[:, kc])
        dprobs[at : at + 384] = shared
        dprobs[at + 384 : at + NEAR] = edges


def main_kernel(
    where, queries, grads, outputs, stats, m2, p2, s2, z3, x3, s3,
    output, scales, dscores, gm2, gp2, gs2, gz3, gx3, gs3,
    far,
):
    chips = where[1] // 2
    core = where[0] % 2
    chip = where[0] // 2
    quad = chip // 2
    for n, piece in enumerate((m2, p2, s2, z3, x3, s3)):
        far[64 * n : 64 * n + 64] = piece[...]
    far2 = jnp.where(chip % 2 == 0, chip + 3, chip - 3)
    far3 = jnp.where(quad % 2 == 0, quad + 3, quad - 3)
    quads = chips // 2
    rows_bias = row_bias(
        (
            (64, bias(jnp.where(core == 0, chip >= 2, chip + 2 < chips), 2)),
            (64, bias(jnp.where(core == 0, chip + 2 < chips, chip >= 2), 2)),
            (64, bias((far2 >= 0) & (far2 < chips), 2)),
            (64, F32(3)),
            (64, bias(jnp.where(chip % ROW < ROW // 2, chip >= ROW, chip + ROW < chips), 3)),
            (64, bias((far3 >= 0) & (far3 < quads), 3)),
        )
    )
    for h in range(4):
        kc, vc = columns_of(h)
        qh = queries[:, kc]
        gh = grads[:, kc]
        scores = dot(far[:, kc], qh, NT) * FACTOR2 + rows_bias
        before = stats[h : h + 1]
        highest = jnp.maximum(before, jnp.max(scores, axis=0, keepdims=True))
        weight = jnp.exp2(scores - highest)
        shrink = jnp.exp2(before - highest)
        total = stats[4 + h : 5 + h] * shrink + jnp.sum(weight, axis=0, keepdims=True)
        inverse = 1.0 / total
        scale = shrink * inverse
        probs_far = weight * inverse
        low_far = probs_far.astype(BF16)
        attended = outputs[HEAD * h : HEAD * h + HEAD] * scale + dot(far[:, vc], low_far, TN)
        delta = jnp.sum(gh.astype(F32).T * attended, axis=0, keepdims=True)
        output[:, kc] = attended.T
        scales[h : h + 1] = scale
        scales[4 + h : 5 + h] = delta
        dscore_far = (probs_far * (dot(far[:, vc], gh, NT) - delta)).astype(BF16)
        dscores[FAR * h : FAR * h + FAR] = dscore_far
        terms_k = (dot(dscore_far, qh) * FACTOR).astype(BF16)
        terms_v = dot(low_far, gh).astype(BF16)
        for n, piece in enumerate((gm2, gp2, gs2, gz3, gx3, gs3)):
            piece[:, kc] = terms_k[64 * n : 64 * n + 64]
            piece[:, vc] = terms_v[64 * n : 64 * n + 64]


def rest_kernel(
    where, queries, grads, near, weights, dprobs, scales, dscores, output,
    m2, p2, s2, z3, x3, s3,
    keep, send, grad_below, grad_above,
    outs,
):
    core = where[0] % 2
    spread = spread_matrix(BLOCK, 64, 2)
    for h in range(4):
        kc, vc = columns_of(h)
        at = NEAR * h
        probs = weights[at : at + NEAR] * scales[h : h + 1]
        low = probs.astype(BF16)
        dscore = (probs * (dprobs[at : at + NEAR] - scales[4 + h : 5 + h])).astype(BF16)
        far = jnp.concatenate([piece[:, kc] for piece in (m2, p2, s2, z3, x3, s3)], axis=0)
        query_grad = back(dscore, near, kc) + dot(far, dscores[FAR * h : FAR * h + FAR], TN)
        outs[:, kc] = output[:, kc]
        outs[:, vc] = query_grad.T * FACTOR
        for columns, weight, rows, scale in (
            (kc, dscore, queries[:, kc], FACTOR),
            (vc, low, grads[:, kc], 1.0),
        ):
            shared = dot(weight[0:384], rows) * scale
            part_a = dot(weight[384:576, 0:128], rows[0:128]) * scale
            part_b = dot(weight[384:576, 128:256], rows[128:256]) * scale
            outs[:, PAIR + columns.start : PAIR + columns.stop] = shared[0:256]
            terms = shared[256:384].astype(BF16)
            grad_below[0:128, columns] = (
                part_a[0:128] + dot(spread, part_b[128:192].astype(BF16))
            ).astype(BF16)
            grad_below[128:192, columns] = terms[0:64]
            grad_above[0:128, columns] = (
                part_b[0:128] + dot(spread, part_a[128:192].astype(BF16))
            ).astype(BF16)
            grad_above[128:192, columns] = terms[64:128]
    keep[...] = outs[block_at(core), :]
    send[...] = outs[block_at(1 - core), :]


def fold_kernel(
    where, grad_below, grad_above, s3, z3, same2, cross2, other2,
    out_same, out_cross, half_same, half_cross, keep3, send3,
):
    even = (where[0] // 2) % 2 == 0

    def weigh(matrix, use):
        return jnp.where(use, matrix, jnp.zeros_like(matrix))

    def fold(base, pieces2, rows, use, fine, half):
        def rows_of(n):
            return jnp.concatenate(
                [piece[32 * n : 32 * n + 32] for piece in (pieces2, other2)]
                + [piece[rows + 16 * n : rows + 16 * n + 16] for piece in (z3, s3)],
                axis=0,
            )

        fine_matrix = jnp.concatenate(
            [spread_matrix(128, 32, 4), weigh(spread_matrix(128, 32, 4), use)]
            + [weigh(spread_matrix(128, 16, 8), use)] * 2,
            axis=1,
        )
        half_matrix = jnp.concatenate(
            [spread_matrix(64, 32, 2), weigh(spread_matrix(64, 32, 2), use)]
            + [weigh(spread_matrix(64, 16, 4), use)] * 2,
            axis=1,
        )
        return (
            (base[0:128].astype(F32) + dot(fine_matrix, rows_of(fine))).astype(BF16),
            (base[128:192].astype(F32) + dot(half_matrix, rows_of(half))).astype(BF16),
        )

    first = where[0] % 2 == 0
    from2 = jnp.where(first, same2[...], cross2[...])
    to2 = jnp.where(first, cross2[...], same2[...])
    fine_below, half_below = fold(grad_below, from2, 0, jnp.logical_not(even), 1, 0)
    fine_above, half_above = fold(grad_above, to2, 32, even, 0, 1)
    out_same[...] = jnp.where(first, fine_above, fine_below)
    out_cross[...] = jnp.where(first, fine_below, fine_above)
    half_same[...] = jnp.where(first, half_below, half_above)
    half_cross[...] = jnp.where(first, half_above, half_below)
    row = pl.multiple_of((where[0] // 2) % 2 * 32, 32)
    own3 = (z3[pl.ds(row, 32), :].astype(F32) + s3[pl.ds(row, 32), :].astype(F32)).astype(BF16)
    keep3[...] = jnp.where(first, own3[0:16], own3[16:32])
    send3[...] = jnp.where(first, own3[16:32], own3[0:16])


def join_kernel(where, out_keep, out_recv, attended, qg):
    core = where[0] % 2
    mine = half_columns(core)
    other = half_columns(1 - core)
    attended[:, mine] = out_keep[:, 0:512].astype(BF16)
    attended[:, other] = out_recv[:, 0:512].astype(BF16)
    qg[:, mine] = out_keep[:, 512:1024]
    qg[:, other] = out_recv[:, 512:1024]


def final_kernel(
    where, keep, recv, keep3, recv3, fine_same, fine_cross, half_same, half_cross,
    kg, vg, total, sems,
):
    core = where[0] % 2
    matrix = jnp.concatenate([spread_matrix(BLOCK, 64, 2), spread_matrix(BLOCK, 16, 8)], axis=1)
    copies = []
    for n, (side, own, fine, half, last) in enumerate(
        (
            (core, keep, fine_same, half_same, keep3),
            (1 - core, recv, fine_cross, half_cross, recv3),
        )
    ):
        coarse = jnp.concatenate([half[...], last[...]], axis=0)
        total[n] = own[:, PAIR : 2 * PAIR] + fine[...].astype(F32) + dot(matrix, coarse)
        for m, target in enumerate((kg, vg)):
            copies.append(
                pltpu.make_async_copy(
                    total.at[n, :, HALF * m : HALF * (m + 1)],
                    target.at[:, half_columns(side)],
                    sems.at[2 * n + m],
                )
            )
            copies[-1].start()
    for copy in copies:
        copy.wait()


def call(kernel, where, args, outs, scratch=(), space=pltpu.VMEM):
    return pl.pallas_call(
        kernel,
        out_shape=[jax.ShapeDtypeStruct(shape, dtype) for shape, dtype in outs],
        in_specs=[pl.BlockSpec(memory_space=pltpu.SMEM)]
        + [pl.BlockSpec(memory_space=pltpu.VMEM)] * len(args),
        out_specs=[pl.BlockSpec(memory_space=space)] * len(outs),
        scratch_shapes=list(scratch),
        compiler_params=pltpu.CompilerParams(vmem_limit_bytes=32 * 1024 * 1024),
    )(where, *args)


def sources(chips):
    def opposite(p):
        turn = ROW // 2 + 1 if p % 2 == 0 else ROW // 2 - 1
        return p - p % ROW + (p + turn) % ROW

    near = {
        "fine_same": lambda p, c: (p - 1, 1) if c == 1 else (p + 1, 0),
        "half_same": lambda p, c: (p - 1, 0) if c == 0 else (p + 1, 1),
        "far2": lambda p, c: (p + 2 if p % 2 == 0 else p - 2, c),
        "z3": lambda p, c: (opposite(p), c),
        "x3": lambda p, c: (p - ROW if p % ROW < ROW // 2 else p + ROW, c),
        "s3": lambda p, c: (p + 6 if p // 2 % 2 == 0 else p - 6, c),
    }
    closing = {
        "fine_same": lambda p, c: (p, 1 - c),
        "half_same": lambda p, c: (p, 1 - c),
        "far2": lambda p, c: (p ^ 1, c),
        "x3": lambda p, c: (p - p % ROW + ROW - 1 - p % ROW, c),
        "s3": lambda p, c: (p ^ 1, c),
    }

    def source(name, p, c):
        found = near[name](p, c)
        return found if 0 <= found[0] < chips else closing[name](p, c)

    return source


def on_device(query_rows, key_rows, value_rows, out_grad):
    position = lax.axis_index(AXES)
    devices = lax.axis_size(AXES)
    chips = devices // 2
    plan = sources(chips)
    where = jnp.stack([position, jnp.int32(devices)]).astype(jnp.int32)

    def swap(x):
        return lax.ppermute(x, AXES, [(i, i ^ 1) for i in range(devices)])

    def pairs(name):
        found = []
        for chip in range(chips):
            for core in range(2):
                source, side = plan(name, chip, core)
                found.append((2 * source + side, 2 * chip + core))
        return found

    def fetch(x, name):
        return lax.ppermute(x, AXES, pairs(name))

    def give(x, name):
        return lax.ppermute(x, AXES, [(b, a) for a, b in pairs(name)])

    recv_q = swap(query_rows)
    recv_g = swap(out_grad)
    own_kv, other_kv, half_kv = call(
        open_kernel, where, (key_rows, value_rows), [((BLOCK, PAIR), BF16)] * 3
    )
    recv_q, recv_g, own_kv, other_kv, half_kv = lax.optimization_barrier(
        (recv_q, recv_g, own_kv, other_kv, half_kv)
    )
    fine_cross = swap(fetch(other_kv, "fine_same"))
    half_same = fetch(half_kv, "half_same")
    half_cross = swap(half_same)
    fine_same = fetch(own_kv, "fine_same")
    recv_kv = swap(other_kv)
    near = (fine_same, fine_cross, half_same, half_cross)
    same2, cross2, other2, quad3 = call(
        coarse_kernel, where, (own_kv, recv_kv, *near), [((64, PAIR), BF16)] * 4
    )
    z3 = fetch(quad3, "z3")
    s3 = fetch(quad3, "s3")
    s2 = fetch(other2, "far2")
    same2 = fetch(same2, "half_same")
    cross2 = fetch(cross2, "fine_same")
    x3 = fetch(z3, "x3")
    queries, grads, near_kv, weights, dprobs, stats, outputs = call(
        near_kernel,
        where,
        (query_rows, out_grad, recv_q, recv_g, own_kv, recv_kv, *near),
        [
            ((2 * BLOCK, HALF), BF16),
            ((2 * BLOCK, HALF), BF16),
            ((768, PAIR), BF16),
            ((4 * NEAR, 2 * BLOCK), F32),
            ((4 * NEAR, 2 * BLOCK), F32),
            ((8, 2 * BLOCK), F32),
            ((4 * HEAD, 2 * BLOCK), F32),
        ],
    )
    far = (same2, cross2, s2, z3, x3, s3)
    output, scales, dscores, gm2, gp2, gs2, gz3, gx3, gs3 = call(
        main_kernel,
        where,
        (queries, grads, outputs, stats, *far),
        [
            ((2 * BLOCK, HALF), F32),
            ((8, 2 * BLOCK), F32),
            ((4 * FAR, 2 * BLOCK), BF16),
        ]
        + [((64, PAIR), BF16)] * 6,
        scratch=[pltpu.VMEM((FAR, PAIR), BF16)],
    )
    back_s3 = give(gs3, "s3")
    gz3, gs2, gp2, scales = lax.optimization_barrier((gz3 + give(gx3, "x3"), gs2, gp2, scales))
    back_z3 = give(gz3, "z3")
    back_s2 = give(gs2, "far2")
    back_m2 = give(gm2, "half_same")
    back_p2 = give(gp2, "fine_same")
    keep, send, grad_below, grad_above = call(
        rest_kernel,
        where,
        (queries, grads, near_kv, weights, dprobs, scales, dscores, output, *far),
        [
            ((BLOCK, 2 * PAIR), F32),
            ((BLOCK, 2 * PAIR), F32),
            ((192, PAIR), BF16),
            ((192, PAIR), BF16),
        ],
        scratch=[pltpu.VMEM((2 * BLOCK, 2 * PAIR), F32)],
    )
    fine_same, fine_cross, half_same, half_cross, keep3, send3 = call(
        fold_kernel,
        where,
        (grad_below, grad_above, back_s3, back_z3, back_m2, back_p2, back_s2),
        [((BLOCK, PAIR), BF16)] * 2
        + [((BLOCK // 2, PAIR), BF16)] * 2
        + [((16, PAIR), BF16)] * 2,
    )
    fine_same = give(fine_same, "fine_same")
    fine_cross = give(swap(fine_cross), "fine_same")
    half_same = give(half_same, "half_same")
    half_cross = give(swap(half_cross), "half_same")
    send, send3 = lax.optimization_barrier((send, send3))
    recv3 = swap(send3)
    recv = swap(send)
    attended, query_grad = call(
        join_kernel, where, (keep, recv), [((BLOCK, PAIR), BF16), ((BLOCK, PAIR), F32)]
    )
    attended, query_grad, keep3 = lax.optimization_barrier((attended, query_grad, keep3))
    key_grad, value_grad = call(
        final_kernel,
        where,
        (keep, recv, keep3, recv3, fine_same, fine_cross, half_same, half_cross),
        [((BLOCK, PAIR), F32)] * 2,
        scratch=[pltpu.VMEM((2, BLOCK, PAIR), F32), pltpu.SemaphoreType.DMA((4,))],
        space=pl.ANY,
    )
    return attended, query_grad, key_grad, value_grad


def solution(mesh):
    spec = P(AXES, None)
    return jax.shard_map(
        on_device, mesh=mesh, in_specs=(spec,) * 4, out_specs=(spec,) * 4, check_vma=False
    )
```

```python
import math

import jax
import jax.numpy as jnp
from jax import lax
from jax.experimental import pallas as pl
from jax.experimental.pallas import tpu as pltpu
from jax.sharding import PartitionSpec as P

HEADS = 8
HEAD = 128
LEVELS = 3
BLOCK = 128
HALF = 512
PAIR = 1024
ROW = 8
AXES = ("outer", "seq")
NEGATIVE = -1e30
FACTOR = 1.0 / math.sqrt(HEAD)
FACTOR2 = FACTOR / math.log(2.0)
BF16 = jnp.bfloat16
F32 = jnp.float32


def dot(a, b, dims=((1,), (0,))):
    return lax.dot_general(a, b, (dims, ((), ())), preferred_element_type=F32)


def pool_matrix(rows, columns, span):
    i = lax.broadcasted_iota(jnp.int32, (rows, columns), 0)
    j = lax.broadcasted_iota(jnp.int32, (rows, columns), 1)
    return jnp.where(j // span == i, 1.0 / span, 0.0).astype(BF16)


def spread_matrix(rows, columns, span):
    i = lax.broadcasted_iota(jnp.int32, (rows, columns), 0)
    j = lax.broadcasted_iota(jnp.int32, (rows, columns), 1)
    return jnp.where(i // span == j, 1.0 / span, 0.0).astype(BF16)


def half_columns(core):
    return pl.ds(pl.multiple_of(core * HALF, HALF), HALF)


def block_at(core):
    return pl.ds(pl.multiple_of(core * BLOCK, BLOCK), BLOCK)


def open_kernel(where, k, v, own, other, coarse):
    core = where[0] % 2
    halve = pool_matrix(64, BLOCK, 2)
    for n, half, fine in ((1, 1 - core, other), (0, core, own)):
        columns = half_columns(half)
        fine[:, 0:512] = k[:, columns]
        fine[:, 512:1024] = v[:, columns]
        coarse[64 * n : 64 * n + 64] = dot(halve, fine[...]).astype(BF16)


def sides(first, own, recv, fine_same, fine_cross, half_same, half_cross):
    def pick(a, b):
        return jnp.where(first, a[...], b[...])

    return (
        pick(own, recv),
        pick(recv, own),
        pick(fine_cross, fine_same),
        pick(fine_same, fine_cross),
        pick(half_same[0:64], half_cross[64:128]),
        pick(half_cross[64:128], half_same[0:64]),
    )


def coarse_kernel(
    where, own, recv, fine_same, fine_cross, half_same, half_cross, same2, cross2, other2, quad3
):
    even = (where[0] // 2) % 2 == 0
    first = where[0] % 2 == 0
    low, high, fine_below, fine_above, half_below, half_above = sides(
        first, own, recv, fine_same, fine_cross, half_same, half_cross
    )
    fine = jnp.concatenate([pool_matrix(32, BLOCK, 4), pool_matrix(16, BLOCK, 8)], axis=0)
    half = jnp.concatenate([pool_matrix(32, 64, 2), pool_matrix(16, 64, 4)], axis=0)
    own_low = dot(fine[32:48], low).astype(BF16)
    own_high = dot(fine[32:48], high).astype(BF16)
    below_low = dot(half, half_below).astype(BF16)
    below_high = dot(fine, fine_below).astype(BF16)
    above_low = dot(fine, fine_above).astype(BF16)
    above_high = dot(half, half_above).astype(BF16)
    b2 = jnp.concatenate([below_low[0:32], below_high[0:32]], axis=0)
    a2 = jnp.concatenate([above_low[0:32], above_high[0:32]], axis=0)
    same2[...] = jnp.where(first, b2, a2)
    cross2[...] = jnp.where(first, a2, b2)
    other2[...] = jnp.where(even, a2, b2)
    own3 = jnp.concatenate([own_low, own_high], axis=0)
    b3 = jnp.concatenate([below_low[32:48], below_high[32:48]], axis=0)
    a3 = jnp.concatenate([above_low[32:48], above_high[32:48]], axis=0)
    quad3[0:32] = jnp.where(even, own3, b3)
    quad3[32:64] = jnp.where(even, a3, own3)


NEAR = 576
FAR = 384
NT = ((1,), (1,))
TN = ((0,), (0,))


def bias(valid, level):
    return jnp.where(valid, F32(level), F32(NEGATIVE))


def row_bias(pieces):
    return jnp.concatenate([jnp.full((rows, 1), value, F32) for rows, value in pieces], axis=0)


def columns_of(h):
    return (
        slice(h * HEAD, (h + 1) * HEAD),
        slice(HALF + h * HEAD, HALF + (h + 1) * HEAD),
    )


def back(weight, near, columns):
    edges = jnp.concatenate(
        [
            dot(near[384:576, columns], weight[384:576, 0:128], TN),
            dot(near[576:768, columns], weight[384:576, 128:256], TN),
        ],
        axis=1,
    )
    return dot(near[0:384, columns], weight[0:384], TN) + edges


def near_kernel(
    where, q, g, recv_q, recv_g, own_kv, recv_kv, fine_same, fine_cross, half_same, half_cross,
    queries, grads, keyvals, weights, dprobs, stats, outputs,
):
    chips = where[1] // 2
    core = where[0] % 2
    chip = where[0] // 2
    mine = half_columns(core)
    queries[block_at(core), :] = q[:, mine]
    queries[block_at(1 - core), :] = recv_q[:, mine]
    grads[block_at(core), :] = g[:, mine]
    grads[block_at(1 - core), :] = recv_g[:, mine]
    low, high, fine_below, fine_above, half_below, half_above = sides(
        core == 0, own_kv, recv_kv, fine_same, fine_cross, half_same, half_cross
    )
    halve = pool_matrix(64, BLOCK, 2)
    keyvals[0:128] = low
    keyvals[128:256] = high
    keyvals[256:320] = half_below
    keyvals[320:384] = half_above
    keyvals[384:512] = fine_below
    keyvals[512:576] = dot(halve, fine_above).astype(BF16)
    keyvals[576:704] = fine_above
    keyvals[704:768] = dot(halve, fine_below).astype(BF16)
    has_below = chip >= 1
    has_above = chip < chips - 1
    side = lax.broadcasted_iota(jnp.int32, (1, 256), 1) < 128
    fine_bias = jnp.where(side, bias(has_below, 0), bias(has_above, 0))
    half_bias = jnp.where(side, bias(has_above, 1), bias(has_below, 1))
    rows_bias = row_bias(((256, F32(0.0)), (64, bias(has_below, 1)), (64, bias(has_above, 1))))

    def product(columns, rows):
        shared = dot(keyvals[0:384, columns], rows, NT)
        edges = jnp.concatenate(
            [
                dot(keyvals[384:576, columns], rows[0:128], NT),
                dot(keyvals[576:768, columns], rows[128:256], NT),
            ],
            axis=1,
        )
        return shared, edges

    for h in range(4):
        kc, vc = columns_of(h)
        at = NEAR * h
        shared, edges = product(kc, queries[:, kc])
        scores = jnp.concatenate(
            [
                shared * FACTOR2 + rows_bias,
                edges[0:128] * FACTOR2 + fine_bias,
                edges[128:192] * FACTOR2 + half_bias,
            ],
            axis=0,
        )
        highest = jnp.max(scores, axis=0, keepdims=True)
        weight = jnp.exp2(scores - highest)
        weights[at : at + NEAR] = weight
        stats[h : h + 1] = highest
        stats[4 + h : 5 + h] = jnp.sum(weight, axis=0, keepdims=True)
        outputs[HEAD * h : HEAD * h + HEAD] = back(weight.astype(BF16), keyvals, vc)
        shared, edges = product(vc, grads[:, kc])
        dprobs[at : at + 384] = shared
        dprobs[at + 384 : at + NEAR] = edges


def main_kernel(
    where, queries, grads, outputs, stats, m2, p2, s2, z3, x3, s3,
    output, scales, dscores, gm2, gp2, gs2, gz3, gx3, gs3,
    far,
):
    chips = where[1] // 2
    core = where[0] % 2
    chip = where[0] // 2
    quad = chip // 2
    for n, piece in enumerate((m2, p2, s2, z3, x3, s3)):
        far[64 * n : 64 * n + 64] = piece[...]
    far2 = jnp.where(chip % 2 == 0, chip + 3, chip - 3)
    far3 = jnp.where(quad % 2 == 0, quad + 3, quad - 3)
    quads = chips // 2
    rows_bias = row_bias(
        (
            (64, bias(jnp.where(core == 0, chip >= 2, chip + 2 < chips), 2)),
            (64, bias(jnp.where(core == 0, chip + 2 < chips, chip >= 2), 2)),
            (64, bias((far2 >= 0) & (far2 < chips), 2)),
            (64, F32(3)),
            (64, bias(jnp.where(chip % ROW < ROW // 2, chip >= ROW, chip + ROW < chips), 3)),
            (64, bias((far3 >= 0) & (far3 < quads), 3)),
        )
    )
    heads = [columns_of(h) for h in range(4)]
    scores = [dot(far[:, kc], queries[:, kc], NT) * FACTOR2 + rows_bias for kc, _ in heads]
    dprobs = [dot(far[:, vc], grads[:, kc], NT) for kc, vc in heads]
    probs = []
    for h in range(4):
        before = stats[h : h + 1]
        highest = jnp.maximum(before, jnp.max(scores[h], axis=0, keepdims=True))
        weight = jnp.exp2(scores[h] - highest)
        shrink = jnp.exp2(before - highest)
        total = stats[4 + h : 5 + h] * shrink + jnp.sum(weight, axis=0, keepdims=True)
        inverse = 1.0 / total
        scales[h : h + 1] = shrink * inverse
        probs.append(weight * inverse)
    lows = [p.astype(BF16) for p in probs]
    attended = [
        outputs[HEAD * h : HEAD * h + HEAD] * scales[h : h + 1] + dot(far[:, vc], lows[h], TN)
        for h, (_, vc) in enumerate(heads)
    ]
    terms_v = [dot(lows[h], grads[:, kc]).astype(BF16) for h, (kc, _) in enumerate(heads)]
    terms_k = []
    for h, (kc, _) in enumerate(heads):
        delta = jnp.sum(grads[:, kc].astype(F32).T * attended[h], axis=0, keepdims=True)
        scales[4 + h : 5 + h] = delta
        dscore = (probs[h] * (dprobs[h] - delta)).astype(BF16)
        dscores[FAR * h : FAR * h + FAR] = dscore
        terms_k.append((dot(dscore, queries[:, kc]) * FACTOR).astype(BF16))
    for h, (kc, vc) in enumerate(heads):
        output[:, kc] = attended[h].T
        for n, piece in enumerate((gm2, gp2, gs2, gz3, gx3, gs3)):
            piece[:, kc] = terms_k[h][64 * n : 64 * n + 64]
            piece[:, vc] = terms_v[h][64 * n : 64 * n + 64]


def rest_kernel(
    where, queries, grads, near, weights, dprobs, scales, dscores, output,
    m2, p2, s2, z3, x3, s3,
    keep, send, grad_below, grad_above,
    outs,
):
    core = where[0] % 2
    spread = spread_matrix(BLOCK, 64, 2)
    for h in range(4):
        kc, vc = columns_of(h)
        at = NEAR * h
        probs = weights[at : at + NEAR] * scales[h : h + 1]
        low = probs.astype(BF16)
        dscore = (probs * (dprobs[at : at + NEAR] - scales[4 + h : 5 + h])).astype(BF16)
        far = jnp.concatenate([piece[:, kc] for piece in (m2, p2, s2, z3, x3, s3)], axis=0)
        query_grad = back(dscore, near, kc) + dot(far, dscores[FAR * h : FAR * h + FAR], TN)
        outs[:, kc] = output[:, kc]
        outs[:, vc] = query_grad.T * FACTOR
        for columns, weight, rows, scale in (
            (kc, dscore, queries[:, kc], FACTOR),
            (vc, low, grads[:, kc], 1.0),
        ):
            shared = dot(weight[0:384], rows) * scale
            part_a = dot(weight[384:576, 0:128], rows[0:128]) * scale
            part_b = dot(weight[384:576, 128:256], rows[128:256]) * scale
            outs[:, PAIR + columns.start : PAIR + columns.stop] = shared[0:256]
            terms = shared[256:384].astype(BF16)
            grad_below[0:128, columns] = (
                part_a[0:128] + dot(spread, part_b[128:192].astype(BF16))
            ).astype(BF16)
            grad_below[128:192, columns] = terms[0:64]
            grad_above[0:128, columns] = (
                part_b[0:128] + dot(spread, part_a[128:192].astype(BF16))
            ).astype(BF16)
            grad_above[128:192, columns] = terms[64:128]
    keep[...] = outs[block_at(core), :]
    send[...] = outs[block_at(1 - core), :]


def fold_kernel(
    where, grad_below, grad_above, s3, z3, same2, cross2, other2,
    out_same, out_cross, half_same, half_cross, keep3, send3,
):
    even = (where[0] // 2) % 2 == 0

    def weigh(matrix, use):
        return jnp.where(use, matrix, jnp.zeros_like(matrix))

    def fold(base, pieces2, rows, use, fine, half):
        def rows_of(n):
            return jnp.concatenate(
                [piece[32 * n : 32 * n + 32] for piece in (pieces2, other2)]
                + [piece[rows + 16 * n : rows + 16 * n + 16] for piece in (z3, s3)],
                axis=0,
            )

        fine_matrix = jnp.concatenate(
            [spread_matrix(128, 32, 4), weigh(spread_matrix(128, 32, 4), use)]
            + [weigh(spread_matrix(128, 16, 8), use)] * 2,
            axis=1,
        )
        half_matrix = jnp.concatenate(
            [spread_matrix(64, 32, 2), weigh(spread_matrix(64, 32, 2), use)]
            + [weigh(spread_matrix(64, 16, 4), use)] * 2,
            axis=1,
        )
        return (
            (base[0:128].astype(F32) + dot(fine_matrix, rows_of(fine))).astype(BF16),
            (base[128:192].astype(F32) + dot(half_matrix, rows_of(half))).astype(BF16),
        )

    first = where[0] % 2 == 0
    from2 = jnp.where(first, same2[...], cross2[...])
    to2 = jnp.where(first, cross2[...], same2[...])
    fine_below, half_below = fold(grad_below, from2, 0, jnp.logical_not(even), 1, 0)
    fine_above, half_above = fold(grad_above, to2, 32, even, 0, 1)
    out_same[...] = jnp.where(first, fine_above, fine_below)
    out_cross[...] = jnp.where(first, fine_below, fine_above)
    half_same[...] = jnp.where(first, half_below, half_above)
    half_cross[...] = jnp.where(first, half_above, half_below)
    row = pl.multiple_of((where[0] // 2) % 2 * 32, 32)
    own3 = (z3[pl.ds(row, 32), :].astype(F32) + s3[pl.ds(row, 32), :].astype(F32)).astype(BF16)
    keep3[...] = jnp.where(first, own3[0:16], own3[16:32])
    send3[...] = jnp.where(first, own3[16:32], own3[0:16])


def join_kernel(where, out_keep, out_recv, attended, qg):
    core = where[0] % 2
    mine = half_columns(core)
    other = half_columns(1 - core)
    attended[:, mine] = out_keep[:, 0:512].astype(BF16)
    attended[:, other] = out_recv[:, 0:512].astype(BF16)
    qg[:, mine] = out_keep[:, 512:1024]
    qg[:, other] = out_recv[:, 512:1024]


def final_kernel(
    where, keep, recv, keep3, recv3, fine_same, fine_cross, half_same, half_cross,
    kg, vg, total, sems,
):
    core = where[0] % 2
    matrix = jnp.concatenate([spread_matrix(BLOCK, 64, 2), spread_matrix(BLOCK, 16, 8)], axis=1)
    copies = []
    for n, (side, own, fine, half, last) in enumerate(
        (
            (core, keep, fine_same, half_same, keep3),
            (1 - core, recv, fine_cross, half_cross, recv3),
        )
    ):
        coarse = jnp.concatenate([half[...], last[...]], axis=0)
        total[n] = own[:, PAIR : 2 * PAIR] + fine[...].astype(F32) + dot(matrix, coarse)
        for m, target in enumerate((kg, vg)):
            copies.append(
                pltpu.make_async_copy(
                    total.at[n, :, HALF * m : HALF * (m + 1)],
                    target.at[:, half_columns(side)],
                    sems.at[2 * n + m],
                )
            )
            copies[-1].start()
    for copy in copies:
        copy.wait()


def call(kernel, where, args, outs, scratch=(), space=pltpu.VMEM):
    return pl.pallas_call(
        kernel,
        out_shape=[jax.ShapeDtypeStruct(shape, dtype) for shape, dtype in outs],
        in_specs=[pl.BlockSpec(memory_space=pltpu.SMEM)]
        + [pl.BlockSpec(memory_space=pltpu.VMEM)] * len(args),
        out_specs=[pl.BlockSpec(memory_space=space)] * len(outs),
        scratch_shapes=list(scratch),
        compiler_params=pltpu.CompilerParams(vmem_limit_bytes=32 * 1024 * 1024),
    )(where, *args)


def sources(chips):
    def opposite(p):
        turn = ROW // 2 + 1 if p % 2 == 0 else ROW // 2 - 1
        return p - p % ROW + (p + turn) % ROW

    near = {
        "fine_same": lambda p, c: (p - 1, 1) if c == 1 else (p + 1, 0),
        "half_same": lambda p, c: (p - 1, 0) if c == 0 else (p + 1, 1),
        "far2": lambda p, c: (p + 2 if p % 2 == 0 else p - 2, c),
        "z3": lambda p, c: (opposite(p), c),
        "x3": lambda p, c: (p - ROW if p % ROW < ROW // 2 else p + ROW, c),
        "s3": lambda p, c: (p + 6 if p // 2 % 2 == 0 else p - 6, c),
    }
    closing = {
        "fine_same": lambda p, c: (p, 1 - c),
        "half_same": lambda p, c: (p, 1 - c),
        "far2": lambda p, c: (p ^ 1, c),
        "x3": lambda p, c: (p - p % ROW + ROW - 1 - p % ROW, c),
        "s3": lambda p, c: (p ^ 1, c),
    }

    def source(name, p, c):
        found = near[name](p, c)
        return found if 0 <= found[0] < chips else closing[name](p, c)

    return source


def on_device(query_rows, key_rows, value_rows, out_grad):
    position = lax.axis_index(AXES)
    devices = lax.axis_size(AXES)
    chips = devices // 2
    plan = sources(chips)
    where = jnp.stack([position, jnp.int32(devices)]).astype(jnp.int32)

    def swap(x):
        return lax.ppermute(x, AXES, [(i, i ^ 1) for i in range(devices)])

    def pairs(name):
        found = []
        for chip in range(chips):
            for core in range(2):
                source, side = plan(name, chip, core)
                found.append((2 * source + side, 2 * chip + core))
        return found

    def fetch(x, name):
        return lax.ppermute(x, AXES, pairs(name))

    def give(x, name):
        return lax.ppermute(x, AXES, [(b, a) for a, b in pairs(name)])

    recv_q = swap(query_rows)
    recv_g = swap(out_grad)
    own_kv, other_kv, half_kv = call(
        open_kernel, where, (key_rows, value_rows), [((BLOCK, PAIR), BF16)] * 3
    )
    recv_q, recv_g, own_kv, other_kv, half_kv = lax.optimization_barrier(
        (recv_q, recv_g, own_kv, other_kv, half_kv)
    )
    fine_cross = swap(fetch(other_kv, "fine_same"))
    half_same = fetch(half_kv, "half_same")
    half_cross = swap(half_same)
    fine_same = fetch(own_kv, "fine_same")
    recv_kv = swap(other_kv)
    near = (fine_same, fine_cross, half_same, half_cross)
    same2, cross2, other2, quad3 = call(
        coarse_kernel, where, (own_kv, recv_kv, *near), [((64, PAIR), BF16)] * 4
    )
    z3 = fetch(quad3, "z3")
    s3 = fetch(quad3, "s3")
    s2 = fetch(other2, "far2")
    same2 = fetch(same2, "half_same")
    cross2 = fetch(cross2, "fine_same")
    x3 = fetch(z3, "x3")
    queries, grads, near_kv, weights, dprobs, stats, outputs = call(
        near_kernel,
        where,
        (query_rows, out_grad, recv_q, recv_g, own_kv, recv_kv, *near),
        [
            ((2 * BLOCK, HALF), BF16),
            ((2 * BLOCK, HALF), BF16),
            ((768, PAIR), BF16),
            ((4 * NEAR, 2 * BLOCK), F32),
            ((4 * NEAR, 2 * BLOCK), F32),
            ((8, 2 * BLOCK), F32),
            ((4 * HEAD, 2 * BLOCK), F32),
        ],
    )
    far = (same2, cross2, s2, z3, x3, s3)
    output, scales, dscores, gm2, gp2, gs2, gz3, gx3, gs3 = call(
        main_kernel,
        where,
        (queries, grads, outputs, stats, *far),
        [
            ((2 * BLOCK, HALF), F32),
            ((8, 2 * BLOCK), F32),
            ((4 * FAR, 2 * BLOCK), BF16),
        ]
        + [((64, PAIR), BF16)] * 6,
        scratch=[pltpu.VMEM((FAR, PAIR), BF16)],
    )
    back_s3 = give(gs3, "s3")
    gz3, gs2, gp2, scales = lax.optimization_barrier((gz3 + give(gx3, "x3"), gs2, gp2, scales))
    back_z3 = give(gz3, "z3")
    back_s2 = give(gs2, "far2")
    back_m2 = give(gm2, "half_same")
    back_p2 = give(gp2, "fine_same")
    keep, send, grad_below, grad_above = call(
        rest_kernel,
        where,
        (queries, grads, near_kv, weights, dprobs, scales, dscores, output, *far),
        [
            ((BLOCK, 2 * PAIR), F32),
            ((BLOCK, 2 * PAIR), F32),
            ((192, PAIR), BF16),
            ((192, PAIR), BF16),
        ],
        scratch=[pltpu.VMEM((2 * BLOCK, 2 * PAIR), F32)],
    )
    fine_same, fine_cross, half_same, half_cross, keep3, send3 = call(
        fold_kernel,
        where,
        (grad_below, grad_above, back_s3, back_z3, back_m2, back_p2, back_s2),
        [((BLOCK, PAIR), BF16)] * 2
        + [((BLOCK // 2, PAIR), BF16)] * 2
        + [((16, PAIR), BF16)] * 2,
    )
    fine_same = give(fine_same, "fine_same")
    fine_cross = give(swap(fine_cross), "fine_same")
    half_same = give(half_same, "half_same")
    half_cross = give(swap(half_cross), "half_same")
    send, send3 = lax.optimization_barrier((send, send3))
    recv3 = swap(send3)
    recv = swap(send)
    attended, query_grad = call(
        join_kernel, where, (keep, recv), [((BLOCK, PAIR), BF16), ((BLOCK, PAIR), F32)]
    )
    attended, query_grad, keep3 = lax.optimization_barrier((attended, query_grad, keep3))
    key_grad, value_grad = call(
        final_kernel,
        where,
        (keep, recv, keep3, recv3, fine_same, fine_cross, half_same, half_cross),
        [((BLOCK, PAIR), F32)] * 2,
        scratch=[pltpu.VMEM((2, BLOCK, PAIR), F32), pltpu.SemaphoreType.DMA((4,))],
        space=pl.ANY,
    )
    return attended, query_grad, key_grad, value_grad


def solution(mesh):
    spec = P(AXES, None)
    return jax.shard_map(
        on_device, mesh=mesh, in_specs=(spec,) * 4, out_specs=(spec,) * 4, check_vma=False
    )
```

```python
import math

import jax
import jax.numpy as jnp
from jax import lax
from jax.experimental import pallas as pl
from jax.experimental.pallas import tpu as pltpu
from jax.sharding import PartitionSpec as P

HEADS = 8
HEAD = 128
LEVELS = 3
BLOCK = 128
HALF = 512
PAIR = 1024
ROW = 8
AXES = ("outer", "seq")
NEGATIVE = -1e30
FACTOR = 1.0 / math.sqrt(HEAD)
FACTOR2 = FACTOR / math.log(2.0)
BF16 = jnp.bfloat16
F32 = jnp.float32


def dot(a, b, dims=((1,), (0,))):
    return lax.dot_general(a, b, (dims, ((), ())), preferred_element_type=F32)


def pool_matrix(rows, columns, span):
    i = lax.broadcasted_iota(jnp.int32, (rows, columns), 0)
    j = lax.broadcasted_iota(jnp.int32, (rows, columns), 1)
    return jnp.where(j // span == i, 1.0 / span, 0.0).astype(BF16)


def spread_matrix(rows, columns, span):
    i = lax.broadcasted_iota(jnp.int32, (rows, columns), 0)
    j = lax.broadcasted_iota(jnp.int32, (rows, columns), 1)
    return jnp.where(i // span == j, 1.0 / span, 0.0).astype(BF16)


def half_columns(core):
    return pl.ds(pl.multiple_of(core * HALF, HALF), HALF)


def block_at(core):
    return pl.ds(pl.multiple_of(core * BLOCK, BLOCK), BLOCK)


def open_kernel(where, k, v, own, other, coarse):
    core = where[0] % 2
    halve = pool_matrix(64, BLOCK, 2)
    for n, half, fine in ((1, 1 - core, other), (0, core, own)):
        columns = half_columns(half)
        fine[:, 0:512] = k[:, columns]
        fine[:, 512:1024] = v[:, columns]
        coarse[64 * n : 64 * n + 64] = dot(halve, fine[...]).astype(BF16)


def sides(first, own, recv, fine_same, fine_cross, half_same, half_cross):
    def pick(a, b):
        return jnp.where(first, a[...], b[...])

    return (
        pick(own, recv),
        pick(recv, own),
        pick(fine_cross, fine_same),
        pick(fine_same, fine_cross),
        pick(half_same[0:64], half_cross[64:128]),
        pick(half_cross[64:128], half_same[0:64]),
    )


def coarse_kernel(
    where, own, recv, fine_same, fine_cross, half_same, half_cross, same2, cross2, other2, quad3
):
    even = (where[0] // 2) % 2 == 0
    first = where[0] % 2 == 0
    low, high, fine_below, fine_above, half_below, half_above = sides(
        first, own, recv, fine_same, fine_cross, half_same, half_cross
    )
    fine = jnp.concatenate([pool_matrix(32, BLOCK, 4), pool_matrix(16, BLOCK, 8)], axis=0)
    half = jnp.concatenate([pool_matrix(32, 64, 2), pool_matrix(16, 64, 4)], axis=0)
    own_low = dot(fine[32:48], low).astype(BF16)
    own_high = dot(fine[32:48], high).astype(BF16)
    below_low = dot(half, half_below).astype(BF16)
    below_high = dot(fine, fine_below).astype(BF16)
    above_low = dot(fine, fine_above).astype(BF16)
    above_high = dot(half, half_above).astype(BF16)
    b2 = jnp.concatenate([below_low[0:32], below_high[0:32]], axis=0)
    a2 = jnp.concatenate([above_low[0:32], above_high[0:32]], axis=0)
    same2[...] = jnp.where(first, b2, a2)
    cross2[...] = jnp.where(first, a2, b2)
    other2[...] = jnp.where(even, a2, b2)
    own3 = jnp.concatenate([own_low, own_high], axis=0)
    b3 = jnp.concatenate([below_low[32:48], below_high[32:48]], axis=0)
    a3 = jnp.concatenate([above_low[32:48], above_high[32:48]], axis=0)
    quad3[0:32] = jnp.where(even, own3, b3)
    quad3[32:64] = jnp.where(even, a3, own3)


NEAR = 576
FAR = 384
NT = ((1,), (1,))
TN = ((0,), (0,))


def bias(valid, level):
    return jnp.where(valid, F32(level), F32(NEGATIVE))


def row_bias(pieces):
    return jnp.concatenate([jnp.full((rows, 1), value, F32) for rows, value in pieces], axis=0)


def columns_of(h):
    return (
        slice(h * HEAD, (h + 1) * HEAD),
        slice(HALF + h * HEAD, HALF + (h + 1) * HEAD),
    )


def back(weight, near, columns):
    edges = jnp.concatenate(
        [
            dot(near[384:576, columns], weight[384:576, 0:128], TN),
            dot(near[576:768, columns], weight[384:576, 128:256], TN),
        ],
        axis=1,
    )
    return dot(near[0:384, columns], weight[0:384], TN) + edges


def near_kernel(
    where, q, g, recv_q, recv_g, own_kv, recv_kv, fine_same, fine_cross, half_same, half_cross,
    queries, grads, keyvals, weights, dprobs, stats, outputs,
):
    chips = where[1] // 2
    core = where[0] % 2
    chip = where[0] // 2
    mine = half_columns(core)
    queries[block_at(core), :] = q[:, mine]
    queries[block_at(1 - core), :] = recv_q[:, mine]
    grads[block_at(core), :] = g[:, mine]
    grads[block_at(1 - core), :] = recv_g[:, mine]
    low, high, fine_below, fine_above, half_below, half_above = sides(
        core == 0, own_kv, recv_kv, fine_same, fine_cross, half_same, half_cross
    )
    halve = pool_matrix(64, BLOCK, 2)
    keyvals[0:128] = low
    keyvals[128:256] = high
    keyvals[256:320] = half_below
    keyvals[320:384] = half_above
    keyvals[384:512] = fine_below
    keyvals[512:576] = dot(halve, fine_above).astype(BF16)
    keyvals[576:704] = fine_above
    keyvals[704:768] = dot(halve, fine_below).astype(BF16)
    has_below = chip >= 1
    has_above = chip < chips - 1
    side = lax.broadcasted_iota(jnp.int32, (1, 256), 1) < 128
    fine_bias = jnp.where(side, bias(has_below, 0), bias(has_above, 0))
    half_bias = jnp.where(side, bias(has_above, 1), bias(has_below, 1))
    rows_bias = row_bias(((256, F32(0.0)), (64, bias(has_below, 1)), (64, bias(has_above, 1))))

    def product(columns, rows):
        shared = dot(keyvals[0:384, columns], rows, NT)
        edges = jnp.concatenate(
            [
                dot(keyvals[384:576, columns], rows[0:128], NT),
                dot(keyvals[576:768, columns], rows[128:256], NT),
            ],
            axis=1,
        )
        return shared, edges

    for h in range(4):
        kc, vc = columns_of(h)
        at = NEAR * h
        shared, edges = product(kc, queries[:, kc])
        scores = jnp.concatenate(
            [
                shared * FACTOR2 + rows_bias,
                edges[0:128] * FACTOR2 + fine_bias,
                edges[128:192] * FACTOR2 + half_bias,
            ],
            axis=0,
        )
        highest = jnp.max(scores, axis=0, keepdims=True)
        weight = jnp.exp2(scores - highest)
        weights[at : at + NEAR] = weight
        stats[h : h + 1] = highest
        stats[4 + h : 5 + h] = jnp.sum(weight, axis=0, keepdims=True)
        outputs[HEAD * h : HEAD * h + HEAD] = back(weight.astype(BF16), keyvals, vc)
        shared, edges = product(vc, grads[:, kc])
        dprobs[at : at + 384] = shared
        dprobs[at + 384 : at + NEAR] = edges


def main_kernel(
    where, queries, grads, outputs, stats, m2, p2, s2, z3, x3, s3,
    output, scales, dscores, gm2, gp2, gs2, gz3, gx3, gs3,
    far,
):
    chips = where[1] // 2
    core = where[0] % 2
    chip = where[0] // 2
    quad = chip // 2
    for n, piece in enumerate((m2, p2, s2, z3, x3, s3)):
        far[64 * n : 64 * n + 64] = piece[...]
    far2 = jnp.where(chip % 2 == 0, chip + 3, chip - 3)
    far3 = jnp.where(quad % 2 == 0, quad + 3, quad - 3)
    quads = chips // 2
    rows_bias = row_bias(
        (
            (64, bias(jnp.where(core == 0, chip >= 2, chip + 2 < chips), 2)),
            (64, bias(jnp.where(core == 0, chip + 2 < chips, chip >= 2), 2)),
            (64, bias((far2 >= 0) & (far2 < chips), 2)),
            (64, F32(3)),
            (64, bias(jnp.where(chip % ROW < ROW // 2, chip >= ROW, chip + ROW < chips), 3)),
            (64, bias((far3 >= 0) & (far3 < quads), 3)),
        )
    )
    heads = [columns_of(h) for h in range(4)]
    scores = [dot(far[:, kc], queries[:, kc], NT) * FACTOR2 + rows_bias for kc, _ in heads]
    dprobs = [dot(far[:, vc], grads[:, kc], NT) for kc, vc in heads]
    probs = []
    for h in range(4):
        before = stats[h : h + 1]
        highest = jnp.maximum(before, jnp.max(scores[h], axis=0, keepdims=True))
        weight = jnp.exp2(scores[h] - highest)
        shrink = jnp.exp2(before - highest)
        total = stats[4 + h : 5 + h] * shrink + jnp.sum(weight, axis=0, keepdims=True)
        inverse = 1.0 / total
        scales[h : h + 1] = shrink * inverse
        probs.append(weight * inverse)
    lows = [p.astype(BF16) for p in probs]
    attended = [
        outputs[HEAD * h : HEAD * h + HEAD] * scales[h : h + 1] + dot(far[:, vc], lows[h], TN)
        for h, (_, vc) in enumerate(heads)
    ]
    terms_v = [dot(lows[h], grads[:, kc]).astype(BF16) for h, (kc, _) in enumerate(heads)]
    terms_k = []
    for h, (kc, _) in enumerate(heads):
        delta = jnp.sum(grads[:, kc].astype(F32).T * attended[h], axis=0, keepdims=True)
        scales[4 + h : 5 + h] = delta
        dscore = (probs[h] * (dprobs[h] - delta)).astype(BF16)
        dscores[FAR * h : FAR * h + FAR] = dscore
        terms_k.append((dot(dscore, queries[:, kc]) * FACTOR).astype(BF16))
    for h, (kc, vc) in enumerate(heads):
        output[:, kc] = attended[h].T
        for n, piece in enumerate((gm2, gp2, gs2, gz3, gx3, gs3)):
            piece[:, kc] = terms_k[h][64 * n : 64 * n + 64]
            piece[:, vc] = terms_v[h][64 * n : 64 * n + 64]


def rest_kernel(
    where, queries, grads, near, weights, dprobs, scales, dscores, output,
    m2, p2, s2, z3, x3, s3,
    keep, send, grad_below, grad_above,
    outs,
):
    core = where[0] % 2
    spread = spread_matrix(BLOCK, 64, 2)
    for h in range(4):
        kc, vc = columns_of(h)
        at = NEAR * h
        probs = weights[at : at + NEAR] * scales[h : h + 1]
        low = probs.astype(BF16)
        dscore = (probs * (dprobs[at : at + NEAR] - scales[4 + h : 5 + h])).astype(BF16)
        far = jnp.concatenate([piece[:, kc] for piece in (m2, p2, s2, z3, x3, s3)], axis=0)
        query_grad = back(dscore, near, kc) + dot(far, dscores[FAR * h : FAR * h + FAR], TN)
        outs[:, kc] = output[:, kc]
        outs[:, vc] = query_grad.T * FACTOR
        for columns, weight, rows, scale in (
            (kc, dscore, queries[:, kc], FACTOR),
            (vc, low, grads[:, kc], 1.0),
        ):
            shared = dot(weight[0:384], rows) * scale
            part_a = dot(weight[384:576, 0:128], rows[0:128]) * scale
            part_b = dot(weight[384:576, 128:256], rows[128:256]) * scale
            outs[:, PAIR + columns.start : PAIR + columns.stop] = shared[0:256]
            terms = shared[256:384].astype(BF16)
            grad_below[0:128, columns] = (
                part_a[0:128] + dot(spread, part_b[128:192].astype(BF16))
            ).astype(BF16)
            grad_below[128:192, columns] = terms[0:64]
            grad_above[0:128, columns] = (
                part_b[0:128] + dot(spread, part_a[128:192].astype(BF16))
            ).astype(BF16)
            grad_above[128:192, columns] = terms[64:128]
    keep[...] = outs[block_at(core), :]
    send[...] = outs[block_at(1 - core), :]


def fold_kernel(
    where, grad_below, grad_above, s3, z3, same2, cross2, other2,
    out_same, out_cross, half_same, half_cross, keep3, send3,
):
    even = (where[0] // 2) % 2 == 0

    def weigh(matrix, use):
        return jnp.where(use, matrix, jnp.zeros_like(matrix))

    def fold(base, pieces2, rows, use, fine, half):
        def rows_of(n):
            return jnp.concatenate(
                [piece[32 * n : 32 * n + 32] for piece in (pieces2, other2)]
                + [piece[rows + 16 * n : rows + 16 * n + 16] for piece in (z3, s3)],
                axis=0,
            )

        fine_matrix = jnp.concatenate(
            [spread_matrix(128, 32, 4), weigh(spread_matrix(128, 32, 4), use)]
            + [weigh(spread_matrix(128, 16, 8), use)] * 2,
            axis=1,
        )
        half_matrix = jnp.concatenate(
            [spread_matrix(64, 32, 2), weigh(spread_matrix(64, 32, 2), use)]
            + [weigh(spread_matrix(64, 16, 4), use)] * 2,
            axis=1,
        )
        return (
            (base[0:128].astype(F32) + dot(fine_matrix, rows_of(fine))).astype(BF16),
            (base[128:192].astype(F32) + dot(half_matrix, rows_of(half))).astype(BF16),
        )

    first = where[0] % 2 == 0
    from2 = jnp.where(first, same2[...], cross2[...])
    to2 = jnp.where(first, cross2[...], same2[...])
    fine_below, half_below = fold(grad_below, from2, 0, jnp.logical_not(even), 1, 0)
    fine_above, half_above = fold(grad_above, to2, 32, even, 0, 1)
    out_same[...] = jnp.where(first, fine_above, fine_below)
    out_cross[...] = jnp.where(first, fine_below, fine_above)
    half_same[...] = jnp.where(first, half_below, half_above)
    half_cross[...] = jnp.where(first, half_above, half_below)
    row = pl.multiple_of((where[0] // 2) % 2 * 32, 32)
    own3 = (z3[pl.ds(row, 32), :].astype(F32) + s3[pl.ds(row, 32), :].astype(F32)).astype(BF16)
    keep3[...] = jnp.where(first, own3[0:16], own3[16:32])
    send3[...] = jnp.where(first, own3[16:32], own3[0:16])


def join_kernel(where, out_keep, out_recv, attended, qg):
    core = where[0] % 2
    mine = half_columns(core)
    other = half_columns(1 - core)
    attended[:, mine] = out_keep[:, 0:512].astype(BF16)
    attended[:, other] = out_recv[:, 0:512].astype(BF16)
    qg[:, mine] = out_keep[:, 512:1024]
    qg[:, other] = out_recv[:, 512:1024]


def final_kernel(
    where, keep, recv, keep3, recv3, fine_same, fine_cross, half_same, half_cross,
    kg, vg, total, sems,
):
    core = where[0] % 2
    matrix = jnp.concatenate([spread_matrix(BLOCK, 64, 2), spread_matrix(BLOCK, 16, 8)], axis=1)
    copies = []
    for n, (side, own, fine, half, last) in enumerate(
        (
            (core, keep, fine_same, half_same, keep3),
            (1 - core, recv, fine_cross, half_cross, recv3),
        )
    ):
        coarse = jnp.concatenate([half[...], last[...]], axis=0)
        total[n] = own[:, PAIR : 2 * PAIR] + fine[...].astype(F32) + dot(matrix, coarse)
        for m, target in enumerate((kg, vg)):
            copies.append(
                pltpu.make_async_copy(
                    total.at[n, :, HALF * m : HALF * (m + 1)],
                    target.at[:, half_columns(side)],
                    sems.at[2 * n + m],
                )
            )
            copies[-1].start()
    for copy in copies:
        copy.wait()


def call(kernel, where, args, outs, scratch=(), space=pltpu.VMEM):
    return pl.pallas_call(
        kernel,
        out_shape=[jax.ShapeDtypeStruct(shape, dtype) for shape, dtype in outs],
        in_specs=[pl.BlockSpec(memory_space=pltpu.SMEM)]
        + [pl.BlockSpec(memory_space=pltpu.VMEM)] * len(args),
        out_specs=[pl.BlockSpec(memory_space=space)] * len(outs),
        scratch_shapes=list(scratch),
        compiler_params=pltpu.CompilerParams(vmem_limit_bytes=32 * 1024 * 1024),
    )(where, *args)


def sources(chips):
    def opposite(p):
        turn = ROW // 2 + 1 if p % 2 == 0 else ROW // 2 - 1
        return p - p % ROW + (p + turn) % ROW

    near = {
        "fine_same": lambda p, c: (p - 1, 1) if c == 1 else (p + 1, 0),
        "half_same": lambda p, c: (p - 1, 0) if c == 0 else (p + 1, 1),
        "far2": lambda p, c: (p + 2 if p % 2 == 0 else p - 2, c),
        "z3": lambda p, c: (opposite(p), c),
        "x3": lambda p, c: (p - ROW if p % ROW < ROW // 2 else p + ROW, c),
        "s3": lambda p, c: (p + 6 if p // 2 % 2 == 0 else p - 6, c),
    }
    closing = {
        "fine_same": lambda p, c: (p, 1 - c),
        "half_same": lambda p, c: (p, 1 - c),
        "far2": lambda p, c: (p ^ 1, c),
        "x3": lambda p, c: (p - p % ROW + ROW - 1 - p % ROW, c),
        "s3": lambda p, c: (p ^ 1, c),
    }

    def source(name, p, c):
        found = near[name](p, c)
        return found if 0 <= found[0] < chips else closing[name](p, c)

    return source


def on_device(query_rows, key_rows, value_rows, out_grad):
    position = lax.axis_index(AXES)
    devices = lax.axis_size(AXES)
    chips = devices // 2
    plan = sources(chips)
    where = jnp.stack([position, jnp.int32(devices)]).astype(jnp.int32)

    def swap(x):
        return lax.ppermute(x, AXES, [(i, i ^ 1) for i in range(devices)])

    def pairs(name):
        found = []
        for chip in range(chips):
            for core in range(2):
                source, side = plan(name, chip, core)
                found.append((2 * source + side, 2 * chip + core))
        return found

    def fetch(x, name):
        return lax.ppermute(x, AXES, pairs(name))

    def give(x, name):
        return lax.ppermute(x, AXES, [(b, a) for a, b in pairs(name)])

    recv_q = swap(query_rows)
    recv_g = swap(out_grad)
    own_kv, other_kv, half_kv = call(
        open_kernel, where, (key_rows, value_rows), [((BLOCK, PAIR), BF16)] * 3
    )
    recv_q, recv_g, own_kv, other_kv, half_kv = lax.optimization_barrier(
        (recv_q, recv_g, own_kv, other_kv, half_kv)
    )
    fine_cross = swap(fetch(other_kv, "fine_same"))
    half_same = fetch(half_kv, "half_same")
    half_cross = swap(half_same)
    fine_same = fetch(own_kv, "fine_same")
    recv_kv = swap(other_kv)
    near = (fine_same, fine_cross, half_same, half_cross)
    same2, cross2, other2, quad3 = call(
        coarse_kernel, where, (own_kv, recv_kv, *near), [((64, PAIR), BF16)] * 4
    )
    z3 = fetch(quad3, "z3")
    s3 = fetch(quad3, "s3")
    s2 = fetch(other2, "far2")
    same2 = fetch(same2, "half_same")
    cross2 = fetch(cross2, "fine_same")
    x3 = fetch(z3, "x3")
    queries, grads, near_kv, weights, dprobs, stats, outputs = call(
        near_kernel,
        where,
        (query_rows, out_grad, recv_q, recv_g, own_kv, recv_kv, *near),
        [
            ((2 * BLOCK, HALF), BF16),
            ((2 * BLOCK, HALF), BF16),
            ((768, PAIR), BF16),
            ((4 * NEAR, 2 * BLOCK), F32),
            ((4 * NEAR, 2 * BLOCK), F32),
            ((8, 2 * BLOCK), F32),
            ((4 * HEAD, 2 * BLOCK), F32),
        ],
    )
    far = (same2, cross2, s2, z3, x3, s3)
    output, scales, dscores, gm2, gp2, gs2, gz3, gx3, gs3 = call(
        main_kernel,
        where,
        (queries, grads, outputs, stats, *far),
        [
            ((2 * BLOCK, HALF), F32),
            ((8, 2 * BLOCK), F32),
            ((4 * FAR, 2 * BLOCK), BF16),
        ]
        + [((64, PAIR), BF16)] * 6,
        scratch=[pltpu.VMEM((FAR, PAIR), BF16)],
    )
    back_s3 = give(gs3, "s3")
    gz3, gs2, gp2, scales = lax.optimization_barrier((gz3 + give(gx3, "x3"), gs2, gp2, scales))
    back_z3 = give(gz3, "z3")
    back_s2 = give(gs2, "far2")
    back_m2 = give(gm2, "half_same")
    back_p2 = give(gp2, "fine_same")
    keep, send, grad_below, grad_above = call(
        rest_kernel,
        where,
        (queries, grads, near_kv, weights, dprobs, scales, dscores, output, *far),
        [
            ((BLOCK, 2 * PAIR), F32),
            ((BLOCK, 2 * PAIR), F32),
            ((192, PAIR), BF16),
            ((192, PAIR), BF16),
        ],
        scratch=[pltpu.VMEM((2 * BLOCK, 2 * PAIR), F32)],
    )
    fine_same, fine_cross, half_same, half_cross, keep3, send3 = call(
        fold_kernel,
        where,
        (grad_below, grad_above, back_s3, back_z3, back_m2, back_p2, back_s2),
        [((BLOCK, PAIR), BF16)] * 2
        + [((BLOCK // 2, PAIR), BF16)] * 2
        + [((16, PAIR), BF16)] * 2,
    )
    fine_cross = swap(give(fine_cross, "half_same"))
    half_cross = swap(give(half_cross, "fine_same"))
    fine_same = give(fine_same, "fine_same")
    half_same = give(half_same, "half_same")
    send, send3 = lax.optimization_barrier((send, send3))
    recv3 = swap(send3)
    recv = swap(send)
    attended, query_grad = call(
        join_kernel, where, (keep, recv), [((BLOCK, PAIR), BF16), ((BLOCK, PAIR), F32)]
    )
    attended, query_grad, keep3 = lax.optimization_barrier((attended, query_grad, keep3))
    key_grad, value_grad = call(
        final_kernel,
        where,
        (keep, recv, keep3, recv3, fine_same, fine_cross, half_same, half_cross),
        [((BLOCK, PAIR), F32)] * 2,
        scratch=[pltpu.VMEM((2, BLOCK, PAIR), F32), pltpu.SemaphoreType.DMA((4,))],
        space=pl.ANY,
    )
    return attended, query_grad, key_grad, value_grad


def solution(mesh):
    spec = P(AXES, None)
    return jax.shard_map(
        on_device, mesh=mesh, in_specs=(spec,) * 4, out_specs=(spec,) * 4, check_vma=False
    )
```

```python
import math

import jax
import jax.numpy as jnp
from jax import lax
from jax.experimental import pallas as pl
from jax.experimental.pallas import tpu as pltpu
from jax.sharding import PartitionSpec as P

HEADS = 8
HEAD = 128
LEVELS = 3
BLOCK = 128
HALF = 512
PAIR = 1024
ROW = 8
AXES = ("outer", "seq")
NEGATIVE = -1e30
FACTOR = 1.0 / math.sqrt(HEAD)
FACTOR2 = FACTOR / math.log(2.0)
BF16 = jnp.bfloat16
F32 = jnp.float32


def dot(a, b, dims=((1,), (0,))):
    return lax.dot_general(a, b, (dims, ((), ())), preferred_element_type=F32)


def pool_matrix(rows, columns, span):
    i = lax.broadcasted_iota(jnp.int32, (rows, columns), 0)
    j = lax.broadcasted_iota(jnp.int32, (rows, columns), 1)
    return jnp.where(j // span == i, 1.0 / span, 0.0).astype(BF16)


def spread_matrix(rows, columns, span):
    i = lax.broadcasted_iota(jnp.int32, (rows, columns), 0)
    j = lax.broadcasted_iota(jnp.int32, (rows, columns), 1)
    return jnp.where(i // span == j, 1.0 / span, 0.0).astype(BF16)


def half_columns(core):
    return pl.ds(pl.multiple_of(core * HALF, HALF), HALF)


def block_at(core):
    return pl.ds(pl.multiple_of(core * BLOCK, BLOCK), BLOCK)


def open_kernel(where, k, v, own, other, coarse):
    core = where[0] % 2
    halve = pool_matrix(64, BLOCK, 2)
    for n, half, fine in ((1, 1 - core, other), (0, core, own)):
        columns = half_columns(half)
        fine[:, 0:512] = k[:, columns]
        fine[:, 512:1024] = v[:, columns]
        coarse[64 * n : 64 * n + 64] = dot(halve, fine[...]).astype(BF16)


def sides(first, own, recv, fine_same, fine_cross, half_same, half_cross):
    def pick(a, b):
        return jnp.where(first, a[...], b[...])

    return (
        pick(own, recv),
        pick(recv, own),
        pick(fine_cross, fine_same),
        pick(fine_same, fine_cross),
        pick(half_same[0:64], half_cross[64:128]),
        pick(half_cross[64:128], half_same[0:64]),
    )


def coarse_kernel(
    where, own, recv, fine_same, fine_cross, half_same, half_cross, same2, cross2, other2, quad3
):
    even = (where[0] // 2) % 2 == 0
    first = where[0] % 2 == 0
    fine = jnp.concatenate([pool_matrix(32, BLOCK, 4), pool_matrix(16, BLOCK, 8)], axis=0)
    half = jnp.concatenate([pool_matrix(32, 64, 2), pool_matrix(16, 64, 4)], axis=0)
    eighth = pool_matrix(16, BLOCK, 8)
    pooled = [
        dot(eighth, own[...]),
        dot(eighth, recv[...]),
        dot(fine, fine_same[...]),
        dot(fine, fine_cross[...]),
        dot(half, half_same[0:64]),
        dot(half, half_cross[64:128]),
    ]
    mine, other, same, cross, part_same, part_cross = [x.astype(BF16) for x in pooled]
    own_low, own_high = jnp.where(first, mine, other), jnp.where(first, other, mine)
    below_high, above_low = jnp.where(first, cross, same), jnp.where(first, same, cross)
    below_low = jnp.where(first, part_same, part_cross)
    above_high = jnp.where(first, part_cross, part_same)
    b2 = jnp.concatenate([below_low[0:32], below_high[0:32]], axis=0)
    a2 = jnp.concatenate([above_low[0:32], above_high[0:32]], axis=0)
    same2[...] = jnp.where(first, b2, a2)
    cross2[...] = jnp.where(first, a2, b2)
    other2[...] = jnp.where(even, a2, b2)
    own3 = jnp.concatenate([own_low, own_high], axis=0)
    b3 = jnp.concatenate([below_low[32:48], below_high[32:48]], axis=0)
    a3 = jnp.concatenate([above_low[32:48], above_high[32:48]], axis=0)
    quad3[0:32] = jnp.where(even, own3, b3)
    quad3[32:64] = jnp.where(even, a3, own3)


NEAR = 576
FAR = 384
NT = ((1,), (1,))
TN = ((0,), (0,))


def bias(valid, level):
    return jnp.where(valid, F32(level), F32(NEGATIVE))


def row_bias(pieces):
    return jnp.concatenate([jnp.full((rows, 1), value, F32) for rows, value in pieces], axis=0)


def columns_of(h):
    return (
        slice(h * HEAD, (h + 1) * HEAD),
        slice(HALF + h * HEAD, HALF + (h + 1) * HEAD),
    )


def back(weight, near, columns):
    edges = jnp.concatenate(
        [
            dot(near[384:576, columns], weight[384:576, 0:128], TN),
            dot(near[576:768, columns], weight[384:576, 128:256], TN),
        ],
        axis=1,
    )
    return dot(near[0:384, columns], weight[0:384], TN) + edges


def near_kernel(
    where, q, g, recv_q, recv_g, own_kv, recv_kv, fine_same, fine_cross, half_same, half_cross,
    queries, grads, keyvals, weights, dprobs, stats, outputs,
):
    chips = where[1] // 2
    core = where[0] % 2
    chip = where[0] // 2
    mine = half_columns(core)
    queries[block_at(core), :] = q[:, mine]
    queries[block_at(1 - core), :] = recv_q[:, mine]
    grads[block_at(core), :] = g[:, mine]
    grads[block_at(1 - core), :] = recv_g[:, mine]
    low, high, fine_below, fine_above, half_below, half_above = sides(
        core == 0, own_kv, recv_kv, fine_same, fine_cross, half_same, half_cross
    )
    halve = pool_matrix(64, BLOCK, 2)
    keyvals[0:128] = low
    keyvals[128:256] = high
    keyvals[256:320] = half_below
    keyvals[320:384] = half_above
    keyvals[384:512] = fine_below
    keyvals[512:576] = dot(halve, fine_above).astype(BF16)
    keyvals[576:704] = fine_above
    keyvals[704:768] = dot(halve, fine_below).astype(BF16)
    has_below = chip >= 1
    has_above = chip < chips - 1
    side = lax.broadcasted_iota(jnp.int32, (1, 256), 1) < 128
    fine_bias = jnp.where(side, bias(has_below, 0), bias(has_above, 0))
    half_bias = jnp.where(side, bias(has_above, 1), bias(has_below, 1))
    rows_bias = row_bias(((256, F32(0.0)), (64, bias(has_below, 1)), (64, bias(has_above, 1))))

    def product(columns, rows):
        shared = dot(keyvals[0:384, columns], rows, NT)
        edges = jnp.concatenate(
            [
                dot(keyvals[384:576, columns], rows[0:128], NT),
                dot(keyvals[576:768, columns], rows[128:256], NT),
            ],
            axis=1,
        )
        return shared, edges

    for h in range(4):
        kc, vc = columns_of(h)
        at = NEAR * h
        shared, edges = product(kc, queries[:, kc])
        scores = jnp.concatenate(
            [
                shared * FACTOR2 + rows_bias,
                edges[0:128] * FACTOR2 + fine_bias,
                edges[128:192] * FACTOR2 + half_bias,
            ],
            axis=0,
        )
        highest = jnp.max(scores, axis=0, keepdims=True)
        weight = jnp.exp2(scores - highest)
        weights[at : at + NEAR] = weight
        stats[h : h + 1] = highest
        stats[4 + h : 5 + h] = jnp.sum(weight, axis=0, keepdims=True)
        outputs[HEAD * h : HEAD * h + HEAD] = back(weight.astype(BF16), keyvals, vc)
        shared, edges = product(vc, grads[:, kc])
        dprobs[at : at + 384] = shared
        dprobs[at + 384 : at + NEAR] = edges


def main_kernel(
    where, queries, grads, outputs, stats, m2, p2, s2, z3, x3, s3,
    output, scales, dscores, gm2, gp2, gs2, gz3, gx3, gs3,
    far,
):
    chips = where[1] // 2
    core = where[0] % 2
    chip = where[0] // 2
    quad = chip // 2
    for n, piece in enumerate((m2, p2, s2, z3, x3, s3)):
        far[64 * n : 64 * n + 64] = piece[...]
    far2 = jnp.where(chip % 2 == 0, chip + 3, chip - 3)
    far3 = jnp.where(quad % 2 == 0, quad + 3, quad - 3)
    quads = chips // 2
    rows_bias = row_bias(
        (
            (64, bias(jnp.where(core == 0, chip >= 2, chip + 2 < chips), 2)),
            (64, bias(jnp.where(core == 0, chip + 2 < chips, chip >= 2), 2)),
            (64, bias((far2 >= 0) & (far2 < chips), 2)),
            (64, F32(3)),
            (64, bias(jnp.where(chip % ROW < ROW // 2, chip >= ROW, chip + ROW < chips), 3)),
            (64, bias((far3 >= 0) & (far3 < quads), 3)),
        )
    )
    heads = [columns_of(h) for h in range(4)]
    scores = [dot(far[:, kc], queries[:, kc], NT) * FACTOR2 + rows_bias for kc, _ in heads]
    dprobs = [dot(far[:, vc], grads[:, kc], NT) for kc, vc in heads]
    probs = []
    for h in range(4):
        before = stats[h : h + 1]
        highest = jnp.maximum(before, jnp.max(scores[h], axis=0, keepdims=True))
        weight = jnp.exp2(scores[h] - highest)
        shrink = jnp.exp2(before - highest)
        total = stats[4 + h : 5 + h] * shrink + jnp.sum(weight, axis=0, keepdims=True)
        inverse = 1.0 / total
        scales[h : h + 1] = shrink * inverse
        probs.append(weight * inverse)
    lows = [p.astype(BF16) for p in probs]
    attended = [
        outputs[HEAD * h : HEAD * h + HEAD] * scales[h : h + 1] + dot(far[:, vc], lows[h], TN)
        for h, (_, vc) in enumerate(heads)
    ]
    terms_v = [dot(lows[h], grads[:, kc]).astype(BF16) for h, (kc, _) in enumerate(heads)]
    terms_k = []
    for h, (kc, _) in enumerate(heads):
        delta = jnp.sum(grads[:, kc].astype(F32).T * attended[h], axis=0, keepdims=True)
        scales[4 + h : 5 + h] = delta
        dscore = (probs[h] * (dprobs[h] - delta)).astype(BF16)
        dscores[FAR * h : FAR * h + FAR] = dscore
        terms_k.append((dot(dscore, queries[:, kc]) * FACTOR).astype(BF16))
    for h, (kc, vc) in enumerate(heads):
        output[:, kc] = attended[h].T
        for n, piece in enumerate((gm2, gp2, gs2, gz3, gx3, gs3)):
            piece[:, kc] = terms_k[h][64 * n : 64 * n + 64]
            piece[:, vc] = terms_v[h][64 * n : 64 * n + 64]


def rest_kernel(
    where, queries, grads, near, weights, dprobs, scales, dscores, output,
    m2, p2, s2, z3, x3, s3,
    keep, send, grad_below, grad_above,
    outs,
):
    core = where[0] % 2
    spread = spread_matrix(BLOCK, 64, 2)
    for h in range(4):
        kc, vc = columns_of(h)
        at = NEAR * h
        probs = weights[at : at + NEAR] * scales[h : h + 1]
        low = probs.astype(BF16)
        dscore = (probs * (dprobs[at : at + NEAR] - scales[4 + h : 5 + h])).astype(BF16)
        far = jnp.concatenate([piece[:, kc] for piece in (m2, p2, s2, z3, x3, s3)], axis=0)
        query_grad = back(dscore, near, kc) + dot(far, dscores[FAR * h : FAR * h + FAR], TN)
        outs[:, kc] = output[:, kc]
        outs[:, vc] = query_grad.T * FACTOR
        for columns, weight, rows, scale in (
            (kc, dscore, queries[:, kc], FACTOR),
            (vc, low, grads[:, kc], 1.0),
        ):
            shared = dot(weight[0:384], rows) * scale
            part_a = dot(weight[384:576, 0:128], rows[0:128]) * scale
            part_b = dot(weight[384:576, 128:256], rows[128:256]) * scale
            outs[:, PAIR + columns.start : PAIR + columns.stop] = shared[0:256]
            terms = shared[256:384].astype(BF16)
            grad_below[0:128, columns] = (
                part_a[0:128] + dot(spread, part_b[128:192].astype(BF16))
            ).astype(BF16)
            grad_below[128:192, columns] = terms[0:64]
            grad_above[0:128, columns] = (
                part_b[0:128] + dot(spread, part_a[128:192].astype(BF16))
            ).astype(BF16)
            grad_above[128:192, columns] = terms[64:128]
    keep[...] = outs[block_at(core), :]
    send[...] = outs[block_at(1 - core), :]


def fold_kernel(
    where, grad_below, grad_above, s3, z3, same2, cross2, other2,
    out_same, out_cross, half_same, half_cross, keep3, send3,
):
    even = (where[0] // 2) % 2 == 0

    def weigh(matrix, use):
        return jnp.where(use, matrix, jnp.zeros_like(matrix))

    def fold(base, pieces2, rows, use, fine, half):
        def rows_of(n):
            return jnp.concatenate(
                [piece[32 * n : 32 * n + 32] for piece in (pieces2, other2)]
                + [piece[rows + 16 * n : rows + 16 * n + 16] for piece in (z3, s3)],
                axis=0,
            )

        fine_matrix = jnp.concatenate(
            [spread_matrix(128, 32, 4), weigh(spread_matrix(128, 32, 4), use)]
            + [weigh(spread_matrix(128, 16, 8), use)] * 2,
            axis=1,
        )
        half_matrix = jnp.concatenate(
            [spread_matrix(64, 32, 2), weigh(spread_matrix(64, 32, 2), use)]
            + [weigh(spread_matrix(64, 16, 4), use)] * 2,
            axis=1,
        )
        return (
            (base[0:128].astype(F32) + dot(fine_matrix, rows_of(fine))).astype(BF16),
            (base[128:192].astype(F32) + dot(half_matrix, rows_of(half))).astype(BF16),
        )

    first = where[0] % 2 == 0
    from2 = jnp.where(first, same2[...], cross2[...])
    to2 = jnp.where(first, cross2[...], same2[...])
    fine_below, half_below = fold(grad_below, from2, 0, jnp.logical_not(even), 1, 0)
    fine_above, half_above = fold(grad_above, to2, 32, even, 0, 1)
    out_same[...] = jnp.where(first, fine_above, fine_below)
    out_cross[...] = jnp.where(first, fine_below, fine_above)
    half_same[...] = jnp.where(first, half_below, half_above)
    half_cross[...] = jnp.where(first, half_above, half_below)
    row = pl.multiple_of((where[0] // 2) % 2 * 32, 32)
    own3 = (z3[pl.ds(row, 32), :].astype(F32) + s3[pl.ds(row, 32), :].astype(F32)).astype(BF16)
    keep3[...] = jnp.where(first, own3[0:16], own3[16:32])
    send3[...] = jnp.where(first, own3[16:32], own3[0:16])


def join_kernel(where, out_keep, out_recv, attended, qg):
    core = where[0] % 2
    mine = half_columns(core)
    other = half_columns(1 - core)
    attended[:, mine] = out_keep[:, 0:512].astype(BF16)
    attended[:, other] = out_recv[:, 0:512].astype(BF16)
    qg[:, mine] = out_keep[:, 512:1024]
    qg[:, other] = out_recv[:, 512:1024]


def write_columns(where, turn, own, fine, half, last, kg, vg, total, sems):
    side = (where[0] + turn) % 2
    matrix = jnp.concatenate([spread_matrix(BLOCK, 64, 2), spread_matrix(BLOCK, 16, 8)], axis=1)
    coarse = jnp.concatenate([half[...], last[...]], axis=0)
    copies = []
    for m, target in enumerate((kg, vg)):
        columns = slice(HALF * m, HALF * (m + 1))
        total[:, columns] = (
            own[:, PAIR + HALF * m : PAIR + HALF * (m + 1)]
            + fine[:, columns].astype(F32)
            + dot(matrix, coarse[:, columns])
        )
        copies.append(
            pltpu.make_async_copy(
                total.at[:, columns], target.at[:, half_columns(side)], sems.at[m]
            )
        )
        copies[-1].start()
    for copy in copies:
        copy.wait()


def final_same_kernel(where, own, fine, half, last, kg, vg, total, sems):
    write_columns(where, 0, own, fine, half, last, kg, vg, total, sems)


def final_cross_kernel(where, own, fine, half, last, kg_in, vg_in, kg, vg, total, sems):
    write_columns(where, 1, own, fine, half, last, kg, vg, total, sems)


def call(kernel, where, args, outs, scratch=(), space=pltpu.VMEM, into=()):
    return pl.pallas_call(
        kernel,
        out_shape=[jax.ShapeDtypeStruct(shape, dtype) for shape, dtype in outs],
        in_specs=[pl.BlockSpec(memory_space=pltpu.SMEM)]
        + [pl.BlockSpec(memory_space=pltpu.VMEM)] * len(args)
        + [pl.BlockSpec(memory_space=pl.ANY)] * len(into),
        out_specs=[pl.BlockSpec(memory_space=space)] * len(outs),
        scratch_shapes=list(scratch),
        compiler_params=pltpu.CompilerParams(vmem_limit_bytes=32 * 1024 * 1024),
        input_output_aliases={1 + len(args) + n: n for n in range(len(into))},
    )(where, *args, *into)


def sources(chips):
    def opposite(p):
        turn = ROW // 2 + 1 if p % 2 == 0 else ROW // 2 - 1
        return p - p % ROW + (p + turn) % ROW

    near = {
        "fine_same": lambda p, c: (p - 1, 1) if c == 1 else (p + 1, 0),
        "half_same": lambda p, c: (p - 1, 0) if c == 0 else (p + 1, 1),
        "far2": lambda p, c: (p + 2 if p % 2 == 0 else p - 2, c),
        "z3": lambda p, c: (opposite(p), c),
        "x3": lambda p, c: (p - ROW if p % ROW < ROW // 2 else p + ROW, c),
        "s3": lambda p, c: (p + 6 if p // 2 % 2 == 0 else p - 6, c),
    }
    closing = {
        "fine_same": lambda p, c: (p, 1 - c),
        "half_same": lambda p, c: (p, 1 - c),
        "far2": lambda p, c: (p ^ 1, c),
        "x3": lambda p, c: (p - p % ROW + ROW - 1 - p % ROW, c),
        "s3": lambda p, c: (p ^ 1, c),
    }

    def source(name, p, c):
        found = near[name](p, c)
        return found if 0 <= found[0] < chips else closing[name](p, c)

    return source


def on_device(query_rows, key_rows, value_rows, out_grad):
    position = lax.axis_index(AXES)
    devices = lax.axis_size(AXES)
    chips = devices // 2
    plan = sources(chips)
    where = jnp.stack([position, jnp.int32(devices)]).astype(jnp.int32)

    def swap(x):
        return lax.ppermute(x, AXES, [(i, i ^ 1) for i in range(devices)])

    def pairs(name):
        found = []
        for chip in range(chips):
            for core in range(2):
                source, side = plan(name, chip, core)
                found.append((2 * source + side, 2 * chip + core))
        return found

    def fetch(x, name):
        return lax.ppermute(x, AXES, pairs(name))

    def give(x, name):
        return lax.ppermute(x, AXES, [(b, a) for a, b in pairs(name)])

    recv_q = swap(query_rows)
    recv_g = swap(out_grad)
    own_kv, other_kv, half_kv = call(
        open_kernel, where, (key_rows, value_rows), [((BLOCK, PAIR), BF16)] * 3
    )
    recv_q, recv_g, own_kv, other_kv, half_kv = lax.optimization_barrier(
        (recv_q, recv_g, own_kv, other_kv, half_kv)
    )
    fine_cross = swap(fetch(other_kv, "fine_same"))
    half_same = fetch(half_kv, "half_same")
    half_cross = swap(half_same)
    fine_same = fetch(own_kv, "fine_same")
    recv_kv = swap(other_kv)
    near = (fine_same, fine_cross, half_same, half_cross)
    same2, cross2, other2, quad3 = call(
        coarse_kernel, where, (own_kv, recv_kv, *near), [((64, PAIR), BF16)] * 4
    )
    z3 = fetch(quad3, "z3")
    s3 = fetch(quad3, "s3")
    s2 = fetch(other2, "far2")
    same2 = fetch(same2, "half_same")
    cross2 = fetch(cross2, "fine_same")
    x3 = fetch(z3, "x3")
    queries, grads, near_kv, weights, dprobs, stats, outputs = call(
        near_kernel,
        where,
        (query_rows, out_grad, recv_q, recv_g, own_kv, recv_kv, *near),
        [
            ((2 * BLOCK, HALF), BF16),
            ((2 * BLOCK, HALF), BF16),
            ((768, PAIR), BF16),
            ((4 * NEAR, 2 * BLOCK), F32),
            ((4 * NEAR, 2 * BLOCK), F32),
            ((8, 2 * BLOCK), F32),
            ((4 * HEAD, 2 * BLOCK), F32),
        ],
    )
    far = (same2, cross2, s2, z3, x3, s3)
    output, scales, dscores, gm2, gp2, gs2, gz3, gx3, gs3 = call(
        main_kernel,
        where,
        (queries, grads, outputs, stats, *far),
        [
            ((2 * BLOCK, HALF), F32),
            ((8, 2 * BLOCK), F32),
            ((4 * FAR, 2 * BLOCK), BF16),
        ]
        + [((64, PAIR), BF16)] * 6,
        scratch=[pltpu.VMEM((FAR, PAIR), BF16)],
    )
    back_s3 = give(gs3, "s3")
    gz3, gs2, gp2, scales = lax.optimization_barrier((gz3 + give(gx3, "x3"), gs2, gp2, scales))
    back_z3 = give(gz3, "z3")
    back_s2 = give(gs2, "far2")
    back_m2 = give(gm2, "half_same")
    back_p2 = give(gp2, "fine_same")
    keep, send, grad_below, grad_above = call(
        rest_kernel,
        where,
        (queries, grads, near_kv, weights, dprobs, scales, dscores, output, *far),
        [
            ((BLOCK, 2 * PAIR), F32),
            ((BLOCK, 2 * PAIR), F32),
            ((192, PAIR), BF16),
            ((192, PAIR), BF16),
        ],
        scratch=[pltpu.VMEM((2 * BLOCK, 2 * PAIR), F32)],
    )
    fine_same, fine_cross, half_same, half_cross, keep3, send3 = call(
        fold_kernel,
        where,
        (grad_below, grad_above, back_s3, back_z3, back_m2, back_p2, back_s2),
        [((BLOCK, PAIR), BF16)] * 2
        + [((BLOCK // 2, PAIR), BF16)] * 2
        + [((16, PAIR), BF16)] * 2,
    )
    fine_same = give(fine_same, "fine_same")
    fine_cross = give(swap(fine_cross), "fine_same")
    half_same = give(half_same, "half_same")
    half_cross = give(swap(half_cross), "half_same")
    send, send3 = lax.optimization_barrier((send, send3))
    recv3 = swap(send3)
    recv = swap(send)
    attended, query_grad = call(
        join_kernel, where, (keep, recv), [((BLOCK, PAIR), BF16), ((BLOCK, PAIR), F32)]
    )
    attended, query_grad, keep3 = lax.optimization_barrier((attended, query_grad, keep3))
    work = [pltpu.VMEM((BLOCK, PAIR), F32), pltpu.SemaphoreType.DMA((2,))]
    written = call(
        final_same_kernel,
        where,
        (keep, fine_same, half_same, keep3),
        [((BLOCK, PAIR), F32)] * 2,
        scratch=work,
        space=pl.ANY,
    )
    key_grad, value_grad = call(
        final_cross_kernel,
        where,
        (recv, fine_cross, half_cross, recv3),
        [((BLOCK, PAIR), F32)] * 2,
        scratch=work,
        space=pl.ANY,
        into=written,
    )
    return attended, query_grad, key_grad, value_grad


def solution(mesh):
    spec = P(AXES, None)
    return jax.shard_map(
        on_device, mesh=mesh, in_specs=(spec,) * 4, out_specs=(spec,) * 4, check_vma=False
    )
```

```python
import math

import jax
import jax.numpy as jnp
from jax import lax
from jax.experimental import pallas as pl
from jax.experimental.pallas import tpu as pltpu
from jax.sharding import PartitionSpec as P

HEADS = 8
HEAD = 128
LEVELS = 3
BLOCK = 128
HALF = 512
PAIR = 1024
ROW = 8
AXES = ("outer", "seq")
NEGATIVE = -1e30
FACTOR = 1.0 / math.sqrt(HEAD)
FACTOR2 = FACTOR / math.log(2.0)
BF16 = jnp.bfloat16
F32 = jnp.float32


def dot(a, b, dims=((1,), (0,))):
    return lax.dot_general(a, b, (dims, ((), ())), preferred_element_type=F32)


def pool_matrix(rows, columns, span):
    i = lax.broadcasted_iota(jnp.int32, (rows, columns), 0)
    j = lax.broadcasted_iota(jnp.int32, (rows, columns), 1)
    return jnp.where(j // span == i, 1.0 / span, 0.0).astype(BF16)


def spread_matrix(rows, columns, span):
    i = lax.broadcasted_iota(jnp.int32, (rows, columns), 0)
    j = lax.broadcasted_iota(jnp.int32, (rows, columns), 1)
    return jnp.where(i // span == j, 1.0 / span, 0.0).astype(BF16)


def half_columns(core):
    return pl.ds(pl.multiple_of(core * HALF, HALF), HALF)


def block_at(core):
    return pl.ds(pl.multiple_of(core * BLOCK, BLOCK), BLOCK)


def open_kernel(where, k, v, own, other, coarse):
    core = where[0] % 2
    halve = pool_matrix(64, BLOCK, 2)
    for n, half, fine in ((1, 1 - core, other), (0, core, own)):
        columns = half_columns(half)
        fine[:, 0:512] = k[:, columns]
        fine[:, 512:1024] = v[:, columns]
        coarse[64 * n : 64 * n + 64] = dot(halve, fine[...]).astype(BF16)


def sides(first, own, recv, fine_same, fine_cross, half_same, half_cross):
    def pick(a, b):
        return jnp.where(first, a[...], b[...])

    return (
        pick(own, recv),
        pick(recv, own),
        pick(fine_cross, fine_same),
        pick(fine_same, fine_cross),
        pick(half_same[0:64], half_cross[64:128]),
        pick(half_cross[64:128], half_same[0:64]),
    )


def coarse_kernel(
    where, own, recv, fine_same, fine_cross, half_same, half_cross, cross2, pair2, quad3
):
    even = (where[0] // 2) % 2 == 0
    first = where[0] % 2 == 0
    low, high, fine_below, fine_above, half_below, half_above = sides(
        first, own, recv, fine_same, fine_cross, half_same, half_cross
    )
    fine = jnp.concatenate([pool_matrix(32, BLOCK, 4), pool_matrix(16, BLOCK, 8)], axis=0)
    half = jnp.concatenate([pool_matrix(32, 64, 2), pool_matrix(16, 64, 4)], axis=0)
    own_low = dot(fine[32:48], low).astype(BF16)
    own_high = dot(fine[32:48], high).astype(BF16)
    below_low = dot(half, half_below).astype(BF16)
    below_high = dot(fine, fine_below).astype(BF16)
    above_low = dot(fine, fine_above).astype(BF16)
    above_high = dot(half, half_above).astype(BF16)
    b2 = jnp.concatenate([below_low[0:32], below_high[0:32]], axis=0)
    a2 = jnp.concatenate([above_low[0:32], above_high[0:32]], axis=0)
    cross2[...] = jnp.where(even, a2, b2)
    pair2[...] = jnp.where(even, b2, a2)
    own3 = jnp.concatenate([own_low, own_high], axis=0)
    b3 = jnp.concatenate([below_low[32:48], below_high[32:48]], axis=0)
    a3 = jnp.concatenate([above_low[32:48], above_high[32:48]], axis=0)
    quad3[0:32] = jnp.where(even, own3, b3)
    quad3[32:64] = jnp.where(even, a3, own3)


NEAR = 576
FAR = 384
NT = ((1,), (1,))
TN = ((0,), (0,))


def bias(valid, level):
    return jnp.where(valid, F32(level), F32(NEGATIVE))


def row_bias(pieces):
    return jnp.concatenate([jnp.full((rows, 1), value, F32) for rows, value in pieces], axis=0)


def columns_of(h):
    return (
        slice(h * HEAD, (h + 1) * HEAD),
        slice(HALF + h * HEAD, HALF + (h + 1) * HEAD),
    )


def back(weight, near, columns):
    edges = jnp.concatenate(
        [
            dot(near[384:576, columns], weight[384:576, 0:128], TN),
            dot(near[576:768, columns], weight[384:576, 128:256], TN),
        ],
        axis=1,
    )
    return dot(near[0:384, columns], weight[0:384], TN) + edges


def near_kernel(
    where, q, g, recv_q, recv_g, own_kv, recv_kv, fine_same, fine_cross, half_same, half_cross,
    queries, grads, keyvals, weights, dprobs, stats, outputs,
):
    chips = where[1] // 2
    core = where[0] % 2
    chip = where[0] // 2
    mine = half_columns(core)
    queries[block_at(core), :] = q[:, mine]
    queries[block_at(1 - core), :] = recv_q[:, mine]
    grads[block_at(core), :] = g[:, mine]
    grads[block_at(1 - core), :] = recv_g[:, mine]
    low, high, fine_below, fine_above, half_below, half_above = sides(
        core == 0, own_kv, recv_kv, fine_same, fine_cross, half_same, half_cross
    )
    halve = pool_matrix(64, BLOCK, 2)
    keyvals[0:128] = low
    keyvals[128:256] = high
    keyvals[256:320] = half_below
    keyvals[320:384] = half_above
    keyvals[384:512] = fine_below
    keyvals[512:576] = dot(halve, fine_above).astype(BF16)
    keyvals[576:704] = fine_above
    keyvals[704:768] = dot(halve, fine_below).astype(BF16)
    has_below = chip >= 1
    has_above = chip < chips - 1
    side = lax.broadcasted_iota(jnp.int32, (1, 256), 1) < 128
    fine_bias = jnp.where(side, bias(has_below, 0), bias(has_above, 0))
    half_bias = jnp.where(side, bias(has_above, 1), bias(has_below, 1))
    rows_bias = row_bias(((256, F32(0.0)), (64, bias(has_below, 1)), (64, bias(has_above, 1))))

    def product(columns, rows):
        shared = dot(keyvals[0:384, columns], rows, NT)
        edges = jnp.concatenate(
            [
                dot(keyvals[384:576, columns], rows[0:128], NT),
                dot(keyvals[576:768, columns], rows[128:256], NT),
            ],
            axis=1,
        )
        return shared, edges

    for h in range(4):
        kc, vc = columns_of(h)
        at = NEAR * h
        shared, edges = product(kc, queries[:, kc])
        scores = jnp.concatenate(
            [
                shared * FACTOR2 + rows_bias,
                edges[0:128] * FACTOR2 + fine_bias,
                edges[128:192] * FACTOR2 + half_bias,
            ],
            axis=0,
        )
        highest = jnp.max(scores, axis=0, keepdims=True)
        weight = jnp.exp2(scores - highest)
        weights[at : at + NEAR] = weight
        stats[h : h + 1] = highest
        stats[4 + h : 5 + h] = jnp.sum(weight, axis=0, keepdims=True)
        outputs[HEAD * h : HEAD * h + HEAD] = back(weight.astype(BF16), keyvals, vc)
        shared, edges = product(vc, grads[:, kc])
        dprobs[at : at + 384] = shared
        dprobs[at + 384 : at + NEAR] = edges


def main_kernel(
    where, queries, grads, outputs, stats, m2, p2, s2, z3, x3, s3,
    output, scales, dscores, gm2, gp2, gs2, gz3, gx3, gs3,
    far,
):
    chips = where[1] // 2
    chip = where[0] // 2
    quad = chip // 2
    for n, piece in enumerate((m2, p2, s2, z3, x3, s3)):
        far[64 * n : 64 * n + 64] = piece[...]
    far2 = jnp.where(chip % 2 == 0, chip + 3, chip - 3)
    far3 = jnp.where(quad % 2 == 0, quad + 3, quad - 3)
    quads = chips // 2
    rows_bias = row_bias(
        (
            (64, bias(jnp.where(chip % 2 == 0, chip >= 2, chip + 2 < chips), 2)),
            (64, bias(jnp.where(chip % 2 == 0, chip + 2 < chips, chip >= 2), 2)),
            (64, bias((far2 >= 0) & (far2 < chips), 2)),
            (64, F32(3)),
            (64, bias(jnp.where(chip % ROW < ROW // 2, chip >= ROW, chip + ROW < chips), 3)),
            (64, bias((far3 >= 0) & (far3 < quads), 3)),
        )
    )
    heads = [columns_of(h) for h in range(4)]
    scores = [dot(far[:, kc], queries[:, kc], NT) * FACTOR2 + rows_bias for kc, _ in heads]
    dprobs = [dot(far[:, vc], grads[:, kc], NT) for kc, vc in heads]
    probs = []
    for h in range(4):
        before = stats[h : h + 1]
        highest = jnp.maximum(before, jnp.max(scores[h], axis=0, keepdims=True))
        weight = jnp.exp2(scores[h] - highest)
        shrink = jnp.exp2(before - highest)
        total = stats[4 + h : 5 + h] * shrink + jnp.sum(weight, axis=0, keepdims=True)
        inverse = 1.0 / total
        scales[h : h + 1] = shrink * inverse
        probs.append(weight * inverse)
    lows = [p.astype(BF16) for p in probs]
    attended = [
        outputs[HEAD * h : HEAD * h + HEAD] * scales[h : h + 1] + dot(far[:, vc], lows[h], TN)
        for h, (_, vc) in enumerate(heads)
    ]
    terms_v = [dot(lows[h], grads[:, kc]).astype(BF16) for h, (kc, _) in enumerate(heads)]
    terms_k = []
    for h, (kc, _) in enumerate(heads):
        delta = jnp.sum(grads[:, kc].astype(F32).T * attended[h], axis=0, keepdims=True)
        scales[4 + h : 5 + h] = delta
        dscore = (probs[h] * (dprobs[h] - delta)).astype(BF16)
        dscores[FAR * h : FAR * h + FAR] = dscore
        terms_k.append((dot(dscore, queries[:, kc]) * FACTOR).astype(BF16))
    for h, (kc, vc) in enumerate(heads):
        output[:, kc] = attended[h].T
        for n, piece in enumerate((gm2, gp2, gs2, gz3, gx3, gs3)):
            piece[:, kc] = terms_k[h][64 * n : 64 * n + 64]
            piece[:, vc] = terms_v[h][64 * n : 64 * n + 64]


def rest_kernel(
    where, queries, grads, near, weights, dprobs, scales, dscores, output,
    m2, p2, s2, z3, x3, s3,
    keep, send, grad_below, grad_above,
    outs,
):
    core = where[0] % 2
    spread = spread_matrix(BLOCK, 64, 2)
    for h in range(4):
        kc, vc = columns_of(h)
        at = NEAR * h
        probs = weights[at : at + NEAR] * scales[h : h + 1]
        low = probs.astype(BF16)
        dscore = (probs * (dprobs[at : at + NEAR] - scales[4 + h : 5 + h])).astype(BF16)
        far = jnp.concatenate([piece[:, kc] for piece in (m2, p2, s2, z3, x3, s3)], axis=0)
        query_grad = back(dscore, near, kc) + dot(far, dscores[FAR * h : FAR * h + FAR], TN)
        outs[:, kc] = output[:, kc]
        outs[:, vc] = query_grad.T * FACTOR
        for columns, weight, rows, scale in (
            (kc, dscore, queries[:, kc], FACTOR),
            (vc, low, grads[:, kc], 1.0),
        ):
            shared = dot(weight[0:384], rows) * scale
            part_a = dot(weight[384:576, 0:128], rows[0:128]) * scale
            part_b = dot(weight[384:576, 128:256], rows[128:256]) * scale
            outs[:, PAIR + columns.start : PAIR + columns.stop] = shared[0:256]
            terms = shared[256:384].astype(BF16)
            grad_below[0:128, columns] = (
                part_a[0:128] + dot(spread, part_b[128:192].astype(BF16))
            ).astype(BF16)
            grad_below[128:192, columns] = terms[0:64]
            grad_above[0:128, columns] = (
                part_b[0:128] + dot(spread, part_a[128:192].astype(BF16))
            ).astype(BF16)
            grad_above[128:192, columns] = terms[64:128]
    keep[...] = outs[block_at(core), :]
    send[...] = outs[block_at(1 - core), :]


def fold_kernel(
    where, grad_below, grad_above, s3, z3, cross2, pair2,
    out_same, out_cross, half_same, half_cross, keep3, send3,
):
    even = (where[0] // 2) % 2 == 0

    def weigh(matrix, use):
        return jnp.where(use, matrix, jnp.zeros_like(matrix))

    def fold(base, pieces2, rows, use, fine, half):
        def rows_of(n):
            return jnp.concatenate(
                [pieces2[32 * n : 32 * n + 32]]
                + [piece[rows + 16 * n : rows + 16 * n + 16] for piece in (z3, s3)],
                axis=0,
            )

        fine_matrix = jnp.concatenate(
            [spread_matrix(128, 32, 4)]
            + [weigh(spread_matrix(128, 16, 8), use)] * 2,
            axis=1,
        )
        half_matrix = jnp.concatenate(
            [spread_matrix(64, 32, 2)]
            + [weigh(spread_matrix(64, 16, 4), use)] * 2,
            axis=1,
        )
        return (
            (base[0:128].astype(F32) + dot(fine_matrix, rows_of(fine))).astype(BF16),
            (base[128:192].astype(F32) + dot(half_matrix, rows_of(half))).astype(BF16),
        )

    first = where[0] % 2 == 0
    from2 = jnp.where(even, pair2[...], cross2[...])
    to2 = jnp.where(even, cross2[...], pair2[...])
    fine_below, half_below = fold(grad_below, from2, 0, jnp.logical_not(even), 1, 0)
    fine_above, half_above = fold(grad_above, to2, 32, even, 0, 1)
    out_same[...] = jnp.where(first, fine_above, fine_below)
    out_cross[...] = jnp.where(first, fine_below, fine_above)
    half_same[...] = jnp.where(first, half_below, half_above)
    half_cross[...] = jnp.where(first, half_above, half_below)
    row = pl.multiple_of((where[0] // 2) % 2 * 32, 32)
    own3 = (z3[pl.ds(row, 32), :].astype(F32) + s3[pl.ds(row, 32), :].astype(F32)).astype(BF16)
    keep3[...] = jnp.where(first, own3[0:16], own3[16:32])
    send3[...] = jnp.where(first, own3[16:32], own3[0:16])


def join_kernel(where, out_keep, out_recv, attended, qg):
    core = where[0] % 2
    mine = half_columns(core)
    other = half_columns(1 - core)
    attended[:, mine] = out_keep[:, 0:512].astype(BF16)
    attended[:, other] = out_recv[:, 0:512].astype(BF16)
    qg[:, mine] = out_keep[:, 512:1024]
    qg[:, other] = out_recv[:, 512:1024]


def final_kernel(
    where, keep, recv, keep3, recv3, fine_same, fine_cross, half_same, half_cross,
    kg, vg, total, sems,
):
    core = where[0] % 2
    matrix = jnp.concatenate([spread_matrix(BLOCK, 64, 2), spread_matrix(BLOCK, 16, 8)], axis=1)
    copies = []
    for n, (side, own, fine, half, last) in enumerate(
        (
            (core, keep, fine_same, half_same, keep3),
            (1 - core, recv, fine_cross, half_cross, recv3),
        )
    ):
        coarse = jnp.concatenate([half[...], last[...]], axis=0)
        total[n] = own[:, PAIR : 2 * PAIR] + fine[...].astype(F32) + dot(matrix, coarse)
        for m, target in enumerate((kg, vg)):
            copies.append(
                pltpu.make_async_copy(
                    total.at[n, :, HALF * m : HALF * (m + 1)],
                    target.at[:, half_columns(side)],
                    sems.at[2 * n + m],
                )
            )
            copies[-1].start()
    for copy in copies:
        copy.wait()


def call(kernel, where, args, outs, scratch=(), space=pltpu.VMEM):
    return pl.pallas_call(
        kernel,
        out_shape=[jax.ShapeDtypeStruct(shape, dtype) for shape, dtype in outs],
        in_specs=[pl.BlockSpec(memory_space=pltpu.SMEM)]
        + [pl.BlockSpec(memory_space=pltpu.VMEM)] * len(args),
        out_specs=[pl.BlockSpec(memory_space=space)] * len(outs),
        scratch_shapes=list(scratch),
        compiler_params=pltpu.CompilerParams(vmem_limit_bytes=32 * 1024 * 1024),
    )(where, *args)


def sources(chips):
    def opposite(p):
        turn = ROW // 2 + 1 if p % 2 == 0 else ROW // 2 - 1
        return p - p % ROW + (p + turn) % ROW

    near = {
        "fine_same": lambda p, c: (p - 1, 1) if c == 1 else (p + 1, 0),
        "half_same": lambda p, c: (p - 1, 0) if c == 0 else (p + 1, 1),
        "cross": lambda p, c: (p - 1 if p % 2 == 0 else p + 1, c),
        "pair": lambda p, c: (p ^ 1, c),
        "z3": lambda p, c: (opposite(p), c),
        "x3": lambda p, c: (p - ROW if p % ROW < ROW // 2 else p + ROW, c),
        "s3": lambda p, c: (p + 6 if p // 2 % 2 == 0 else p - 6, c),
    }
    closing = {
        "fine_same": lambda p, c: (p, 1 - c),
        "half_same": lambda p, c: (p, 1 - c),
        "cross": lambda p, c: (p, 1 - c),
        "x3": lambda p, c: (p - p % ROW + ROW - 1 - p % ROW, c),
        "s3": lambda p, c: (p ^ 1, c),
    }

    def source(name, p, c):
        found = near[name](p, c)
        return found if 0 <= found[0] < chips else closing[name](p, c)

    return source


def on_device(query_rows, key_rows, value_rows, out_grad):
    position = lax.axis_index(AXES)
    devices = lax.axis_size(AXES)
    chips = devices // 2
    plan = sources(chips)
    where = jnp.stack([position, jnp.int32(devices)]).astype(jnp.int32)

    def swap(x):
        return lax.ppermute(x, AXES, [(i, i ^ 1) for i in range(devices)])

    def pairs(name):
        found = []
        for chip in range(chips):
            for core in range(2):
                source, side = plan(name, chip, core)
                found.append((2 * source + side, 2 * chip + core))
        return found

    def fetch(x, name):
        return lax.ppermute(x, AXES, pairs(name))

    def give(x, name):
        return lax.ppermute(x, AXES, [(b, a) for a, b in pairs(name)])

    recv_q = swap(query_rows)
    recv_g = swap(out_grad)
    own_kv, other_kv, half_kv = call(
        open_kernel, where, (key_rows, value_rows), [((BLOCK, PAIR), BF16)] * 3
    )
    recv_q, recv_g, own_kv, other_kv, half_kv = lax.optimization_barrier(
        (recv_q, recv_g, own_kv, other_kv, half_kv)
    )
    fine_cross = swap(fetch(other_kv, "fine_same"))
    half_same = fetch(half_kv, "half_same")
    half_cross = swap(half_same)
    fine_same = fetch(own_kv, "fine_same")
    recv_kv = swap(other_kv)
    near = (fine_same, fine_cross, half_same, half_cross)
    cross2, pair2, quad3 = call(
        coarse_kernel, where, (own_kv, recv_kv, *near), [((64, PAIR), BF16)] * 3
    )
    z3 = fetch(quad3, "z3")
    s3 = fetch(quad3, "s3")
    c2 = fetch(cross2, "cross")
    b2 = fetch(pair2, "pair")
    f2 = fetch(c2, "pair")
    x3 = fetch(z3, "x3")
    queries, grads, near_kv, weights, dprobs, stats, outputs = call(
        near_kernel,
        where,
        (query_rows, out_grad, recv_q, recv_g, own_kv, recv_kv, *near),
        [
            ((2 * BLOCK, HALF), BF16),
            ((2 * BLOCK, HALF), BF16),
            ((768, PAIR), BF16),
            ((4 * NEAR, 2 * BLOCK), F32),
            ((4 * NEAR, 2 * BLOCK), F32),
            ((8, 2 * BLOCK), F32),
            ((4 * HEAD, 2 * BLOCK), F32),
        ],
    )
    far = (c2, b2, f2, z3, x3, s3)
    output, scales, dscores, gm2, gp2, gs2, gz3, gx3, gs3 = call(
        main_kernel,
        where,
        (queries, grads, outputs, stats, *far),
        [
            ((2 * BLOCK, HALF), F32),
            ((8, 2 * BLOCK), F32),
            ((4 * FAR, 2 * BLOCK), BF16),
        ]
        + [((64, PAIR), BF16)] * 6,
        scratch=[pltpu.VMEM((FAR, PAIR), BF16)],
    )
    back_s3 = give(gs3, "s3")
    gz3, shared, scales = lax.optimization_barrier(
        (gz3 + give(gx3, "x3"), fetch(gs2, "pair"), scales)
    )
    gm2 = gm2 + shared
    back_z3 = give(gz3, "z3")
    back_c2 = give(gm2, "cross")
    back_b2 = give(gp2, "pair")
    keep, send, grad_below, grad_above = call(
        rest_kernel,
        where,
        (queries, grads, near_kv, weights, dprobs, scales, dscores, output, *far),
        [
            ((BLOCK, 2 * PAIR), F32),
            ((BLOCK, 2 * PAIR), F32),
            ((192, PAIR), BF16),
            ((192, PAIR), BF16),
        ],
        scratch=[pltpu.VMEM((2 * BLOCK, 2 * PAIR), F32)],
    )
    fine_same, fine_cross, half_same, half_cross, keep3, send3 = call(
        fold_kernel,
        where,
        (grad_below, grad_above, back_s3, back_z3, back_c2, back_b2),
        [((BLOCK, PAIR), BF16)] * 2
        + [((BLOCK // 2, PAIR), BF16)] * 2
        + [((16, PAIR), BF16)] * 2,
    )
    fine_same = give(fine_same, "fine_same")
    fine_cross = give(swap(fine_cross), "fine_same")
    half_same = give(half_same, "half_same")
    half_cross = give(swap(half_cross), "half_same")
    send, send3 = lax.optimization_barrier((send, send3))
    recv3 = swap(send3)
    recv = swap(send)
    attended, query_grad = call(
        join_kernel, where, (keep, recv), [((BLOCK, PAIR), BF16), ((BLOCK, PAIR), F32)]
    )
    attended, query_grad, keep3 = lax.optimization_barrier((attended, query_grad, keep3))
    key_grad, value_grad = call(
        final_kernel,
        where,
        (keep, recv, keep3, recv3, fine_same, fine_cross, half_same, half_cross),
        [((BLOCK, PAIR), F32)] * 2,
        scratch=[pltpu.VMEM((2, BLOCK, PAIR), F32), pltpu.SemaphoreType.DMA((4,))],
        space=pl.ANY,
    )
    return attended, query_grad, key_grad, value_grad


def solution(mesh):
    spec = P(AXES, None)
    return jax.shard_map(
        on_device, mesh=mesh, in_specs=(spec,) * 4, out_specs=(spec,) * 4, check_vma=False
    )
```

```python
import math

import jax
import jax.numpy as jnp
from jax import lax
from jax.experimental import pallas as pl
from jax.experimental.pallas import tpu as pltpu
from jax.sharding import PartitionSpec as P

HEADS = 8
HEAD = 128
LEVELS = 3
BLOCK = 128
HALF = 512
PAIR = 1024
ROW = 8
AXES = ("outer", "seq")
NEGATIVE = -1e30
FACTOR = 1.0 / math.sqrt(HEAD)
FACTOR2 = FACTOR / math.log(2.0)
BF16 = jnp.bfloat16
F32 = jnp.float32


def dot(a, b, dims=((1,), (0,))):
    return lax.dot_general(a, b, (dims, ((), ())), preferred_element_type=F32)


def pool_matrix(rows, columns, span):
    i = lax.broadcasted_iota(jnp.int32, (rows, columns), 0)
    j = lax.broadcasted_iota(jnp.int32, (rows, columns), 1)
    return jnp.where(j // span == i, 1.0 / span, 0.0).astype(BF16)


def spread_matrix(rows, columns, span):
    i = lax.broadcasted_iota(jnp.int32, (rows, columns), 0)
    j = lax.broadcasted_iota(jnp.int32, (rows, columns), 1)
    return jnp.where(i // span == j, 1.0 / span, 0.0).astype(BF16)


def half_columns(core):
    return pl.ds(pl.multiple_of(core * HALF, HALF), HALF)


def block_at(core):
    return pl.ds(pl.multiple_of(core * BLOCK, BLOCK), BLOCK)


def open_kernel(where, k, v, own, other, coarse):
    core = where[0] % 2
    halve = pool_matrix(64, BLOCK, 2)
    for n, half, fine in ((1, 1 - core, other), (0, core, own)):
        columns = half_columns(half)
        fine[:, 0:512] = k[:, columns]
        fine[:, 512:1024] = v[:, columns]
        coarse[64 * n : 64 * n + 64] = dot(halve, fine[...]).astype(BF16)


def sides(first, own, recv, fine_same, fine_cross, half_same, half_cross):
    def pick(a, b):
        return jnp.where(first, a[...], b[...])

    return (
        pick(own, recv),
        pick(recv, own),
        pick(fine_cross, fine_same),
        pick(fine_same, fine_cross),
        pick(half_same[0:64], half_cross[64:128]),
        pick(half_cross[64:128], half_same[0:64]),
    )


def coarse_kernel(
    where, own, recv, fine_same, fine_cross, half_same, half_cross, cross2, pair2, quad3
):
    even = (where[0] // 2) % 2 == 0
    first = where[0] % 2 == 0
    low, high, fine_below, fine_above, half_below, half_above = sides(
        first, own, recv, fine_same, fine_cross, half_same, half_cross
    )
    fine = jnp.concatenate([pool_matrix(32, BLOCK, 4), pool_matrix(16, BLOCK, 8)], axis=0)
    half = jnp.concatenate([pool_matrix(32, 64, 2), pool_matrix(16, 64, 4)], axis=0)
    own_low = dot(fine[32:48], low).astype(BF16)
    own_high = dot(fine[32:48], high).astype(BF16)
    below_low = dot(half, half_below).astype(BF16)
    below_high = dot(fine, fine_below).astype(BF16)
    above_low = dot(fine, fine_above).astype(BF16)
    above_high = dot(half, half_above).astype(BF16)
    b2 = jnp.concatenate([below_low[0:32], below_high[0:32]], axis=0)
    a2 = jnp.concatenate([above_low[0:32], above_high[0:32]], axis=0)
    cross2[...] = jnp.where(even, a2, b2)
    pair2[...] = jnp.where(even, b2, a2)
    own3 = jnp.concatenate([own_low, own_high], axis=0)
    b3 = jnp.concatenate([below_low[32:48], below_high[32:48]], axis=0)
    a3 = jnp.concatenate([above_low[32:48], above_high[32:48]], axis=0)
    quad3[0:32] = jnp.where(even, own3, b3)
    quad3[32:64] = jnp.where(even, a3, own3)


NEAR = 576
FAR = 384
NT = ((1,), (1,))
TN = ((0,), (0,))


def bias(valid, level):
    return jnp.where(valid, F32(level), F32(NEGATIVE))


def row_bias(pieces):
    return jnp.concatenate([jnp.full((rows, 1), value, F32) for rows, value in pieces], axis=0)


def columns_of(h):
    return (
        slice(h * HEAD, (h + 1) * HEAD),
        slice(HALF + h * HEAD, HALF + (h + 1) * HEAD),
    )


def back(weight, near, columns):
    edges = jnp.concatenate(
        [
            dot(near[384:576, columns], weight[384:576, 0:128], TN),
            dot(near[576:768, columns], weight[384:576, 128:256], TN),
        ],
        axis=1,
    )
    return dot(near[0:384, columns], weight[0:384], TN) + edges


def near_kernel(
    where, q, g, recv_q, recv_g, own_kv, recv_kv, fine_same, fine_cross, half_same, half_cross,
    queries, grads, keyvals, weights, dprobs, stats, outputs,
):
    chips = where[1] // 2
    core = where[0] % 2
    chip = where[0] // 2
    mine = half_columns(core)
    queries[block_at(core), :] = q[:, mine]
    queries[block_at(1 - core), :] = recv_q[:, mine]
    grads[block_at(core), :] = g[:, mine]
    grads[block_at(1 - core), :] = recv_g[:, mine]
    low, high, fine_below, fine_above, half_below, half_above = sides(
        core == 0, own_kv, recv_kv, fine_same, fine_cross, half_same, half_cross
    )
    halve = pool_matrix(64, BLOCK, 2)
    keyvals[0:128] = low
    keyvals[128:256] = high
    keyvals[256:320] = half_below
    keyvals[320:384] = half_above
    keyvals[384:512] = fine_below
    keyvals[512:576] = dot(halve, fine_above).astype(BF16)
    keyvals[576:704] = fine_above
    keyvals[704:768] = dot(halve, fine_below).astype(BF16)
    has_below = chip >= 1
    has_above = chip < chips - 1
    side = lax.broadcasted_iota(jnp.int32, (1, 256), 1) < 128
    fine_bias = jnp.where(side, bias(has_below, 0), bias(has_above, 0))
    half_bias = jnp.where(side, bias(has_above, 1), bias(has_below, 1))
    rows_bias = row_bias(((256, F32(0.0)), (64, bias(has_below, 1)), (64, bias(has_above, 1))))

    def product(columns, rows):
        shared = dot(keyvals[0:384, columns], rows, NT)
        edges = jnp.concatenate(
            [
                dot(keyvals[384:576, columns], rows[0:128], NT),
                dot(keyvals[576:768, columns], rows[128:256], NT),
            ],
            axis=1,
        )
        return shared, edges

    for h in range(4):
        kc, vc = columns_of(h)
        at = NEAR * h
        shared, edges = product(kc, queries[:, kc])
        scores = jnp.concatenate(
            [
                shared * FACTOR2 + rows_bias,
                edges[0:128] * FACTOR2 + fine_bias,
                edges[128:192] * FACTOR2 + half_bias,
            ],
            axis=0,
        )
        highest = jnp.max(scores, axis=0, keepdims=True)
        weight = jnp.exp2(scores - highest)
        weights[at : at + NEAR] = weight
        stats[h : h + 1] = highest
        stats[4 + h : 5 + h] = jnp.sum(weight, axis=0, keepdims=True)
        outputs[HEAD * h : HEAD * h + HEAD] = back(weight.astype(BF16), keyvals, vc)
        shared, edges = product(vc, grads[:, kc])
        dprobs[at : at + 384] = shared
        dprobs[at + 384 : at + NEAR] = edges


def main_kernel(
    where, queries, grads, outputs, stats, m2, p2, s2, z3, x3, s3,
    output, scales, dscores, gm2, gp2, gs2, gz3, gx3, gs3,
    far,
):
    chips = where[1] // 2
    chip = where[0] // 2
    quad = chip // 2
    for n, piece in enumerate((m2, p2, s2, z3, x3, s3)):
        far[64 * n : 64 * n + 64] = piece[...]
    far2 = jnp.where(chip % 2 == 0, chip + 3, chip - 3)
    far3 = jnp.where(quad % 2 == 0, quad + 3, quad - 3)
    quads = chips // 2
    rows_bias = row_bias(
        (
            (64, bias(jnp.where(chip % 2 == 0, chip >= 2, chip + 2 < chips), 2)),
            (64, bias(jnp.where(chip % 2 == 0, chip + 2 < chips, chip >= 2), 2)),
            (64, bias((far2 >= 0) & (far2 < chips), 2)),
            (64, F32(3)),
            (64, bias(jnp.where(chip % ROW < ROW // 2, chip >= ROW, chip + ROW < chips), 3)),
            (64, bias((far3 >= 0) & (far3 < quads), 3)),
        )
    )
    heads = [columns_of(h) for h in range(4)]
    scores = [dot(far[:, kc], queries[:, kc], NT) * FACTOR2 + rows_bias for kc, _ in heads]
    dprobs = [dot(far[:, vc], grads[:, kc], NT) for kc, vc in heads]
    probs = []
    for h in range(4):
        before = stats[h : h + 1]
        highest = jnp.maximum(before, jnp.max(scores[h], axis=0, keepdims=True))
        weight = jnp.exp2(scores[h] - highest)
        shrink = jnp.exp2(before - highest)
        total = stats[4 + h : 5 + h] * shrink + jnp.sum(weight, axis=0, keepdims=True)
        inverse = 1.0 / total
        scales[h : h + 1] = shrink * inverse
        probs.append(weight * inverse)
    lows = [p.astype(BF16) for p in probs]
    attended = [
        outputs[HEAD * h : HEAD * h + HEAD] * scales[h : h + 1] + dot(far[:, vc], lows[h], TN)
        for h, (_, vc) in enumerate(heads)
    ]
    terms_v = [dot(lows[h], grads[:, kc]).astype(BF16) for h, (kc, _) in enumerate(heads)]
    terms_k = []
    for h, (kc, _) in enumerate(heads):
        delta = jnp.sum(grads[:, kc].astype(F32).T * attended[h], axis=0, keepdims=True)
        scales[4 + h : 5 + h] = delta
        dscore = (probs[h] * (dprobs[h] - delta)).astype(BF16)
        dscores[FAR * h : FAR * h + FAR] = dscore
        terms_k.append((dot(dscore, queries[:, kc]) * FACTOR).astype(BF16))
    for h, (kc, vc) in enumerate(heads):
        output[:, kc] = attended[h].T
        for n, piece in enumerate((gm2, gp2, gs2, gz3, gx3, gs3)):
            piece[:, kc] = terms_k[h][64 * n : 64 * n + 64]
            piece[:, vc] = terms_v[h][64 * n : 64 * n + 64]


def rest_kernel(
    where, queries, grads, near, weights, dprobs, scales, dscores, output,
    m2, p2, s2, z3, x3, s3,
    keep, send, grad_below, grad_above,
    outs,
):
    core = where[0] % 2
    spread = spread_matrix(BLOCK, 64, 2)
    for h in range(4):
        kc, vc = columns_of(h)
        at = NEAR * h
        probs = weights[at : at + NEAR] * scales[h : h + 1]
        low = probs.astype(BF16)
        dscore = (probs * (dprobs[at : at + NEAR] - scales[4 + h : 5 + h])).astype(BF16)
        far = jnp.concatenate([piece[:, kc] for piece in (m2, p2, s2, z3, x3, s3)], axis=0)
        query_grad = back(dscore, near, kc) + dot(far, dscores[FAR * h : FAR * h + FAR], TN)
        outs[:, kc] = output[:, kc]
        outs[:, vc] = query_grad.T * FACTOR
        for columns, weight, rows, scale in (
            (kc, dscore, queries[:, kc], FACTOR),
            (vc, low, grads[:, kc], 1.0),
        ):
            shared = dot(weight[0:384], rows) * scale
            part_a = dot(weight[384:576, 0:128], rows[0:128]) * scale
            part_b = dot(weight[384:576, 128:256], rows[128:256]) * scale
            outs[:, PAIR + columns.start : PAIR + columns.stop] = shared[0:256]
            terms = shared[256:384].astype(BF16)
            grad_below[0:128, columns] = (
                part_a[0:128] + dot(spread, part_b[128:192].astype(BF16))
            ).astype(BF16)
            grad_below[128:192, columns] = terms[0:64]
            grad_above[0:128, columns] = (
                part_b[0:128] + dot(spread, part_a[128:192].astype(BF16))
            ).astype(BF16)
            grad_above[128:192, columns] = terms[64:128]
    keep[...] = outs[block_at(core), :]
    send[...] = outs[block_at(1 - core), :]


def fold_kernel(
    where, grad_below, grad_above, s3, z3, cross2, pair2,
    out_same, out_cross, half_same, half_cross, keep3, send3,
):
    even = (where[0] // 2) % 2 == 0

    def weigh(matrix, use):
        return jnp.where(use, matrix, jnp.zeros_like(matrix))

    def fold(base, pieces2, rows, use, fine, half):
        def rows_of(n):
            return jnp.concatenate(
                [pieces2[32 * n : 32 * n + 32]]
                + [piece[rows + 16 * n : rows + 16 * n + 16] for piece in (z3, s3)],
                axis=0,
            )

        fine_matrix = jnp.concatenate(
            [spread_matrix(128, 32, 4)]
            + [weigh(spread_matrix(128, 16, 8), use)] * 2,
            axis=1,
        )
        half_matrix = jnp.concatenate(
            [spread_matrix(64, 32, 2)]
            + [weigh(spread_matrix(64, 16, 4), use)] * 2,
            axis=1,
        )
        return (
            (base[0:128].astype(F32) + dot(fine_matrix, rows_of(fine))).astype(BF16),
            (base[128:192].astype(F32) + dot(half_matrix, rows_of(half))).astype(BF16),
        )

    first = where[0] % 2 == 0
    from2 = jnp.where(even, pair2[...], cross2[...])
    to2 = jnp.where(even, cross2[...], pair2[...])
    fine_below, half_below = fold(grad_below, from2, 0, jnp.logical_not(even), 1, 0)
    fine_above, half_above = fold(grad_above, to2, 32, even, 0, 1)
    out_same[...] = jnp.where(first, fine_above, fine_below)
    out_cross[...] = jnp.where(first, fine_below, fine_above)
    half_same[...] = jnp.where(first, half_below, half_above)
    half_cross[...] = jnp.where(first, half_above, half_below)
    row = pl.multiple_of((where[0] // 2) % 2 * 32, 32)
    own3 = (z3[pl.ds(row, 32), :].astype(F32) + s3[pl.ds(row, 32), :].astype(F32)).astype(BF16)
    keep3[...] = jnp.where(first, own3[0:16], own3[16:32])
    send3[...] = jnp.where(first, own3[16:32], own3[0:16])


def join_kernel(where, out_keep, out_recv, attended, qg):
    core = where[0] % 2
    mine = half_columns(core)
    other = half_columns(1 - core)
    attended[:, mine] = out_keep[:, 0:512].astype(BF16)
    attended[:, other] = out_recv[:, 0:512].astype(BF16)
    qg[:, mine] = out_keep[:, 512:1024]
    qg[:, other] = out_recv[:, 512:1024]


def final_kernel(
    where, keep, recv, keep3, recv3, fine_same, fine_cross, half_same, half_cross,
    kg, vg, total, sems,
):
    core = where[0] % 2
    matrix = jnp.concatenate([spread_matrix(BLOCK, 64, 2), spread_matrix(BLOCK, 16, 8)], axis=1)
    copies = []
    for n, (side, own, fine, half, last) in enumerate(
        (
            (core, keep, fine_same, half_same, keep3),
            (1 - core, recv, fine_cross, half_cross, recv3),
        )
    ):
        coarse = jnp.concatenate([half[...], last[...]], axis=0)
        total[n] = own[:, PAIR : 2 * PAIR] + fine[...].astype(F32) + dot(matrix, coarse)
        for m, target in enumerate((kg, vg)):
            copies.append(
                pltpu.make_async_copy(
                    total.at[n, :, HALF * m : HALF * (m + 1)],
                    target.at[:, half_columns(side)],
                    sems.at[2 * n + m],
                )
            )
            copies[-1].start()
    for copy in copies:
        copy.wait()


def call(kernel, where, args, outs, scratch=(), space=pltpu.VMEM):
    return pl.pallas_call(
        kernel,
        out_shape=[jax.ShapeDtypeStruct(shape, dtype) for shape, dtype in outs],
        in_specs=[pl.BlockSpec(memory_space=pltpu.SMEM)]
        + [pl.BlockSpec(memory_space=pltpu.VMEM)] * len(args),
        out_specs=[pl.BlockSpec(memory_space=space)] * len(outs),
        scratch_shapes=list(scratch),
        compiler_params=pltpu.CompilerParams(vmem_limit_bytes=32 * 1024 * 1024),
    )(where, *args)


def sources(chips):
    def opposite(p):
        turn = ROW // 2 + 1 if p % 2 == 0 else ROW // 2 - 1
        return p - p % ROW + (p + turn) % ROW

    near = {
        "fine_same": lambda p, c: (p - 1, 1) if c == 1 else (p + 1, 0),
        "half_same": lambda p, c: (p - 1, 0) if c == 0 else (p + 1, 1),
        "cross": lambda p, c: (p - 1 if p % 2 == 0 else p + 1, c),
        "pair": lambda p, c: (p ^ 1, c),
        "far2": lambda p, c: (p + 2 if p % 2 == 0 else p - 2, c),
        "z3": lambda p, c: (opposite(p), c),
        "x3": lambda p, c: (p - ROW if p % ROW < ROW // 2 else p + ROW, c),
        "s3": lambda p, c: (p + 6 if p // 2 % 2 == 0 else p - 6, c),
    }
    closing = {
        "fine_same": lambda p, c: (p, 1 - c),
        "half_same": lambda p, c: (p, 1 - c),
        "cross": lambda p, c: (p, 1 - c),
        "far2": lambda p, c: (p ^ 1, c),
        "x3": lambda p, c: (p - p % ROW + ROW - 1 - p % ROW, c),
        "s3": lambda p, c: (p ^ 1, c),
    }

    def source(name, p, c):
        found = near[name](p, c)
        return found if 0 <= found[0] < chips else closing[name](p, c)

    return source


def on_device(query_rows, key_rows, value_rows, out_grad):
    position = lax.axis_index(AXES)
    devices = lax.axis_size(AXES)
    chips = devices // 2
    plan = sources(chips)
    where = jnp.stack([position, jnp.int32(devices)]).astype(jnp.int32)

    def swap(x):
        return lax.ppermute(x, AXES, [(i, i ^ 1) for i in range(devices)])

    def pairs(name):
        found = []
        for chip in range(chips):
            for core in range(2):
                source, side = plan(name, chip, core)
                found.append((2 * source + side, 2 * chip + core))
        return found

    def fetch(x, name):
        return lax.ppermute(x, AXES, pairs(name))

    def give(x, name):
        return lax.ppermute(x, AXES, [(b, a) for a, b in pairs(name)])

    recv_q = swap(query_rows)
    recv_g = swap(out_grad)
    own_kv, other_kv, half_kv = call(
        open_kernel, where, (key_rows, value_rows), [((BLOCK, PAIR), BF16)] * 3
    )
    recv_q, recv_g, own_kv, other_kv, half_kv = lax.optimization_barrier(
        (recv_q, recv_g, own_kv, other_kv, half_kv)
    )
    fine_cross = swap(fetch(other_kv, "fine_same"))
    half_same = fetch(half_kv, "half_same")
    half_cross = swap(half_same)
    fine_same = fetch(own_kv, "fine_same")
    recv_kv = swap(other_kv)
    near = (fine_same, fine_cross, half_same, half_cross)
    cross2, pair2, quad3 = call(
        coarse_kernel, where, (own_kv, recv_kv, *near), [((64, PAIR), BF16)] * 3
    )
    z3 = fetch(quad3, "z3")
    s3 = fetch(quad3, "s3")
    c2 = fetch(cross2, "cross")
    b2 = fetch(pair2, "pair")
    f2 = fetch(cross2, "far2")
    x3 = fetch(z3, "x3")
    queries, grads, near_kv, weights, dprobs, stats, outputs = call(
        near_kernel,
        where,
        (query_rows, out_grad, recv_q, recv_g, own_kv, recv_kv, *near),
        [
            ((2 * BLOCK, HALF), BF16),
            ((2 * BLOCK, HALF), BF16),
            ((768, PAIR), BF16),
            ((4 * NEAR, 2 * BLOCK), F32),
            ((4 * NEAR, 2 * BLOCK), F32),
            ((8, 2 * BLOCK), F32),
            ((4 * HEAD, 2 * BLOCK), F32),
        ],
    )
    far = (c2, b2, f2, z3, x3, s3)
    output, scales, dscores, gm2, gp2, gs2, gz3, gx3, gs3 = call(
        main_kernel,
        where,
        (queries, grads, outputs, stats, *far),
        [
            ((2 * BLOCK, HALF), F32),
            ((8, 2 * BLOCK), F32),
            ((4 * FAR, 2 * BLOCK), BF16),
        ]
        + [((64, PAIR), BF16)] * 6,
        scratch=[pltpu.VMEM((FAR, PAIR), BF16)],
    )
    back_s3 = give(gs3, "s3")
    gz3, shared, scales = lax.optimization_barrier(
        (gz3 + give(gx3, "x3"), fetch(gs2, "pair"), scales)
    )
    gm2 = gm2 + shared
    back_z3 = give(gz3, "z3")
    back_c2 = give(gm2, "cross")
    back_b2 = give(gp2, "pair")
    keep, send, grad_below, grad_above = call(
        rest_kernel,
        where,
        (queries, grads, near_kv, weights, dprobs, scales, dscores, output, *far),
        [
            ((BLOCK, 2 * PAIR), F32),
            ((BLOCK, 2 * PAIR), F32),
            ((192, PAIR), BF16),
            ((192, PAIR), BF16),
        ],
        scratch=[pltpu.VMEM((2 * BLOCK, 2 * PAIR), F32)],
    )
    fine_same, fine_cross, half_same, half_cross, keep3, send3 = call(
        fold_kernel,
        where,
        (grad_below, grad_above, back_s3, back_z3, back_c2, back_b2),
        [((BLOCK, PAIR), BF16)] * 2
        + [((BLOCK // 2, PAIR), BF16)] * 2
        + [((16, PAIR), BF16)] * 2,
    )
    fine_same = give(fine_same, "fine_same")
    fine_cross = give(swap(fine_cross), "fine_same")
    half_same = give(half_same, "half_same")
    half_cross = give(swap(half_cross), "half_same")
    send, send3 = lax.optimization_barrier((send, send3))
    recv3 = swap(send3)
    recv = swap(send)
    attended, query_grad = call(
        join_kernel, where, (keep, recv), [((BLOCK, PAIR), BF16), ((BLOCK, PAIR), F32)]
    )
    attended, query_grad, keep3 = lax.optimization_barrier((attended, query_grad, keep3))
    key_grad, value_grad = call(
        final_kernel,
        where,
        (keep, recv, keep3, recv3, fine_same, fine_cross, half_same, half_cross),
        [((BLOCK, PAIR), F32)] * 2,
        scratch=[pltpu.VMEM((2, BLOCK, PAIR), F32), pltpu.SemaphoreType.DMA((4,))],
        space=pl.ANY,
    )
    return attended, query_grad, key_grad, value_grad


def solution(mesh):
    spec = P(AXES, None)
    return jax.shard_map(
        on_device, mesh=mesh, in_specs=(spec,) * 4, out_specs=(spec,) * 4, check_vma=False
    )
```
